32 devices in a mesh: ha: 8 (over y, x, core), wa: 4 (over z).
Axes of the slice: x: 2, y: 2, z: 4, core: 2. Of those that a mesh axis runs over, the one named last changes fastest.
Arguments:
- features: bfloat16 [4, 208, 20, 2048], P(None, 'ha', 'wa'), may hold values from -6 to 6
- row_image: int32 [4, 208], replicated, may hold values from 0 to 15, never falling along the last dimension, each value on 1 to 33 neighbouring positions
- cotangent: bfloat16 [4, 208, 20, 256], P(None, 'ha', 'wa'), may hold values from -6 to 6
- w_one: bfloat16 [2048, 256], P('ha', 'wa'), may hold values from -0.125 to 0.125
- dilated_weight: bfloat16 [3, 9, 2048, 256], P(None, None, 'ha', 'wa'), may hold values from -0.046875 to 0.046875
- w_pool: bfloat16 [2048, 256], P('ha', 'wa'), may hold values from -0.125 to 0.125
- w_proj: bfloat16 [1280, 256], P('ha', 'wa'), may hold values from -0.15625 to 0.15625
- scales: float32 [5, 256], replicated, may hold values from 0.5 to 1.5
- shifts: float32 [5, 256], replicated, may hold values from -3 to 3
- out_scale: float32 [256], replicated, may hold values from 0.5 to 1.5
- out_shift: float32 [256], replicated, may hold values from -3 to 3
Outputs:
- activations: bfloat16 [4, 208, 20, 256], P(None, 'ha', 'wa')
- feature_grad: bfloat16 [4, 208, 20, 2048], P(None, 'ha', 'wa')
- w_one_grad: float32 [2048, 256], P('ha', 'wa')
- w_atrous_grad: float32 [3, 9, 2048, 256], P(None, None, 'ha', 'wa')
- w_pool_grad: float32 [2048, 256], P('ha', 'wa')
- w_proj_grad: float32 [1280, 256], P('ha', 'wa')
- scales_grad: float32 [5, 256], replicated
- shifts_grad: float32 [5, 256], replicated
- out_scale_grad: float32 [256], replicated
- out_shift_grad: float32 [256], replicated
The draws below stay inside these ranges and needn't reach their ends.
Inputs may be any that keep to these rules, and one draw needn't show every extreme that they name: In each micro-batch, row_image never falls along the height and each of the 16 images holds 1 to 33 whole rows, one of them exactly 33.
All inputs are finite; a program needn't handle non-finite values.
Results may differ from the reference program's by a relative error of at most 0.015.
Values may be sent and summed in bfloat16 or wider, within the bound.
No kernel may reach another device: no remote copies, remote signals or barrier semaphores. Data moves between devices by JAX's collectives and lax.ppermute only.
A program may use at most 896 MiB of HBM per device.

```python
import math
from functools import partial
import jax
import jax.numpy as jnp
import numpy as np
from jax import lax

C = 2048
OUT = 256
MICRO = 4
REACH = 18
MOST_ROWS = 33
CAT = 1280
HEIGHT = 208
WIDTH = 20
VALID = 13
NIMG = 16


def levels(own_key, dims, shards, least, top_value):
    def one(axis_at, blocks):
        draws = jax.random.uniform(jax.random.fold_in(jax.random.fold_in(own_key, 6), axis_at), (blocks,), jnp.float32, least / len(shards), top_value / len(shards))
        return jnp.repeat(jnp.exp(draws), dims[axis_at] // blocks).reshape((-1,) + (1,) * (len(dims) - axis_at - 1))

    gain = one(*shards[0])
    for cut in shards[1:]:
        gain = gain * one(*cut)
    return gain


def length_profile(count, total, limit, skew):
    weights = [(1 << 20) // math.isqrt(rank ** skew) + 1 for rank in range(2, count + 1)]
    rest, given = total - limit - (count - 1), [1] * (count - 1)
    while rest > 0:
        free = [i for i in range(count - 1) if given[i] < limit]
        pool, budget = sum([weights[i] for i in free]), rest
        for i in free:
            more = min(limit - given[i], max(1, budget * weights[i] // pool), rest)
            given[i] = given[i] + more
            rest = rest - more
    return np.array([limit] + given)


def uneven_parts(own_key, amount, total, most, slope):
    if amount == 2:
        one = jax.random.randint(own_key, (), max(1, total - most), min(most, total - 1) + 1)
        return jnp.stack([one, total - one])
    tallies = jnp.asarray(length_profile(amount, total, most, slope), jnp.int32)
    couples = (amount - 1) // 2
    donor, receiver = tallies[1:1 + 2 * couples:2], tallies[2:2 + 2 * couples:2]
    slack = jnp.minimum(donor - 1, most - receiver)
    passed = jax.random.randint(jax.random.fold_in(own_key, 1), (couples,), 0, 1 << 20) % (slack + 1)
    tallies = tallies.at[1:1 + 2 * couples:2].set(donor - passed).at[2:2 + 2 * couples:2].set(receiver + passed)
    return tallies[jax.random.permutation(jax.random.fold_in(own_key, 2), amount)]


def scatter_about(stream_key, shape, deviation, most, split=(), held_as=jnp.bfloat16):
    values = deviation * jax.random.normal(stream_key, shape, jnp.float32)
    if split:
        values = values * levels(stream_key, shape, split, -0.22, 0.18)
    return jnp.clip(values, -most, most).astype(held_as)


def setup_inputs(seed: int = 0) -> dict:
    seeds = jax.random.split(jax.random.key(seed), 12)
    features = scatter_about(seeds[0], (MICRO, HEIGHT, WIDTH, C), 1.0, 6.0, ((1, 8), (2, 4)))
    row_image = jax.vmap(lambda own: jnp.searchsorted(jnp.cumsum(uneven_parts(own, NIMG, HEIGHT, MOST_ROWS, 2)), jnp.arange(HEIGHT), side="right"))(jax.random.split(seeds[1], MICRO)).reshape((MICRO, HEIGHT)).astype(jnp.int32)
    cotangent = scatter_about(seeds[2], (MICRO, HEIGHT, WIDTH, OUT), 1.0, 6.0, ((1, 8), (2, 4)))
    w_one = scatter_about(seeds[3], (C, OUT), C ** -0.5, 0.125, ((0, 8), (1, 4)))
    dilated_weight = scatter_about(seeds[4], (3, 9, C, OUT), (9 * C) ** -0.5, 0.046875, ((2, 8), (3, 4)))
    w_pool = scatter_about(seeds[5], (C, OUT), C ** -0.5, 0.125, ((0, 8), (1, 4)))
    w_proj = scatter_about(seeds[6], (CAT, OUT), CAT ** -0.5, 0.15625, ((0, 8), (1, 4)))
    scales = jnp.clip(1.0 + 0.1 * jax.random.normal(seeds[7], (5, OUT), jnp.float32), 0.5, 1.5)
    shifts = scatter_about(seeds[8], (5, OUT), 0.5, 3.0, (), jnp.float32)
    out_scale = jnp.clip(1.0 + 0.1 * jax.random.normal(seeds[9], (OUT,), jnp.float32), 0.5, 1.5)
    out_shift = scatter_about(seeds[10], (OUT,), 0.5, 3.0, (), jnp.float32)
    return dict(features=features, row_image=row_image, cotangent=cotangent, w_one=w_one, dilated_weight=dilated_weight, w_pool=w_pool, w_proj=w_proj, scales=scales, shifts=shifts, out_scale=out_scale, out_shift=out_shift)


dilation_rates = (6, 12, 18)
epsilon = 1e-05

@jax.custom_vjp
def low(v):
    return lax.optimization_barrier(v.astype(jnp.bfloat16)).astype(jnp.float32)

@jax.custom_vjp
def low_back(v):
    return v

def low_keep(v):
    return (low(v), None)

def low_pass(kept, grad):
    return (grad,)

def back_keep(v):
    return (v, None)

def back_low(kept, grad):
    return (low(grad),)
low.defvjp(low_keep, low_pass)
low_back.defvjp(back_keep, back_low)

def matmul_high(einsum_form, left_side, right_side):
    return jnp.einsum(einsum_form, left_side, right_side, precision=lax.Precision.HIGHEST)

def smooth_gate(inputs):
    return inputs * jax.nn.sigmoid(inputs)

def normalize(values, mask_cols, pixel_total, scale_vec, shift_vec):
    first_moment = lax.optimization_barrier(jnp.sum(values * mask_cols, axis=(0, 1))) / pixel_total
    second_moment = lax.optimization_barrier(jnp.sum(values * values * mask_cols, axis=(0, 1))) / pixel_total
    inverse = lax.rsqrt(second_moment - first_moment * first_moment + epsilon)
    return (values - first_moment) * inverse * scale_vec + shift_vec

def atrous_branch(padded_input, padded_row_labels, row_labels, kernels, rate_value):
    result = jnp.zeros((HEIGHT, WIDTH, OUT), jnp.float32)
    for step_row in (-1, 0, 1):
        for step_col in (-1, 0, 1):
            tap_index = 3 * (step_row + 1) + step_col + 1
            top_row = REACH + step_row * rate_value
            left_col = REACH + step_col * rate_value
            window = padded_input[top_row:top_row + HEIGHT, left_col:left_col + WIDTH]
            row_match = (padded_row_labels[top_row:top_row + HEIGHT] == row_labels).astype(jnp.float32)
            result = result + row_match[:, None, None] * matmul_high('hwd,de->hwe', window, kernels[tap_index])
    return result
verified_branch = jax.checkpoint(atrous_branch, static_argnums=(4,))

def layer(row_image, features, w_one, dilated_weight, w_pool, w_proj, scales, shifts, out_scale, out_shift):
    col_mask = (jnp.arange(WIDTH) < VALID).astype(jnp.float32)[None, :, None]
    pixel_total = float(HEIGHT * VALID)
    labels = jnp.arange(NIMG, dtype=jnp.int32)
    results = []
    for batch_index in range(MICRO):
        row_labels = row_image[batch_index]
        masked = low(features[batch_index]) * col_mask
        images = (row_labels[:, None] == labels[None, :]).astype(jnp.float32)
        counts = lax.optimization_barrier(jnp.sum(images, axis=0)) * VALID
        padded_input = jnp.pad(masked, ((REACH, REACH), (REACH, REACH), (0, 0)))
        padded_row_labels = jnp.pad(row_labels, (REACH, REACH), constant_values=-1)
        branch_outputs = [matmul_high('hwd,de->hwe', masked, w_one)]
        for dilation_index in range(3):
            branch_outputs.append(verified_branch(padded_input, padded_row_labels, row_labels, dilated_weight[dilation_index], dilation_rates[dilation_index]))
        act_list = []
        for branch_index in range(4):
            branch_value = low_back(branch_outputs[branch_index])
            act_list.append(smooth_gate(normalize(branch_value, col_mask, pixel_total, scales[branch_index], shifts[branch_index])))
        row_sums = lax.optimization_barrier(jnp.sum(masked, axis=1))
        pooled = low(jnp.dot(images.T, row_sums, precision=lax.Precision.HIGHEST) / counts[:, None])
        pool_out = low_back(jnp.dot(pooled, w_pool, precision=lax.Precision.HIGHEST))
        weighted = counts[:, None]
        pool_first = lax.optimization_barrier(jnp.sum(weighted * pool_out, axis=0)) / pixel_total
        pool_second = lax.optimization_barrier(jnp.sum(weighted * pool_out * pool_out, axis=0)) / pixel_total
        pool_inverse = lax.rsqrt(pool_second - pool_first * pool_first + epsilon)
        pool_act = smooth_gate((pool_out - pool_first) * pool_inverse * scales[4] + shifts[4])
        spread = jnp.dot(images, pool_act, precision=lax.Precision.HIGHEST)
        act_list.append(jnp.broadcast_to(spread[:, None, :], (HEIGHT, WIDTH, OUT)))
        joined = low(jnp.concatenate(act_list, axis=-1))
        projected = low_back(matmul_high('hwk,ke->hwe', joined, w_proj))
        results.append(smooth_gate(normalize(projected, col_mask, pixel_total, out_scale, out_shift)) * col_mask)
    return jnp.stack(results)

def reference(features, row_image, cotangent, w_one, dilated_weight, w_pool, w_proj, scales, shifts, out_scale, out_shift):
    primals = (features.astype(jnp.float32), w_one.astype(jnp.float32), dilated_weight.astype(jnp.float32), w_pool.astype(jnp.float32), w_proj.astype(jnp.float32), scales, shifts, out_scale, out_shift)
    outputs, pullback = jax.vjp(partial(layer, row_image), *primals)
    gradients = pullback(cotangent.astype(jnp.float32))
    return (outputs.astype(jnp.bfloat16), gradients[0].astype(jnp.bfloat16), gradients[1], gradients[2], gradients[3], gradients[4], gradients[5], gradients[6], gradients[7], gradients[8])
```

```python
from functools import partial

import jax
import jax.numpy as jnp
from jax import lax
from jax.experimental import pallas as pl
from jax.experimental.pallas import tpu as pltpu
from jax.sharding import PartitionSpec as P

PADC = 7
IMG_DEV = 2
RATES = (6, 12, 18)
EPS = 1e-05
HIGHEST = lax.Precision.HIGHEST
F32 = jnp.float32
BF16 = jnp.bfloat16


def silu(u):
    return u * jax.nn.sigmoid(u)


def silu_slope(u):
    s = jax.nn.sigmoid(u)
    return s * (1.0 + u * (1.0 - s))


def swap(array, axis, bits, sources=None):
    count = lax.axis_size(axis)
    pairs = [(i, i ^ bits) for i in range(count) if sources is None or sources(i)]
    return lax.ppermute(array, axis, pairs)


def tree_sum(parts):
    while len(parts) > 1:
        parts = [parts[i] + parts[i + 1] for i in range(0, len(parts), 2)]
    return parts[0]


def plane_sum(array, groups):
    total = tree_sum([array] + [swap(array, "ha", k) for k in range(1, lax.axis_size("ha"))])
    bits = 1
    while bits < groups:
        total = total + swap(total, "wa", bits)
        bits *= 2
    return total


def take(array, index):
    return lax.dynamic_index_in_dim(array, index, 0, keepdims=False)


def by_distance(array):
    h = lax.axis_index("ha")
    return jnp.stack([take(array, h ^ k) for k in range(array.shape[0])])


def reduce_chunks(even, odd, groups):
    other = swap(odd, "ha", 1)
    both = [even[q].astype(F32) + other[q].astype(F32) for q in range(even.shape[0])]
    got = [swap(both[q].astype(BF16), "ha", 2 * q) for q in range(1, even.shape[0])]
    total = tree_sum([both[0]] + [part.astype(F32) for part in got])
    bits = 1
    while bits < groups:
        total = total + swap(total.astype(BF16), "wa", bits).astype(F32)
        bits *= 2
    return total


def gather_chunks(chunk):
    count = lax.axis_size("ha")
    near = jnp.stack([chunk] + [swap(chunk, "ha", 2 * q) for q in range(1, count // 2)])
    return near, swap(near, "ha", 1)


def in_order(near, far):
    every = jnp.stack([near, far], axis=1)
    return by_distance(every.reshape((2 * near.shape[0],) + near.shape[1:]))


def columns_of(gathered, first, count):
    planes, _, few, rows = gathered.shape
    picked = gathered[:, first : first + count]
    return picked.swapaxes(0, 1).reshape(count, planes * few, rows)


def line_scatter(parts):
    return lax.psum_scatter(parts, "wa", scatter_dimension=0, tiled=False).astype(F32)


def live_taps(rate, valid):
    return [(a, b) for a in (-1, 0, 1) for b in (-1, 0, 1) if b == 0 or valid > rate]


def span(b, rate, valid):
    return max(0, -b * rate), min(valid, valid - b * rate)


def moves(taps):
    return sorted({a for a, b in taps})


def forward_plain(x, shift, weights, rate, taps):
    valid = x.shape[0]
    moved = {
        a: x if a == 0 else jnp.einsum("pq,wqk->wpk", shift[(a + 1) // 2], x) for a in moves(taps)
    }
    out = jnp.zeros(x.shape[:2] + (weights.shape[1],), F32)
    for t, (a, b) in enumerate(taps):
        low, high = span(b, rate, valid)
        part = jnp.einsum(
            "wpk,ek->wpe", moved[a][low + b * rate : high + b * rate], weights[t], preferred_element_type=F32
        )
        out = out.at[low:high].add(part)
    return out


def backward_plain(x, shift, weights, rate, taps, grad, total):
    valid = x.shape[0]
    moved = {
        a: grad if a == 0 else jnp.einsum("pq,wqe->wpe", shift[(1 - a) // 2], grad)
        for a in moves(taps)
    }
    weight_grads = []
    for t, (a, b) in enumerate(taps):
        low, high = span(b, rate, valid)
        d = moved[a][low:high]
        source = slice(low + b * rate, high + b * rate)
        weight_grads.append(jnp.einsum("wpe,wpk->ek", d, x[source], preferred_element_type=F32))
        total = total.at[source].add(
            jnp.einsum("wpe,ek->wpk", d, weights[t], preferred_element_type=F32)
        )
    return jnp.stack(weight_grads), total


def dot(left, right, dims):
    return lax.dot_general(left, right, ((dims[0], dims[1]), ((), ())), preferred_element_type=F32)


NN = ((1,), (0,))
NT = ((1,), (1,))
TN = ((0,), (0,))
WHOLE = pl.BlockSpec(memory_space=pltpu.VMEM)
SCALAR = pl.BlockSpec(memory_space=pltpu.SMEM)
PARAMS = pltpu.CompilerParams(vmem_limit_bytes=32 * 1024 * 1024)


def ceil_to(n, step):
    return -(-n // step) * step


def spots_of(wanted, held):
    return ((wanted[:, None] == held[None, :]) & (wanted >= 0)[:, None]).astype(BF16)


def mixed_rows(size, micro):
    tall = ceil_to(size, 16)
    mixed = jnp.arange(ceil_to(size * micro, 128), dtype=jnp.int32)
    mixed = jnp.where(mixed < size * micro, mixed, -2)
    apart = jnp.arange(ceil_to(micro * tall, 128), dtype=jnp.int32)
    real = (apart < micro * tall) & (apart % tall < size)
    apart = jnp.where(real, apart % tall * micro + apart // tall, -1)
    return mixed, apart


def extract(features, cotangent, z):
    rows, cols, micro, channels = features.shape
    out = cotangent.shape[-1]
    size = rows * cols
    tall, full = ceil_to(size, 16), ceil_to(size * micro, 16)
    steps = channels // out
    mixed, apart = mixed_rows(size, micro)
    high = mixed.shape[0]
    spots = spots_of(apart[: micro * tall], mixed).reshape(micro, tall, high)
    flat = [jnp.pad(a.reshape(size * micro, -1), ((0, full - size * micro), (0, 0))) for a in (features, cotangent)]

    def kernel(z_ref, f_ref, c_ref, spots_ref, *refs):
        outs, held_ref = refs[:-1], refs[-1]
        held_ref[full:] = jnp.zeros((high - full, out), BF16)

        @pl.when(pl.program_id(0) < steps)
        def _():
            held_ref[:full] = f_ref[...]

        @pl.when(pl.program_id(0) == steps)
        def _():
            held_ref[:full] = c_ref[...]

        for k in range(micro):
            outs[k][...] = dot(spots_ref[z_ref[0] ^ k], held_ref[...], NN).astype(BF16)

    return pl.pallas_call(
        kernel,
        grid=(steps + 1,),
        out_shape=[jax.ShapeDtypeStruct((tall, channels + out), BF16)] * micro,
        in_specs=[
            SCALAR,
            pl.BlockSpec((full, out), lambda i: (0, jnp.minimum(i, steps - 1))),
            pl.BlockSpec((full, out), lambda i: (0, 0)),
            WHOLE,
        ],
        out_specs=[pl.BlockSpec((tall, out), lambda i: (0, i))] * micro,
        scratch_shapes=[pltpu.VMEM((high, out), BF16)],
        compiler_params=PARAMS,
        name="extract",
    )(z.reshape(1), *flat, spots)


def choose(slots, z, blocks, spots, cot_spots, ha):
    tall, wide = slots[0].shape
    out = wide // (ha + 1)
    high = spots.shape[1]

    def kernel(z_ref, *refs):
        spots_ref, cot_ref, send_ref, own_ref, held_ref = refs[len(slots) :]
        for v in range(len(slots)):

            @pl.when(z_ref[0] == v)
            def _():
                for j in range(blocks):
                    held_ref[j * tall : (j + 1) * tall] = refs[v ^ j][...]

        held_ref[blocks * tall :] = jnp.zeros((high - blocks * tall, wide), BF16)
        for d in range(ha):
            lanes = slice(d * out, (d + 1) * out)
            send_ref[d] = dot(spots_ref[...], held_ref[:, lanes], NN).astype(BF16)
        own_ref[...] = dot(cot_ref[...], held_ref[:, ha * out :], NN).astype(BF16)

    return pl.pallas_call(
        kernel,
        out_shape=[
            jax.ShapeDtypeStruct((ha, spots.shape[0], out), BF16),
            jax.ShapeDtypeStruct((cot_spots.shape[0], out), BF16),
        ],
        in_specs=[SCALAR] + [WHOLE] * (len(slots) + 2),
        out_specs=[WHOLE, WHOLE],
        scratch_shapes=[pltpu.VMEM((high, wide), BF16)],
        compiler_params=PARAMS,
        name="choose",
    )(z.reshape(1), *slots, spots, cot_spots)


def unchoose(pieces, z, blocks, spots):
    ha, fit, out = pieces.shape
    planes, tall, thick = spots.shape

    def kernel(z_ref, pieces_ref, spots_ref, *refs):
        outs, held_ref = refs[:-1], refs[-1]
        held_ref[fit:] = jnp.zeros((thick - fit, ha * out), BF16)
        for d in range(ha):
            held_ref[:fit, d * out : (d + 1) * out] = pieces_ref[d]
        for v in range(planes):

            @pl.when(z_ref[0] == v)
            def _():
                for j in range(planes):
                    if j < blocks:
                        outs[v ^ j][...] = dot(spots_ref[j], held_ref[...], NN).astype(BF16)
                    else:
                        outs[v ^ j][...] = jnp.zeros((tall, ha * out), BF16)

    return pl.pallas_call(
        kernel,
        out_shape=[jax.ShapeDtypeStruct((tall, ha * out), BF16)] * planes,
        in_specs=[SCALAR, WHOLE, WHOLE],
        out_specs=[WHOLE] * planes,
        scratch_shapes=[pltpu.VMEM((thick, ha * out), BF16)],
        compiler_params=PARAMS,
        name="unchoose",
    )(z.reshape(1), pieces, spots)


def interleave(got, z, blocks, rows, cols):
    micro = len(got)
    tall, channels = got[0].shape
    size = rows * cols
    full = ceil_to(size * micro, 16)
    lanes = min(channels, 512)
    mixed, apart = mixed_rows(size, micro)
    high = apart.shape[0]
    spots = spots_of(mixed[:full], apart)

    def kernel(z_ref, *refs):
        spots_ref, o_ref, held_ref = refs[micro:]
        for k in range(micro):
            at = pl.multiple_of((z_ref[0] ^ k) * tall, 16)
            held_ref[pl.ds(at, tall)] = jnp.where(z_ref[0] < blocks, refs[k][...], jnp.zeros((), BF16))
        held_ref[micro * tall :] = jnp.zeros((high - micro * tall, lanes), BF16)
        o_ref[...] = dot(spots_ref[...], held_ref[...], NN).astype(BF16)

    out = pl.pallas_call(
        kernel,
        grid=(channels // lanes,),
        out_shape=jax.ShapeDtypeStruct((full, channels), BF16),
        in_specs=[SCALAR] + [pl.BlockSpec((tall, lanes), lambda i: (0, i))] * micro + [WHOLE],
        out_specs=pl.BlockSpec((full, lanes), lambda i: (0, i)),
        scratch_shapes=[pltpu.VMEM((high, lanes), BF16)],
        compiler_params=PARAMS,
        name="interleave",
    )(z.reshape(1), *got, spots)
    return out[: size * micro].reshape(rows, cols, micro, channels)


def arrange(raw, place, h, valid, prows):
    ha, tall, deep = raw.shape
    high = place.shape[1]

    def kernel(h_ref, raw_ref, place_ref, x_ref, held_ref):
        held_ref[tall:] = jnp.zeros((high - tall, deep), BF16)
        for k in range(ha):
            held_ref[:tall] = raw_ref[h_ref[0] ^ k]
            block = dot(place_ref[...], held_ref[...], NN).astype(BF16)
            x_ref[:, k * prows : (k + 1) * prows, :] = block.reshape(valid, prows, deep)

    return pl.pallas_call(
        kernel,
        out_shape=jax.ShapeDtypeStruct((valid, ha * prows, deep), BF16),
        in_specs=[SCALAR, WHOLE, WHOLE],
        out_specs=WHOLE,
        scratch_shapes=[pltpu.VMEM((high, deep), BF16)],
        compiler_params=PARAMS,
        name="arrange",
    )(h.reshape(1), raw, place)


def sides_of(taps):
    return sorted({b for a, b in taps}, key=abs)


def in_steps(low, high, step, body):
    whole = (high - low) // step
    if whole:

        def one(i, carry):
            body(low + i * step, step)
            return carry

        lax.fori_loop(0, whole, one, 0)
    if (high - low) % step:
        body(low + whole * step, (high - low) % step)


def forward_kernel(x, weights, group, prows):
    valid, pheight, deep = x.shape
    wa, few = weights.shape[0], weights.shape[2]
    out = wa * few
    half = pheight // prows // 2
    operands, flops = [x, weights], 0
    for shift, first, rate, taps in group:
        operands += [] if shift is None else [shift]
        spans = [span(b, rate, valid) for a, b in taps]
        flops += 2 * pheight * deep * out * sum(high - low for low, high in spans)
    most = max(len(moves(g[3])) for g in group)
    most_sides = max(len(sides_of(g[3])) for g in group)

    def kernel(x_ref, w_ref, *refs):
        ins = list(refs[: len(operands) - 2])
        even_ref, odd_ref, moved_ref, wide_ref, sum_ref = refs[len(operands) - 2 :]
        for g, (shift, first, rate, taps) in enumerate(group):
            steps, sides = moves(taps), sides_of(taps)
            for i, b in enumerate(sides):
                for n, a in enumerate(steps):
                    t = first + taps.index((a, b))
                    for j in range(wa):
                        wide_ref[i, j * few : (j + 1) * few, n * deep : (n + 1) * deep] = w_ref[j, t]
            source_ref = x_ref
            if shift is not None:
                s_ref = ins.pop(0)
                source_ref = moved_ref

                def move(w, carry):
                    moved_ref[w, :, :deep] = dot(s_ref[0], x_ref[w], NN).astype(BF16)
                    moved_ref[w, :, deep : 2 * deep] = x_ref[w]
                    moved_ref[w, :, 2 * deep :] = dot(s_ref[1], x_ref[w], NN).astype(BF16)
                    return carry

                lax.fori_loop(0, valid, move, 0)

            for i, b in enumerate(sides):

                def columns(w, count):
                    values = source_ref[pl.ds(w + b * rate, count)].reshape(count * pheight, -1)
                    part = dot(values, wide_ref[i, :, : len(steps) * deep], NT)
                    part = part.reshape(count, pheight, out)
                    if b == 0:
                        sum_ref[pl.ds(w, count)] = part
                    else:
                        sum_ref[pl.ds(w, count)] += part

                in_steps(*span(b, rate, valid), 4, columns)

            def store(w, carry):
                at = pl.multiple_of(w * prows, prows)
                for k in range(2 * half):
                    to = odd_ref if k % 2 else even_ref
                    to[k // 2, g, pl.ds(at, prows), :] = sum_ref[w, k * prows : (k + 1) * prows].astype(BF16)
                return carry

            lax.fori_loop(0, valid, store, 0)

    shape = jax.ShapeDtypeStruct((half, len(group), valid * prows, out), BF16)
    return pl.pallas_call(
        kernel,
        out_shape=[shape] * 2,
        in_specs=[WHOLE] * len(operands),
        out_specs=[WHOLE] * 2,
        scratch_shapes=[
            pltpu.VMEM((valid, pheight, most * deep), BF16),
            pltpu.VMEM((most_sides, out, most * deep), BF16),
            pltpu.VMEM((valid, pheight, out), F32),
        ],
        compiler_params=PARAMS,
        cost_estimate=pl.CostEstimate(flops=flops, bytes_accessed=4 * x.size, transcendentals=0),
        name="forward",
    )(*operands)


def backward_kernel(x, weights, group, grads, start, h, place, prows):
    valid, pheight, deep = x.shape
    wa, few = weights.shape[0], weights.shape[2]
    out = wa * few
    ha = pheight // prows
    operands, flops = [h.reshape(1), x, start, *grads, weights], 0
    for shift, first, rate, taps in group:
        operands += [] if shift is None else [shift]
        spans = [span(b, rate, valid) for a, b in taps]
        flops += 4 * pheight * deep * out * sum(high - low for low, high in spans)
    if place is not None:
        operands += [place]
    most = max(len(moves(g[3])) for g in group)
    most_sides = max(len(sides_of(g[3])) for g in group)
    count = sum(len(g[3]) for g in group)

    def kernel(h_ref, x_ref, start_ref, near_ref, far_ref, w_ref, *refs):
        ins = list(refs[: len(operands) - 6])
        grad_ref, last_ref, moved_ref, wide_ref = refs[len(operands) - 6 :][:4]
        total_ref = last_ref if place is None else refs[-1]
        done = 0
        for g, (shift, first, rate, taps) in enumerate(group):
            steps, sides = moves(taps), sides_of(taps)
            for i, b in enumerate(sides):
                for n, a in enumerate(steps):
                    t = first + taps.index((a, b))
                    for j in range(wa):
                        at = n * out + j * few
                        wide_ref[i, at : at + few] = w_ref[j, t]
            s_ref = None if shift is None else ins.pop(0)
            middle = 0 if shift is None else out

            def move(w, carry):
                at = pl.multiple_of(w * prows, prows)
                for k in range(ha):
                    rows = slice(k * prows, (k + 1) * prows)
                    of = far_ref if k % 2 else near_ref
                    moved_ref[w, rows, middle : middle + out] = of[k // 2, g, pl.ds(at, prows), :]
                if s_ref is not None:
                    held = moved_ref[w, :, out : 2 * out]
                    moved_ref[w, :, :out] = dot(s_ref[1], held, NN).astype(BF16)
                    moved_ref[w, :, 2 * out :] = dot(s_ref[0], held, NN).astype(BF16)
                return carry

            lax.fori_loop(0, valid, move, 0)
            wide = len(steps) * out

            for i, b in enumerate(sides):
                low, high = span(b, rate, valid)
                left = moved_ref[low:high, :, :wide].reshape((high - low) * pheight, wide)
                right = x_ref[low + b * rate : high + b * rate].reshape((high - low) * pheight, deep)
                part = dot(left, right, TN).astype(BF16)
                for n, a in enumerate(steps):
                    t = done + taps.index((a, b))
                    for j in range(wa):
                        at = n * out + j * few
                        grad_ref[j, t] = part[at : at + few]
            done += len(taps)

            for i, b in enumerate(sides):

                def columns(w, count):
                    values = moved_ref[pl.ds(w - b * rate, count), :, :wide].reshape(count * pheight, wide)
                    part = dot(values, wide_ref[i, :wide], NN).reshape(count, pheight, deep)
                    if g or b != 0:
                        total_ref[pl.ds(w, count)] += part
                    elif start.ndim == 2:
                        total_ref[pl.ds(w, count)] = part + start_ref[...][None]
                    else:
                        total_ref[pl.ds(w, count)] = part + start_ref[pl.ds(w, count)]

                in_steps(*span(-b, rate, valid), 4, columns)
        if place is not None:
            for k in range(ha):
                block = total_ref[:, k * prows : (k + 1) * prows, :].astype(BF16)
                block = block.reshape(valid * prows, deep)
                piece = dot(ins[-1][...], block, TN).astype(BF16)
                last_ref[h_ref[0] ^ k] = piece[: last_ref.shape[1]]

    shapes = [jax.ShapeDtypeStruct((wa, count, few, deep), BF16)]
    scratch = [
        pltpu.VMEM((valid, pheight, most * out), BF16),
        pltpu.VMEM((most_sides, most * out, deep), BF16),
    ]
    specs = [SCALAR] + [WHOLE] * (len(operands) - 1)
    if place is None:
        shapes.append(jax.ShapeDtypeStruct(x.shape, F32))
    else:
        shapes.append(jax.ShapeDtypeStruct((ha, place.shape[1], deep), BF16))
        scratch.append(pltpu.VMEM(x.shape, F32))
    return pl.pallas_call(
        kernel,
        out_shape=shapes,
        in_specs=specs,
        out_specs=[WHOLE] * 2,
        scratch_shapes=scratch,
        compiler_params=PARAMS,
        cost_estimate=pl.CostEstimate(flops=flops, bytes_accessed=8 * x.size, transcendentals=0),
        name="backward",
    )(*operands)


def local(
    features,
    row_image,
    cotangent,
    w_one,
    dilated_weight,
    w_pool,
    w_proj,
    scales,
    shifts,
    out_scale,
    out_shift,
):
    micro, rows, cols, channels = features.shape
    ha, wa = lax.axis_size("ha"), lax.axis_size("wa")
    h, z = lax.axis_index("ha"), lax.axis_index("wa")
    planes = wa // micro
    batch, part = z // planes, z % planes
    deep = w_one.shape[0] // planes
    out = w_one.shape[1] * wa
    valid = cols * wa - PADC
    blocks = -(-valid // cols)
    prows = -(-rows // 16) * 16
    height, pheight = rows * ha, prows * ha
    images = IMG_DEV * ha
    pixels = float(height * valid)
    size = cols * rows

    fast = planes == 1 and 6 * valid * pheight * out < (16 << 20) and channels % out == 0 and deep == out

    taps = [live_taps(r, valid) for r in RATES]
    kept = [
        dilated_weight[j].swapaxes(1, 2)
        if len(taps[j]) == 9
        else jnp.stack([dilated_weight[j, 3 * (a + 1) + b + 1].T for a, b in taps[j]])
        for j in range(3)
    ]
    few = w_proj.shape[0]
    side = jnp.pad(w_proj.T, ((0, 0), (0, w_one.shape[0] - few)))
    near_weights = jnp.concatenate([w_one.T[None], kept[2], kept[1], w_pool.T[None], side[None]])
    near_weights = lax.all_gather(near_weights, "wa", axis=0, tiled=False)
    far_weights = lax.all_gather(kept[0], "wa", axis=0, tiled=False)
    side = columns_of(near_weights, near_weights.shape[1] - 1, 1)[0]
    proj = in_order(*gather_chunks(side))[..., :few].swapaxes(1, 2).reshape(ha * few, out)
    if planes > 1:
        near_weights = lax.dynamic_slice_in_dim(near_weights, part * deep, deep, 3)
        far_weights = lax.dynamic_slice_in_dim(far_weights, part * deep, deep, 3)
    wide_pool = columns_of(near_weights, near_weights.shape[1] - 2, 1)[0]

    if fast:
        slots = extract(features.transpose(1, 2, 0, 3), cotangent.transpose(1, 2, 0, 3), z)
        tall, fit = slots[0].shape[0], ceil_to(valid * rows, 16)
        slots = [slots[0]] + [swap(slots[k], "wa", k, lambda i: i < blocks) for k in range(1, wa)]
        high, thick = ceil_to(blocks * tall, 128), ceil_to(fit, 128)
        held = jnp.arange(high, dtype=jnp.int32)
        block_row = held % tall
        column = held // tall * cols + block_row % cols
        real = (block_row < size) & (column < valid)
        in_piece = jnp.where(real, column * rows + block_row // cols, -1)
        in_chunk = jnp.where(real, column * prows + block_row // cols, -1)
        spots = (jnp.arange(fit, dtype=jnp.int32)[:, None] == in_piece[None, :]).astype(BF16)
        cot_spots = (jnp.arange(valid * prows, dtype=jnp.int32)[:, None] == in_chunk[None, :]).astype(BF16)
        send, cot = choose(slots, z, blocks, spots, cot_spots, ha)
        raw = lax.all_to_all(send, "ha", 0, 0, tiled=True)
    else:
        f = features.transpose(0, 2, 1, 3).reshape(micro, size, ha, planes, deep)
        f = f.transpose(0, 3, 1, 2, 4).reshape(wa, size, ha * deep)
        c = cotangent.transpose(0, 2, 1, 3).reshape(micro, size, out)
        load = jnp.concatenate([f, jnp.repeat(c, planes, axis=0)], axis=-1)
        slots = [take(load, z)]
        for k in range(1, wa):
            slots.append(swap(take(load, z ^ k), "wa", k, lambda i: i < blocks))
        slots = jnp.stack(slots)
        block = jnp.concatenate([take(slots, z ^ j) for j in range(blocks)])[: valid * rows]
        raw = block[:, : ha * deep].reshape(valid * rows, ha, deep).swapaxes(0, 1)
        raw = lax.all_to_all(raw, "ha", 0, 0, tiled=True)
        cot = block[:, ha * deep :].reshape(valid, rows, out)
        cot = jnp.pad(cot, ((0, 0), (0, prows - rows), (0, 0))).reshape(valid * prows, out)
    cot = cot.astype(F32)

    order = h ^ jnp.arange(ha, dtype=jnp.int32)
    labels = by_distance(take(row_image, batch).reshape(ha, rows))
    number = order[:, None] * rows + jnp.arange(rows, dtype=jnp.int32)[None, :]
    pad = ((0, 0), (0, prows - rows))
    labels = jnp.pad(labels, pad, constant_values=-1).reshape(pheight)
    number = jnp.pad(number, pad, constant_values=-(1 << 20)).reshape(pheight)
    same = (labels[:, None] == labels[None, :]) & (labels >= 0)[:, None]
    apart = number[None, :] - number[:, None]
    shift = [
        jnp.stack([(same & (apart == a * r)).astype(BF16) for a in (-1, 1)]) for r in RATES
    ]
    ids = jnp.arange(images, dtype=jnp.int32)
    member = (labels[:, None] == ids[None, :]).astype(F32)
    counts = jnp.sum(member, axis=0) * valid
    own = member[:prows]
    mask = jnp.tile(jnp.sum(own, axis=1), valid)[:, None]

    groups = [
        (near_weights, [(None, 0, 0, [(0, 0)]), (shift[2], 1, RATES[2], taps[2])]),
        (near_weights, [(shift[1], 1 + len(taps[2]), RATES[1], taps[1])]),
        (far_weights, [(shift[0], 0, RATES[0], taps[0])]),
    ]
    chosen = [[0, 3], [2], [1]]
    if fast:
        spot = jnp.arange(valid * prows, dtype=jnp.int32)
        spot = jnp.where(spot % prows < rows, spot // prows * rows + spot % prows, -1)
        place = (spot[:, None] == jnp.arange(thick, dtype=jnp.int32)[None, :]).astype(BF16)
        x = arrange(raw, place, h, valid, prows)
    else:
        x = by_distance(raw).reshape(ha, valid, rows, deep)
        x = jnp.pad(x, ((0, 0), (0, 0), (0, prows - rows), (0, 0)))
        x = x.swapaxes(0, 1).reshape(valid, pheight, deep)
    branch = []
    for weights, group in groups:
        if fast:
            even, odd = forward_kernel(x, weights, group, prows)
        else:
            sums = jnp.stack(
                [forward_plain(x, s, columns_of(weights, n, len(t)), r, t) for s, n, r, t in group]
            )
            sums = sums.astype(BF16).reshape(len(group), valid, ha // 2, 2, prows, out)
            sums = sums.transpose(3, 2, 0, 1, 4, 5).reshape(2, ha // 2, len(group), valid * prows, out)
            even, odd = sums[0], sums[1]
        branch.append(reduce_chunks(even, odd, planes))
    branch = jnp.stack([branch[0][0], branch[2][0], branch[1][0], branch[0][1]])
    row_sums = jnp.sum(x.astype(F32), axis=0)
    pooled = (jnp.dot(member.T, row_sums, precision=HIGHEST) / counts[:, None]).astype(BF16)
    pool_part = dot(pooled, wide_pool, NT)

    once = (part == 0).astype(F32)
    first = plane_sum(
        jnp.concatenate(
            [once * jnp.sum(branch, axis=1), once * jnp.sum(branch * branch, axis=1), pool_part]
        ),
        planes,
    )
    mean = first[0:4] / pixels
    rstd = lax.rsqrt(first[4:8] / pixels - mean * mean + EPS)
    pool_out = first[8:]
    norm = (branch - mean[:, None]) * rstd[:, None]
    hid = norm * scales[:4, None] + shifts[:4, None]
    act = silu(hid)
    weighted = counts[:, None]
    pool_mean = jnp.sum(weighted * pool_out, axis=0) / pixels
    pool_second = jnp.sum(weighted * pool_out * pool_out, axis=0) / pixels
    pool_rstd = lax.rsqrt(pool_second - pool_mean * pool_mean + EPS)
    pool_norm = (pool_out - pool_mean) * pool_rstd
    pool_hid = pool_norm * scales[4] + shifts[4]
    spread = jnp.dot(own, silu(pool_hid), precision=HIGHEST)
    spread = jnp.broadcast_to(spread[None], (valid, prows, out)).reshape(valid * prows, out)
    joined = jnp.concatenate([act[0], act[1], act[2], act[3], spread], axis=-1).astype(BF16)
    projected = jnp.dot(joined, proj, preferred_element_type=F32)

    held = projected * mask
    second = plane_sum(
        jnp.stack([jnp.sum(held, axis=0), jnp.sum(held * held, axis=0)]) * once, planes
    )
    proj_mean = second[0] / pixels
    proj_rstd = lax.rsqrt(second[1] / pixels - proj_mean * proj_mean + EPS)
    proj_norm = (projected - proj_mean) * proj_rstd
    proj_hid = proj_norm * out_scale + out_shift
    activation = silu(proj_hid).astype(BF16)
    dproj_hid = cot * mask * silu_slope(proj_hid)
    third = plane_sum(
        jnp.stack([jnp.sum(dproj_hid, axis=0), jnp.sum(dproj_hid * proj_norm, axis=0)]) * once, planes
    )
    dproj = (
        out_scale * proj_rstd * (dproj_hid - (third[0] + proj_norm * third[1]) / pixels) * mask
    ).astype(BF16)
    djoined = lax.dot_general(dproj, proj, (((1,), (1,)), ((), ())), preferred_element_type=F32)
    grad_proj = lax.dot_general(joined, dproj, (((0,), (0,)), ((), ())), preferred_element_type=F32)
    dact = jnp.stack([djoined[:, j * out : (j + 1) * out] for j in range(4)])
    dspread = jnp.sum(djoined[:, 4 * out :].reshape(valid, prows, out), axis=0)
    image_part = jnp.dot(own.T, dspread, precision=HIGHEST)
    dhid = dact * silu_slope(hid) * mask
    fourth = plane_sum(
        jnp.concatenate([jnp.sum(dhid, axis=1), jnp.sum(dhid * norm, axis=1), image_part]) * once,
        planes,
    )
    branch_shift, branch_scale, image_total = fourth[0:4], fourth[4:8], fourth[8:]
    dbranch = (
        (scales[:4] * rstd)[:, None]
        * (dhid - (branch_shift[:, None] + norm * branch_scale[:, None]) / pixels)
        * mask
    ).astype(BF16)
    dpool_hid = silu_slope(pool_hid) * image_total
    pool_shift = jnp.sum(dpool_hid, axis=0)
    pool_scale = jnp.sum(dpool_hid * pool_norm, axis=0)
    dpool = (
        scales[4] * pool_rstd * (dpool_hid - weighted * (pool_shift + pool_norm * pool_scale) / pixels)
    ).astype(BF16)
    grad_pool = dot(dpool, pooled, TN)
    dpooled = dot(dpool, wide_pool, NN)

    total = jnp.dot(member, dpooled / counts[:, None], precision=HIGHEST)
    sent = [gather_chunks(jnp.stack([dbranch[j] for j in chosen[g]])) for g in (2, 1, 0)][::-1]
    tap_grads = [None] * 3
    if fast:
        for g in (2, 1, 0):
            weights, group = groups[g]
            ends = place if g == 0 else None
            grads, total = backward_kernel(x, weights, group, sent[g], total, h, ends, prows)
            tap_grads[g] = grads
        back = total[:, :fit]
    else:
        total = jnp.broadcast_to(total[None], (valid,) + total.shape)
        for g in (2, 1, 0):
            weights, group = groups[g]
            every = jnp.stack(sent[g], axis=1).reshape(ha, len(group), valid, prows, out)
            every = every.transpose(1, 2, 0, 3, 4).reshape(len(group), valid, pheight, out)
            found = []
            for (s, n, r, t), d in zip(group, every):
                grads, total = backward_plain(x, s, columns_of(weights, n, len(t)), r, t, d, total)
                found.append(grads.reshape(len(t), wa, out // wa, deep).swapaxes(0, 1).astype(BF16))
            tap_grads[g] = jnp.concatenate(found, axis=1)
        back = total.astype(BF16).reshape(valid, ha, prows, deep)[:, :, :rows]
        back = back.swapaxes(0, 1).reshape(ha, valid * rows, deep)
        back = by_distance(back)

    def in_place(grads):
        if planes == 1:
            return grads
        full = jnp.zeros(grads.shape[:-1] + (deep * planes,), grads.dtype)
        return lax.dynamic_update_slice_in_dim(full, grads, part * deep, grads.ndim - 1)

    grad_proj = by_distance((grad_proj * once).astype(BF16).reshape(ha, few, out))
    proj_chunk = reduce_chunks(grad_proj[0::2], grad_proj[1::2], 1)
    proj_chunk = jnp.pad(proj_chunk.T, ((0, 0), (0, w_one.shape[0] - few))).astype(BF16)
    grad_pool = in_place(grad_pool.astype(BF16)).reshape(wa, 1, out // wa, -1)
    proj_chunk = proj_chunk.reshape(wa, 1, out // wa, -1)
    first_sum = [in_place(tap_grads[0]), grad_pool, proj_chunk]
    tap_out = [line_scatter(in_place(tap_grads[2])), line_scatter(in_place(tap_grads[1])), None]
    first_sum = line_scatter(jnp.concatenate(first_sum, axis=1))
    tap_out[2] = first_sum[1:-2]
    one_out, pool_grad_out = first_sum[0].T, first_sum[-2].T
    proj_out = first_sum[-1][:, :few].T
    blank = jnp.zeros((out // wa, w_one.shape[0]), F32)
    atrous = []
    for j in range(3):
        if len(taps[j]) == 9:
            atrous.append(tap_out[j])
        else:
            found = {3 * (a + 1) + b + 1: tap_out[j][t] for t, (a, b) in enumerate(taps[j])}
            atrous.append(jnp.stack([found.get(t, blank) for t in range(9)]))
    atrous_out = jnp.stack(atrous).swapaxes(2, 3)
    sums = jnp.concatenate([branch_scale, pool_scale[None], branch_shift, pool_shift[None], third])
    sums = sums * once
    bits = 1
    while bits < wa:
        sums = sums + swap(sums, "wa", bits)
        bits *= 2

    back = lax.all_to_all(back, "ha", 0, 0, tiled=True)

    def home(i, k):
        return i ^ k < blocks

    if fast:
        number = jnp.arange(wa * tall, dtype=jnp.int32)
        block_row = number % tall
        column = number // tall * cols + block_row % cols
        real = (block_row < size) & (column < valid)
        in_piece = jnp.where(real, column * rows + block_row // cols, -1)
        in_chunk = jnp.where(real, column * prows + block_row // cols, -1)
        piece_spots = (in_piece[:, None] == jnp.arange(thick, dtype=jnp.int32)[None, :]).astype(BF16)
        chunk_spots = (in_chunk[:, None] == jnp.arange(valid * prows, dtype=jnp.int32)[None, :]).astype(BF16)
        got = unchoose(back, z, blocks, piece_spots.reshape(wa, tall, thick))
        got = [got[0]] + [swap(got[k], "wa", k, partial(home, k=k)) for k in range(1, wa)]
        df = interleave(got, z, blocks, rows, cols).transpose(2, 0, 1, 3)
        acts = jnp.dot(chunk_spots, activation, preferred_element_type=F32).astype(BF16)
        acts = acts.reshape(wa, tall, out)
        acts = [take(acts, z ^ k) for k in range(wa)]
        acts = [acts[0]] + [swap(acts[k], "wa", k, partial(home, k=k)) for k in range(1, wa)]
        acts = interleave(acts, z, blocks, rows, cols).transpose(2, 0, 1, 3)
    else:

        def send_home(array):
            array = jnp.pad(array, ((0, wa * size - valid * rows), (0, 0))).reshape(wa, size, -1)
            got = [take(array, z)]
            got += [swap(take(array, z ^ k), "wa", k, partial(home, k=k)) for k in range(1, wa)]
            got = jnp.stack(got)
            got = jnp.where(z < blocks, got, jnp.zeros((), got.dtype))
            return jnp.stack([take(got, z ^ t) for t in range(wa)])

        back = back.swapaxes(0, 1).reshape(valid * rows, ha * deep)
        df = send_home(back).reshape(micro, planes, cols, rows, ha, deep)
        df = df.transpose(0, 3, 2, 4, 1, 5).reshape(features.shape)
        activation = activation.reshape(valid, prows, out)[:, :rows].reshape(valid * rows, out)
        acts = send_home(activation).reshape(micro, planes, cols, rows, out)[:, 0].swapaxes(1, 2)
    return (
        acts,
        df,
        one_out,
        atrous_out,
        pool_grad_out,
        proj_out,
        sums[0:5],
        sums[5:10],
        sums[11],
        sums[10],
    )


def solution(mesh):
    specs = (
        P(None, "ha", "wa", None),
        P(),
        P(None, "ha", "wa", None),
        P("ha", "wa"),
        P(None, None, "ha", "wa"),
        P("ha", "wa"),
        P("ha", "wa"),
        P(),
        P(),
        P(),
        P(),
    )
    out_specs = (
        P(None, "ha", "wa", None),
        P(None, "ha", "wa", None),
        P("ha", "wa"),
        P(None, None, "ha", "wa"),
        P("ha", "wa"),
        P("ha", "wa"),
        P(),
        P(),
        P(),
        P(),
    )
    return jax.shard_map(local, mesh=mesh, in_specs=specs, out_specs=out_specs, check_vma=False)
```

```python
from functools import partial

import jax
import jax.numpy as jnp
import numpy as np
from jax import lax
from jax.experimental import pallas as pl
from jax.experimental.pallas import tpu as pltpu
from jax.sharding import PartitionSpec as P

PADC = 7
IMG_DEV = 2
RATES = (6, 12, 18)
EPS = 1e-05
HIGHEST = lax.Precision.HIGHEST
F32 = jnp.float32
BF16 = jnp.bfloat16


def silu(u):
    return u * jax.nn.sigmoid(u)


def silu_slope(u):
    s = jax.nn.sigmoid(u)
    return s * (1.0 + u * (1.0 - s))


def swap(array, axis, bits, sources=None):
    count = lax.axis_size(axis)
    pairs = [(i, i ^ bits) for i in range(count) if sources is None or sources(i)]
    return lax.ppermute(array, axis, pairs)


def after(value, *others):
    return lax.optimization_barrier((value, *others))[0]


def tree_sum(parts):
    while len(parts) > 1:
        parts = [parts[i] + parts[i + 1] for i in range(0, len(parts), 2)]
    return parts[0]


def plane_parts(array):
    return [array] + [swap(array, "ha", k) for k in range(1, lax.axis_size("ha"))]


def plane_sum(array, groups):
    total = tree_sum(plane_parts(array))
    bits = 1
    while bits < groups:
        total = total + swap(total, "wa", bits)
        bits *= 2
    return total


def take(array, index):
    return lax.dynamic_index_in_dim(array, index, 0, keepdims=False)


def by_distance(array):
    h = lax.axis_index("ha")
    return jnp.stack([take(array, h ^ k) for k in range(array.shape[0])])


def spread_chunks(even, odd):
    other = swap(odd, "ha", 1)
    both = [even[q].astype(F32) + other[q].astype(F32) for q in range(even.shape[0])]
    return both[:1] + [swap(both[q].astype(BF16), "ha", 2 * q) for q in range(1, len(both))]


def sum_chunks(parts, groups):
    total = tree_sum([part.astype(F32) for part in parts])
    bits = 1
    while bits < groups:
        total = total + swap(total.astype(BF16), "wa", bits).astype(F32)
        bits *= 2
    return total


def reduce_square(even, odd):
    other = swap(odd, "ha", 1)
    half = even.shape[1] // 2
    low = even[:, :half].astype(F32) + other[:, :half].astype(F32)
    high = even[:, half:].astype(F32) + other[:, half:].astype(F32)
    low_got = swap(low[1::2].astype(BF16), "ha", 2)
    high_got = swap(high[2:].astype(BF16), "ha", 4)
    low_last = swap((low[2] + low_got[1].astype(F32)).astype(BF16), "ha", 4)
    high_last = swap((high[1] + high_got[1].astype(F32)).astype(BF16), "ha", 2)
    return low[0], low_got, low_last, high[0], high_got, high_last


def gather_square(chunk):
    half = chunk.shape[0] // 2
    low, high = chunk[:half], chunk[half:]
    low_one = swap(low, "ha", 2)
    high_one = swap(high, "ha", 4)
    low_two = swap(jnp.stack([low, low_one]), "ha", 4)
    high_two = swap(jnp.stack([high, high_one]), "ha", 2)
    near = [chunk, low_one, high_one, low_two, high_two]
    return near + [swap(piece, "ha", 1) for piece in near]


def piece_of(k, branch, branches):
    q, half = k // 2, branches // 2
    first = 5 * (k % 2)
    low = branch < half
    inner = branch if low else branch - half
    if q == 0:
        return first, (branch,)
    if q == (1 if low else 2):
        return first + (1 if low else 2), (inner,)
    return first + (3 if low else 4), (int(q == 3), inner)


def gather_near(chunk):
    return [chunk] + [swap(chunk, "ha", 2 * q) for q in range(1, lax.axis_size("ha") // 2)]


def gather_chunks(chunk):
    near = jnp.stack(gather_near(chunk))
    return near, swap(near, "ha", 1)


def in_order(near, far):
    every = jnp.stack([near, far], axis=1)
    return by_distance(every.reshape((2 * near.shape[0],) + near.shape[1:]))


def gather_columns(own):
    gathered = lax.all_gather(own, "wa", axis=0, tiled=False)
    planes, count, few, rows = gathered.shape
    return gathered.swapaxes(0, 1).reshape(count, planes * few, rows)


def neighbour(array, pairs):
    return lax.ppermute(array, "wa", pairs)


def gather_early(own, others):
    right = neighbour(own, [(0, 1), (1, 2), (2, 3)])
    left = neighbour(own, [(1, 0), (2, 1), (3, 2)])
    right_two = neighbour(after(right, others), [(2, 3)])
    left_two = neighbour(after(left, others), [(1, 0), (2, 1)])
    return right, left, right_two, left_two


def gather_late(own, early, *others):
    z = lax.axis_index("wa")
    right, left, right_two, left_two = early
    left_three = neighbour(left_two, [(1, 0)])
    last_two = neighbour(after(right, *others), [(1, 2)])
    last_three = neighbour(last_two, [(2, 3)])
    found = [
        lax.select_n(z, own, right, last_two, last_three),
        lax.select_n(z, left, own, right, right_two),
        lax.select_n(z, left_two, left, own, right),
        lax.select_n(z, left_three, left_two, left, own),
    ]
    return jnp.concatenate(found, axis=1)


def exchange_sum(parts):
    z = lax.axis_index("wa")
    got = [swap(take(parts, z ^ k), "wa", k) for k in range(1, lax.axis_size("wa"))]
    return tree_sum([take(parts, z)] + got)


def line_scatter(parts):
    return lax.psum_scatter(parts, "wa", scatter_dimension=0, tiled=False).astype(F32)


def live_taps(rate, valid):
    return [(a, b) for a in (-1, 0, 1) for b in (-1, 0, 1) if b == 0 or valid > rate]


def span(b, rate, valid):
    return max(0, -b * rate), min(valid, valid - b * rate)


def moves(taps):
    return sorted({a for a, b in taps})


def forward_plain(x, shift, weights, rate, taps):
    valid = x.shape[0]
    moved = {
        a: x if a == 0 else jnp.einsum("pq,wqk->wpk", shift[(a + 1) // 2], x) for a in moves(taps)
    }
    out = jnp.zeros(x.shape[:2] + (weights.shape[1],), F32)
    for t, (a, b) in enumerate(taps):
        low, high = span(b, rate, valid)
        part = jnp.einsum(
            "wpk,ek->wpe", moved[a][low + b * rate : high + b * rate], weights[t], preferred_element_type=F32
        )
        out = out.at[low:high].add(part)
    return out


def backward_plain(x, shift, weights, rate, taps, grad, total):
    valid = x.shape[0]
    moved = {
        a: grad if a == 0 else jnp.einsum("pq,wqe->wpe", shift[(1 - a) // 2], grad)
        for a in moves(taps)
    }
    weight_grads = []
    for t, (a, b) in enumerate(taps):
        low, high = span(b, rate, valid)
        d = moved[a][low:high]
        source = slice(low + b * rate, high + b * rate)
        weight_grads.append(jnp.einsum("wpe,wpk->ek", d, x[source], preferred_element_type=F32))
        total = total.at[source].add(
            jnp.einsum("wpe,ek->wpk", d, weights[t], preferred_element_type=F32)
        )
    return jnp.stack(weight_grads), total


def dot(left, right, dims):
    return lax.dot_general(left, right, ((dims[0], dims[1]), ((), ())), preferred_element_type=F32)


NN = ((1,), (0,))
NT = ((1,), (1,))
TN = ((0,), (0,))
WHOLE = pl.BlockSpec(memory_space=pltpu.VMEM)
SCALAR = pl.BlockSpec(memory_space=pltpu.SMEM)
NO_COST = pl.CostEstimate(flops=0, bytes_accessed=0, transcendentals=0)
WIDE = pltpu.CompilerParams(vmem_limit_bytes=60 * 1024 * 1024)
PARAMS = pltpu.CompilerParams(vmem_limit_bytes=32 * 1024 * 1024)


def ceil_to(n, step):
    return -(-n // step) * step


def pack_weights(w_one, dilated, w_pool, w_proj, taps):
    rows, deep = w_one.shape
    order = [(j, 3 * (a + 1) + b + 1) for j in range(3) for a, b in taps[j]]

    def kernel(one_ref, dilated_ref, pool_ref, proj_ref, out_ref):
        out_ref[0] = one_ref[...]
        for at, (j, t) in enumerate(order):
            out_ref[at + 1] = dilated_ref[j, t]
        out_ref[len(order) + 1] = pool_ref[...]
        out_ref[len(order) + 2] = proj_ref[...]

    return pl.pallas_call(
        kernel,
        out_shape=jax.ShapeDtypeStruct((len(order) + 3, rows, deep), BF16),
        in_specs=[WHOLE] * 4,
        out_specs=WHOLE,
        compiler_params=PARAMS,
        name="pack_weights",
    )(w_one, dilated, w_pool, w_proj)


def spots_of(wanted, held):
    return ((wanted[:, None] == held[None, :]) & (wanted >= 0)[:, None]).astype(BF16)


def mixed_rows(size, micro):
    tall = ceil_to(size, 16)
    mixed = np.arange(ceil_to(size * micro, 128))
    mixed = np.where(mixed < size * micro, mixed, -2)
    apart = np.arange(ceil_to(micro * tall, 128))
    real = (apart < micro * tall) & (apart % tall < size)
    return mixed, np.where(real, apart % tall * micro + apart // tall, -1)


def block_rows(count, tall, rows, cols, valid, pitch):
    row = np.arange(count)
    column = row // tall * cols + row % tall % cols
    real = (row % tall < rows * cols) & (column < valid)
    return np.where(real, column * pitch + row % tall // cols, -1)


def padded_rows(count, valid, prows, rows):
    row = np.arange(count)
    real = (row < valid * prows) & (row % prows < rows)
    return np.where(real, row // prows * rows + row % prows, -1)


def extract(features, cotangent, z):
    rows, cols, micro, channels = features.shape
    out = cotangent.shape[-1]
    size = rows * cols
    tall, full = ceil_to(size, 16), ceil_to(size * micro, 16)
    steps = channels // out
    mixed, apart = mixed_rows(size, micro)
    high = mixed.shape[0]
    spots = spots_of(apart[: micro * tall], mixed).reshape(micro, tall, high)
    flat = [jnp.pad(a.reshape(size * micro, -1), ((0, full - size * micro), (0, 0))) for a in (features, cotangent)]

    def kernel(z_ref, f_ref, c_ref, spots_ref, *refs):
        outs, held_ref = refs[:-1], refs[-1]
        held_ref[full:] = jnp.zeros((high - full, out), BF16)

        @pl.when(pl.program_id(0) < steps)
        def _():
            held_ref[:full] = f_ref[...]

        @pl.when(pl.program_id(0) == steps)
        def _():
            held_ref[:full] = c_ref[...]

        for k in range(micro):
            outs[k][...] = dot(spots_ref[z_ref[0] ^ k], held_ref[...], NN).astype(BF16)

    return pl.pallas_call(
        kernel,
        grid=(steps + 1,),
        out_shape=[jax.ShapeDtypeStruct((tall, channels + out), BF16)] * micro,
        in_specs=[
            SCALAR,
            pl.BlockSpec((full, out), lambda i: (0, jnp.minimum(i, steps - 1))),
            pl.BlockSpec((full, out), lambda i: (0, 0)),
            WHOLE,
        ],
        out_specs=[pl.BlockSpec((tall, out), lambda i: (0, i))] * micro,
        scratch_shapes=[pltpu.VMEM((high, out), BF16)],
        compiler_params=PARAMS,
        name="extract",
    )(z.reshape(1), *flat, spots)


def choose(slots, z, blocks, spots, last_spots, lanes):
    tall, wide = slots[0].shape
    high = spots.shape[1]
    count = wide // lanes - 1

    def kernel(z_ref, *refs):
        spots_ref, last_ref, send_ref, own_ref, held_ref = refs[len(slots) :]
        for v in range(len(slots)):

            @pl.when(z_ref[0] == v)
            def _():
                for j in range(blocks):
                    held_ref[j * tall : (j + 1) * tall] = refs[v ^ j][...]

        held_ref[blocks * tall :] = jnp.zeros((high - blocks * tall, wide), BF16)
        for d in range(count):
            part = held_ref[:, d * lanes : (d + 1) * lanes]
            send_ref[d] = dot(spots_ref[...], part, NN).astype(BF16)
        own_ref[...] = dot(last_ref[...], held_ref[:, count * lanes :], NN).astype(BF16)

    return pl.pallas_call(
        kernel,
        out_shape=[
            jax.ShapeDtypeStruct((count, spots.shape[0], lanes), BF16),
            jax.ShapeDtypeStruct((last_spots.shape[0], lanes), BF16),
        ],
        in_specs=[SCALAR] + [WHOLE] * (len(slots) + 2),
        out_specs=[WHOLE] * 2,
        scratch_shapes=[pltpu.VMEM((high, wide), BF16)],
        compiler_params=PARAMS,
        name="choose",
    )(z.reshape(1), *slots, spots, last_spots)


def unchoose(pieces, last, z, blocks, spots, last_spots):
    ha, fit, out = pieces.shape
    planes, tall, thick = spots.shape
    wide = (ha + 1) * out

    def kernel(z_ref, pieces_ref, last_ref, spots_ref, last_spots_ref, *refs):
        outs, held_ref = refs[:-1], refs[-1]
        held_ref[fit:] = jnp.zeros((thick - fit, ha * out), BF16)
        for d in range(ha):
            held_ref[:fit, d * out : (d + 1) * out] = pieces_ref[d]
        for v in range(planes):

            @pl.when(z_ref[0] == v)
            def _():
                for j in range(planes):
                    if j < blocks:
                        outs[v ^ j][:, : ha * out] = dot(spots_ref[j], held_ref[...], NN).astype(BF16)
                        outs[v ^ j][:, ha * out :] = dot(last_spots_ref[j], last_ref[...], NN).astype(BF16)
                    else:
                        outs[v ^ j][...] = jnp.zeros((tall, wide), BF16)

    return pl.pallas_call(
        kernel,
        out_shape=[jax.ShapeDtypeStruct((tall, wide), BF16)] * planes,
        in_specs=[SCALAR] + [WHOLE] * 4,
        out_specs=[WHOLE] * planes,
        scratch_shapes=[pltpu.VMEM((thick, ha * out), BF16)],
        compiler_params=PARAMS,
        name="unchoose",
    )(z.reshape(1), pieces, last, spots, last_spots)


def order_chunks(near, far, h, few):
    half, out, _ = near.shape

    def kernel(h_ref, near_ref, far_ref, out_ref):
        for k in range(2 * half):
            chunk = (far_ref if k % 2 else near_ref)[k // 2]
            at = pl.multiple_of((h_ref[0] ^ k) * few, 16)
            out_ref[pl.ds(at, few), :] = chunk.T[:few]

    return pl.pallas_call(
        kernel,
        out_shape=jax.ShapeDtypeStruct((2 * half * few, out), BF16),
        in_specs=[SCALAR, WHOLE, WHOLE],
        out_specs=WHOLE,
        compiler_params=PARAMS,
        cost_estimate=NO_COST,
        name="order_chunks",
    )(h.reshape(1), near, far)


def interleave(got, z, blocks, rows, cols, out, others):
    micro = len(got)
    tall, channels = got[0].shape
    channels -= out
    size = rows * cols
    full = ceil_to(size * micro, 16)
    lanes = 2 * out
    mixed, apart = mixed_rows(size, micro)
    high = apart.shape[0]
    spots = spots_of(mixed[:full], apart)

    def kernel(z_ref, *refs):
        spots_ref, df_ref, act_ref, held_ref = refs[2 * micro], refs[-3], refs[-2], refs[-1]
        held_ref[micro * tall :] = jnp.zeros((high - micro * tall, lanes), BF16)

        def place(parts, wide):
            for k in range(micro):
                at = pl.multiple_of((z_ref[0] ^ k) * tall, 16)
                part = jnp.where(z_ref[0] < blocks, parts[k][...], jnp.zeros((), BF16))
                held_ref[pl.ds(at, tall), :wide] = part
            return dot(spots_ref[...], held_ref[:, :wide], NN).astype(BF16)

        @pl.when(pl.program_id(0) == 0)
        def _():
            act_ref[...] = place(refs[micro : 2 * micro], out)

        df_ref[...] = place(refs[:micro], lanes)

    df, act = pl.pallas_call(
        kernel,
        grid=(channels // lanes,),
        out_shape=[jax.ShapeDtypeStruct((full, channels), BF16), jax.ShapeDtypeStruct((full, out), BF16)],
        in_specs=[SCALAR]
        + [pl.BlockSpec((tall, lanes), lambda i: (0, i))] * micro
        + [pl.BlockSpec((tall, out), lambda i: (0, channels // out))] * micro
        + [WHOLE]
        + [pl.BlockSpec(memory_space=pl.ANY)] * len(others),
        out_specs=[pl.BlockSpec((full, lanes), lambda i: (0, i)), pl.BlockSpec((full, out), lambda i: (0, 0))],
        scratch_shapes=[pltpu.VMEM((high, lanes), BF16)],
        compiler_params=PARAMS,
        name="interleave",
    )(z.reshape(1), *got, *got, spots, *others)
    return [a[: size * micro].reshape(rows, cols, micro, -1).transpose(2, 0, 1, 3) for a in (df, act)]


def arrange(raw, place, h, valid, prows):
    ha, tall, deep = raw.shape
    high = place.shape[1]

    def kernel(h_ref, raw_ref, place_ref, x_ref, sum_ref, held_ref):
        held_ref[tall:] = jnp.zeros((high - tall, deep), BF16)
        for k in range(ha):
            held_ref[:tall] = raw_ref[h_ref[0] ^ k]
            block = dot(place_ref[...], held_ref[...], NN).reshape(valid, prows, deep)
            x_ref[:, k * prows : (k + 1) * prows, :] = block.astype(BF16)
            sum_ref[k * prows : (k + 1) * prows] = jnp.sum(block, axis=0)

    return pl.pallas_call(
        kernel,
        out_shape=[
            jax.ShapeDtypeStruct((valid, ha * prows, deep), BF16),
            jax.ShapeDtypeStruct((ha * prows, deep), F32),
        ],
        in_specs=[SCALAR, WHOLE, WHOLE],
        out_specs=[WHOLE, WHOLE],
        scratch_shapes=[pltpu.VMEM((high, deep), BF16)],
        compiler_params=PARAMS,
        name="arrange",
    )(h.reshape(1), raw, place)


def sides_of(taps):
    return sorted({b for a, b in taps}, key=abs)


def in_steps(low, high, step, body):
    whole = (high - low) // step
    if whole:

        def one(i, carry):
            body(low + i * step, step)
            return carry

        lax.fori_loop(0, whole, one, 0)
    if (high - low) % step:
        body(low + whole * step, (high - low) % step)


def forward_kernel(x, weights, group, prows):
    valid, pheight, deep = x.shape
    out = weights.shape[1]
    half = pheight // prows // 2
    operands, flops = [x, weights], 0
    for shift, first, rate, taps in group:
        operands += [] if shift is None else [shift]
        spans = [span(b, rate, valid) for a, b in taps]
        flops += 2 * pheight * deep * out * sum(high - low for low, high in spans)
    most = max(len(moves(g[3])) for g in group)
    most_sides = max(len(sides_of(g[3])) for g in group)

    def kernel(x_ref, w_ref, *refs):
        ins = list(refs[: len(operands) - 2])
        even_ref, odd_ref, moved_ref, wide_ref, sum_ref = refs[len(operands) - 2 :]
        for g, (shift, first, rate, taps) in enumerate(group):
            steps, sides = moves(taps), sides_of(taps)
            for i, b in enumerate(sides):
                for n, a in enumerate(steps):
                    wide_ref[i, :, n * deep : (n + 1) * deep] = w_ref[first + taps.index((a, b))]
            source_ref = x_ref
            if shift is not None:
                s_ref = ins.pop(0)
                source_ref = moved_ref

                def move(w, carry):
                    values = x_ref[w]
                    both = dot(s_ref[...].reshape(2 * pheight, pheight), values, NN).astype(BF16)
                    moved_ref[w, :, :deep] = both[:pheight]
                    moved_ref[w, :, deep : 2 * deep] = values
                    moved_ref[w, :, 2 * deep :] = both[pheight:]
                    return carry

                lax.fori_loop(0, valid, move, 0, unroll=True)

            for i, b in enumerate(sides):

                def columns(w, count):
                    values = source_ref[pl.ds(w + b * rate, count)].reshape(count * pheight, -1)
                    part = dot(values, wide_ref[i, :, : len(steps) * deep], NT)
                    part = part.reshape(count, pheight, out)
                    if b == 0:
                        sum_ref[pl.ds(w, count)] = part
                    else:
                        sum_ref[pl.ds(w, count)] += part

                in_steps(*span(b, rate, valid), 7, columns)

            def store(w, carry):
                at = pl.multiple_of(w * prows, prows)
                for k in range(2 * half):
                    to = odd_ref if k % 2 else even_ref
                    to[k // 2, g, pl.ds(at, prows), :] = sum_ref[w, k * prows : (k + 1) * prows].astype(BF16)
                return carry

            lax.fori_loop(0, valid, store, 0, unroll=True)

    shape = jax.ShapeDtypeStruct((half, len(group), valid * prows, out), BF16)
    return pl.pallas_call(
        kernel,
        out_shape=[shape] * 2,
        in_specs=[WHOLE] * len(operands),
        out_specs=[WHOLE] * 2,
        scratch_shapes=[
            pltpu.VMEM((valid, pheight, most * deep), BF16),
            pltpu.VMEM((most_sides, out, most * deep), BF16),
            pltpu.VMEM((valid, pheight, out), F32),
        ],
        compiler_params=PARAMS,
        cost_estimate=NO_COST,
        name="forward",
    )(*operands)


def loaded(operands):
    return [
        pl.BlockSpec(a.shape, lambda i, n=a.ndim: (0,) * n, pipeline_mode=pl.Buffered(1)) for a in operands
    ]


def build_moved(pieces, moved_ref, s_ref, g, branches, valid, ha, prows, out):
    middle = 0 if s_ref is None else out

    def move(w, carry):
        at = pl.multiple_of(w * prows, prows)
        for k in range(ha):
            piece, index = piece_of(k, g, branches)
            rows = slice(k * prows, (k + 1) * prows)
            moved_ref[w, rows, middle : middle + out] = pieces[piece][(*index, pl.ds(at, prows))]
        if s_ref is not None:
            held = moved_ref[w, :, out : 2 * out]
            both = dot(s_ref[...].reshape(2 * ha * prows, ha * prows), held, NN).astype(BF16)
            moved_ref[w, :, :out] = both[ha * prows :]
            moved_ref[w, :, 2 * out :] = both[: ha * prows]
        return carry

    lax.fori_loop(0, valid, move, 0, unroll=True)


def weights_backward(x, group, pieces, wa, prows):
    valid, pheight, deep = x.shape
    out = pieces[0].shape[-1]
    few, ha, branches = out // wa, pheight // prows, len(group)
    shifts = [g[0] for g in group if g[0] is not None]
    operands = [x, *shifts, *pieces]
    shape = wa, sum(len(g[3]) for g in group), few, deep
    most = max(len(moves(g[3])) for g in group)

    def kernel(x_ref, *refs):
        shift_refs = list(refs[: len(shifts)])
        piece_refs = refs[len(shifts) : len(operands) - 1]
        grad_ref, moved_ref = refs[len(operands) - 1 :]
        done = 0
        for g, (shift, first, rate, taps) in enumerate(group):
            steps = moves(taps)
            s_ref = None if shift is None else shift_refs.pop(0)
            build_moved(piece_refs, moved_ref, s_ref, g, branches, valid, ha, prows, out)
            wide = len(steps) * out
            for b in sides_of(taps):
                low, high = span(b, rate, valid)
                left = moved_ref[low:high, :, :wide].reshape((high - low) * pheight, wide)
                right = x_ref[low + b * rate : high + b * rate].reshape((high - low) * pheight, deep)
                part = dot(left, right, TN).astype(BF16)
                for n, a in enumerate(steps):
                    t = done + taps.index((a, b))
                    for j in range(wa):
                        at = n * out + j * few
                        grad_ref[j, t] = part[at : at + few]
            done += len(taps)

    return pl.pallas_call(
        kernel,
        out_shape=jax.ShapeDtypeStruct(shape, BF16),
        grid=(1,),
        in_specs=loaded(operands),
        out_specs=pl.BlockSpec(shape, lambda i: (0, 0, 0, 0)),
        scratch_shapes=[pltpu.VMEM((valid, pheight, most * out), BF16)],
        compiler_params=WIDE,
        cost_estimate=NO_COST,
        name="weights_backward",
    )(*operands)


def features_backward(x, weights, group, pieces, start, h, place, fit, prows):
    valid, pheight, deep = x.shape
    out = weights.shape[1]
    ha, branches = pheight // prows, len(group)
    shifts = [g[0] for g in group if g[0] is not None]
    operands = [h.reshape(1), start, weights, place, *shifts, *pieces]
    high = place.shape[1]
    most = max(len(moves(g[3])) for g in group)
    most_sides = max(len(sides_of(g[3])) for g in group)

    def kernel(h_ref, start_ref, w_ref, place_ref, *refs):
        shift_refs = list(refs[: len(shifts)])
        piece_refs = refs[len(shifts) : len(operands) - 4]
        last_ref, moved_ref, wide_ref, total_ref, held_ref = refs[len(operands) - 4 :]
        for g, (shift, first, rate, taps) in enumerate(group):
            steps, sides = moves(taps), sides_of(taps)
            s_ref = None if shift is None else shift_refs.pop(0)
            build_moved(piece_refs, moved_ref, s_ref, g, branches, valid, ha, prows, out)
            for i, b in enumerate(sides):
                for n, a in enumerate(steps):
                    wide_ref[i, n * out : (n + 1) * out] = w_ref[first + taps.index((a, b))]
            wide = len(steps) * out
            for i, b in enumerate(sides):

                def columns(w, count):
                    values = moved_ref[pl.ds(w - b * rate, count), :, :wide].reshape(count * pheight, wide)
                    part = dot(values, wide_ref[i, :wide], NN).reshape(count, pheight, deep)
                    if g or b != 0:
                        total_ref[pl.ds(w, count)] += part
                    else:
                        total_ref[pl.ds(w, count)] = part + start_ref[...][None]

                in_steps(*span(-b, rate, valid), 4, columns)
        held_ref[valid * prows :] = jnp.zeros((high - valid * prows, deep), BF16)
        for k in range(ha):
            block = total_ref[:, k * prows : (k + 1) * prows, :].astype(BF16)
            held_ref[: valid * prows] = block.reshape(valid * prows, deep)
            last_ref[h_ref[0] ^ k] = dot(place_ref[...], held_ref[...], NN).astype(BF16)

    return pl.pallas_call(
        kernel,
        out_shape=jax.ShapeDtypeStruct((ha, fit, deep), BF16),
        grid=(1,),
        in_specs=[SCALAR] + loaded(operands[1:]),
        out_specs=pl.BlockSpec((ha, fit, deep), lambda i: (0, 0, 0)),
        scratch_shapes=[
            pltpu.VMEM((valid, pheight, most * out), BF16),
            pltpu.VMEM((most_sides, most * out, deep), BF16),
            pltpu.VMEM(x.shape, F32),
            pltpu.VMEM((high, deep), BF16),
        ],
        compiler_params=WIDE,
        cost_estimate=NO_COST,
        name="features_backward",
    )(*operands)


def real_rows(pixels, prows, rows):
    return (lax.broadcasted_iota(jnp.int32, (pixels, 1), 0) % prows < rows).astype(F32)


def total_of(refs):
    return tree_sum([r[...] for r in refs])


def column_sum(values):
    return jnp.sum(values, axis=0, keepdims=True)


def small_kernel(kernel, name, operands, shapes):
    return pl.pallas_call(
        kernel,
        out_shape=[jax.ShapeDtypeStruct(s, t) for s, t in shapes],
        in_specs=[WHOLE] * len(operands),
        out_specs=[WHOLE] * len(shapes),
        compiler_params=PARAMS,
        cost_estimate=NO_COST,
        name=name,
    )(*operands)


def branch_sums(parts, pool_part):
    _, pixels, out = parts[0].shape
    images = pool_part.shape[0]

    def kernel(low, low_got, low_last, high, high_got, high_last, pool_ref, branch_ref, sum_ref):
        for j in range(4):
            own, got, last = (low, low_got, low_last) if j < 2 else (high, high_got, high_last)
            value = own[j % 2] + got[0, j % 2].astype(F32) + last[j % 2].astype(F32)
            branch_ref[j] = value
            sum_ref[j : j + 1] = column_sum(value)
            sum_ref[4 + j : 5 + j] = column_sum(value * value)
        sum_ref[8:] = pool_ref[...]

    shapes = [((4, pixels, out), F32), ((8 + images, out), F32)]
    return small_kernel(kernel, "branch_sums", [*parts, pool_part], shapes)


def project(sums, branch, scales, shifts, counts, own, proj, rows, pixel_total):
    _, pixels, out = branch.shape
    images = counts.shape[0]
    prows = own.shape[0]
    many = len(sums)

    def kernel(*refs):
        branch_ref, scale_ref, shift_ref, count_ref, own_ref, proj_ref = refs[many : many + 6]
        joined_ref, projected_ref, second_ref, stat_ref, pool_ref = refs[many + 6 :]
        total = total_of(refs[:many])
        mean = total[0:4] / pixel_total
        rstd = lax.rsqrt(total[4:8] / pixel_total - mean * mean + EPS)
        stat_ref[0:4] = mean
        stat_ref[4:8] = rstd
        scale, shift = scale_ref[...], shift_ref[...]
        for j in range(4):
            norm = (branch_ref[j] - mean[j : j + 1]) * rstd[j : j + 1]
            hid = norm * scale[j : j + 1] + shift[j : j + 1]
            joined_ref[:, j * out : (j + 1) * out] = silu(hid).astype(BF16)
        pool_out = total[8:]
        weighted = count_ref[...]
        pool_mean = column_sum(weighted * pool_out) / pixel_total
        pool_second = column_sum(weighted * pool_out * pool_out) / pixel_total
        pool_rstd = lax.rsqrt(pool_second - pool_mean * pool_mean + EPS)
        pool_norm = (pool_out - pool_mean) * pool_rstd
        pool_hid = pool_norm * scale[4:5] + shift[4:5]
        pool_ref[0] = pool_norm
        pool_ref[1] = pool_hid
        pool_ref[2] = jnp.broadcast_to(pool_rstd, pool_out.shape)
        pool_act = silu(pool_hid)
        spread = jnp.zeros((prows, out), F32)
        for i in range(images):
            spread = spread + own_ref[:, i : i + 1] * pool_act[i : i + 1]
        spread = spread.astype(BF16)
        for w in range(pixels // prows):
            joined_ref[w * prows : (w + 1) * prows, 4 * out :] = spread
        projected = dot(joined_ref[...], proj_ref[...], NN)
        projected_ref[...] = projected
        held = projected * real_rows(pixels, prows, rows)
        second_ref[...] = jnp.zeros(second_ref.shape, F32)
        second_ref[0:1] = column_sum(held)
        second_ref[1:2] = column_sum(held * held)

    shapes = [((pixels, 5 * out), BF16), ((pixels, out), F32), ((8, out), F32), ((8, out), F32), ((3, images, out), F32)]
    return small_kernel(kernel, "project", [*sums, branch, scales, shifts, counts, own, proj], shapes)


def activate(sums, projected, cot, out_scale, out_shift, prows, rows, pixel_total):
    pixels, out = projected.shape
    many = len(sums)

    def kernel(*refs):
        projected_ref, cot_ref, scale_ref, shift_ref = refs[many : many + 4]
        act_ref, norm_ref, dhid_ref, third_ref, rstd_ref = refs[many + 4 :]
        total = total_of(refs[:many])
        mean = total[0:1] / pixel_total
        rstd = lax.rsqrt(total[1:2] / pixel_total - mean * mean + EPS)
        rstd_ref[...] = jnp.broadcast_to(rstd, rstd_ref.shape)
        norm = (projected_ref[...] - mean) * rstd
        norm_ref[...] = norm
        hid = norm * scale_ref[...] + shift_ref[...]
        act_ref[...] = silu(hid).astype(BF16)
        dhid = cot_ref[...].astype(F32) * real_rows(pixels, prows, rows) * silu_slope(hid)
        dhid_ref[...] = dhid
        third_ref[...] = jnp.zeros(third_ref.shape, F32)
        third_ref[0:1] = column_sum(dhid)
        third_ref[1:2] = column_sum(dhid * norm)

    shapes = [((pixels, out), BF16), ((pixels, out), F32), ((pixels, out), F32), ((8, out), F32), ((8, out), F32)]
    operands = [*sums, projected, cot, out_scale[None], out_shift[None]]
    return small_kernel(kernel, "activate", operands, shapes)


def unproject(sums, norm, dhid, rstd, out_scale, proj, joined, branch, stats, scales, shifts, own, ha, rows, pixel_total):
    _, pixels, out = branch.shape
    prows, images = own.shape
    many = len(sums)

    def kernel(*refs):
        norm_ref, dhid_ref, rstd_ref, oscale_ref, proj_ref, joined_ref = refs[many : many + 6]
        branch_ref, stat_ref, scale_ref, shift_ref, own_ref = refs[many + 6 : many + 11]
        third_ref, grad_ref, back_ref, fourth_ref = refs[many + 11 :]
        total = total_of(refs[:many])
        third_ref[...] = total
        mask = real_rows(pixels, prows, rows)
        dproj = dhid_ref[...] - (total[0:1] + norm_ref[...] * total[1:2]) / pixel_total
        dproj = (oscale_ref[...] * rstd_ref[0:1] * dproj * mask).astype(BF16)
        grad = dot(joined_ref[...], dproj, TN)
        grad_ref[...] = jnp.zeros(grad_ref.shape, BF16)
        few = 5 * out // ha
        for d in range(ha):
            grad_ref[d, :, :few] = grad[d * few : (d + 1) * few].T.astype(BF16)
        for j in range(5):
            dact = dot(dproj, proj_ref[j * out : (j + 1) * out], NT)
            if j < 4:
                branch_norm = (branch_ref[j] - stat_ref[j : j + 1]) * stat_ref[4 + j : 5 + j]
                hid = branch_norm * scale_ref[j : j + 1] + shift_ref[j : j + 1]
                back = dact * silu_slope(hid) * mask
                back_ref[j] = back
                fourth_ref[j : j + 1] = column_sum(back)
                fourth_ref[4 + j : 5 + j] = column_sum(back * branch_norm)
            else:
                across = jnp.sum(dact.reshape(pixels // prows, prows, out), axis=0)
                for i in range(images):
                    fourth_ref[8 + i : 9 + i] = column_sum(own_ref[:, i : i + 1] * across)

    shapes = [((8, out), F32), ((ha, out, out), BF16), ((4, pixels, out), F32), ((8 + images, out), F32)]
    operands = [*sums, norm, dhid, rstd, out_scale[None], proj, joined, branch, stats, scales, shifts, own]
    return small_kernel(kernel, "unproject", operands, shapes)


def branch_gradients(sums, back, branch, stats, scales, counts, pool, prows, rows, pixel_total):
    _, pixels, out = branch.shape
    images = counts.shape[0]
    many = len(sums)

    def kernel(*refs):
        back_ref, branch_ref, stat_ref, scale_ref, count_ref, pool_ref = refs[many : many + 6]
        grad_ref, dpool_ref, sum_ref = refs[many + 6 :]
        total = total_of(refs[:many])
        mask = real_rows(pixels, prows, rows)
        for j in range(4):
            rstd = stat_ref[4 + j : 5 + j]
            norm = (branch_ref[j] - stat_ref[j : j + 1]) * rstd
            value = back_ref[j] - (total[j : j + 1] + norm * total[4 + j : 5 + j]) / pixel_total
            grad_ref[j] = (scale_ref[j : j + 1] * rstd * value * mask).astype(BF16)
        dhid = silu_slope(pool_ref[1]) * total[8:]
        pool_shift = column_sum(dhid)
        pool_scale = column_sum(dhid * pool_ref[0])
        value = dhid - count_ref[...] * (pool_shift + pool_ref[0] * pool_scale) / pixel_total
        dpool_ref[...] = (scale_ref[4:5] * pool_ref[2] * value).astype(BF16)
        sum_ref[...] = jnp.zeros(sum_ref.shape, F32)
        sum_ref[0:4] = total[4:8]
        sum_ref[4:5] = pool_scale
        sum_ref[5:9] = total[0:4]
        sum_ref[9:10] = pool_shift

    shapes = [((4, pixels, out), BF16), ((images, out), BF16), ((16, out), F32)]
    operands = [*sums, back, branch, stats, scales, counts, pool]
    return small_kernel(kernel, "branch_gradients", operands, shapes)


def local(
    features,
    row_image,
    cotangent,
    w_one,
    dilated_weight,
    w_pool,
    w_proj,
    scales,
    shifts,
    out_scale,
    out_shift,
):
    micro, rows, cols, channels = features.shape
    ha, wa = lax.axis_size("ha"), lax.axis_size("wa")
    h, z = lax.axis_index("ha"), lax.axis_index("wa")
    planes = wa // micro
    batch, part = z // planes, z % planes
    deep = w_one.shape[0] // planes
    out = w_one.shape[1] * wa
    valid = cols * wa - PADC
    blocks = -(-valid // cols)
    prows = -(-rows // 16) * 16
    height, pheight = rows * ha, prows * ha
    images = IMG_DEV * ha
    pixels = float(height * valid)
    size = cols * rows

    fast = planes == 1 and wa == 4 and 6 * valid * pheight * out < (16 << 20) and channels % out == 0 and deep == out

    taps = [live_taps(r, valid) for r in RATES]
    few = w_proj.shape[0]
    side = jnp.pad(w_proj.T, ((0, 0), (0, w_one.shape[0] - few)))
    turned = dilated_weight.swapaxes(2, 3)
    if fast:
        weights = pack_weights(w_one.T, turned, w_pool.T, side, taps)
    else:
        picked = [turned[j, 3 * (a + 1) + b + 1] for j in range(3) for a, b in taps[j]]
        weights = gather_columns(jnp.stack([w_one.T, *picked, w_pool.T, side]))

    if fast:
        slots = extract(features.transpose(1, 2, 0, 3), cotangent.transpose(1, 2, 0, 3), z)
        tall, fit = slots[0].shape[0], ceil_to(valid * rows, 16)
        early = gather_early(weights, slots[0])
        slots = [slots[0]] + [swap(slots[k], "wa", k, lambda i: i < blocks) for k in range(1, wa)]
        slots = after(slots, early)
        high, thick = ceil_to(blocks * tall, 128), ceil_to(fit, 128)
        in_piece = block_rows(high, tall, rows, cols, valid, rows)
        in_chunk = block_rows(high, tall, rows, cols, valid, prows)
        spots = spots_of(np.arange(fit), in_piece)
        cot_spots = spots_of(np.arange(valid * prows), in_chunk)
        send, cot = choose(slots, z, blocks, spots, cot_spots, deep)
        raw = lax.all_to_all(send, "ha", 0, 0, tiled=True)
    else:
        f = features.transpose(0, 2, 1, 3).reshape(micro, size, ha, planes, deep)
        f = f.transpose(0, 3, 1, 2, 4).reshape(wa, size, ha * deep)
        c = cotangent.transpose(0, 2, 1, 3).reshape(micro, size, out)
        load = jnp.concatenate([f, jnp.repeat(c, planes, axis=0)], axis=-1)
        slots = [take(load, z)]
        for k in range(1, wa):
            slots.append(swap(take(load, z ^ k), "wa", k, lambda i: i < blocks))
        slots = jnp.stack(slots)
        block = jnp.concatenate([take(slots, z ^ j) for j in range(blocks)])[: valid * rows]
        raw = block[:, : ha * deep].reshape(valid * rows, ha, deep).swapaxes(0, 1)
        raw = lax.all_to_all(raw, "ha", 0, 0, tiled=True)
        cot = block[:, ha * deep :].reshape(valid, rows, out)
        cot = jnp.pad(cot, ((0, 0), (0, prows - rows), (0, 0))).reshape(valid * prows, out)
    if fast:
        weights = gather_late(weights, early, send)
    if fast:
        proj = order_chunks(*gather_chunks(weights[-1]), h, few)
    else:
        proj = in_order(*gather_chunks(weights[-1]))[..., :few].swapaxes(1, 2).reshape(ha * few, out)
    if planes > 1:
        weights = lax.dynamic_slice_in_dim(weights, part * deep, deep, 2)
    wide_pool = weights[-2]

    order = h ^ jnp.arange(ha, dtype=jnp.int32)
    labels = by_distance(take(row_image, batch).reshape(ha, rows))
    number = order[:, None] * rows + jnp.arange(rows, dtype=jnp.int32)[None, :]
    pad = ((0, 0), (0, prows - rows))
    labels = jnp.pad(labels, pad, constant_values=-1).reshape(pheight)
    number = jnp.pad(number, pad, constant_values=-(1 << 20)).reshape(pheight)
    same = (labels[:, None] == labels[None, :]) & (labels >= 0)[:, None]
    apart = number[None, :] - number[:, None]
    shift = [
        jnp.stack([(same & (apart == a * r)).astype(BF16) for a in (-1, 1)]) for r in RATES
    ]
    ids = jnp.arange(images, dtype=jnp.int32)
    member = (labels[:, None] == ids[None, :]).astype(F32)
    counts = jnp.sum(member, axis=0) * valid
    own = member[:prows]
    mask = jnp.tile(jnp.sum(own, axis=1), valid)[:, None]

    ahead = [1, 1 + len(taps[0]), 1 + len(taps[0]) + len(taps[1])]
    group = [(None, 0, 0, [(0, 0)])] + [(shift[j], ahead[j], RATES[j], taps[j]) for j in range(3)]
    if fast:
        place = spots_of(padded_rows(valid * prows, valid, prows, rows), np.arange(thick))
        x, row_sums = arrange(raw, place, h, valid, prows)
        unplace = spots_of(np.arange(fit), padded_rows(ceil_to(valid * prows, 128), valid, prows, rows))
    else:
        x = by_distance(raw).reshape(ha, valid, rows, deep)
        x = jnp.pad(x, ((0, 0), (0, 0), (0, prows - rows), (0, 0)))
        x = x.swapaxes(0, 1).reshape(valid, pheight, deep)
        row_sums = jnp.sum(x.astype(F32), axis=0)
    if fast:
        branch_parts = reduce_square(*forward_kernel(x, weights, group, prows))
    else:
        sums = jnp.stack([forward_plain(x, s, weights[n : n + len(t)], r, t) for s, n, r, t in group])
        sums = sums.astype(BF16).reshape(len(group), valid, ha // 2, 2, prows, out)
        sums = sums.transpose(3, 2, 0, 1, 4, 5).reshape(2, ha // 2, len(group), valid * prows, out)
        branch = sum_chunks(spread_chunks(sums[0], sums[1]), planes)
    pooled = (jnp.dot(member.T, row_sums, precision=HIGHEST) / counts[:, None]).astype(BF16)
    pool_part = dot(pooled, wide_pool, NT)

    weighted = counts[:, None]
    once = (part == 0).astype(F32)
    if fast:
        branch, first = branch_sums(branch_parts, pool_part)
        joined, projected, second, stats, pool = project(
            plane_parts(first), branch, scales, shifts, weighted, own, proj, rows, pixels
        )
        activation, proj_norm, dproj_hid, third, proj_rstd = activate(
            plane_parts(second), projected, cot, out_scale, out_shift, prows, rows, pixels
        )
        third, grad_proj, dhid, fourth = unproject(
            plane_parts(third),
            proj_norm,
            dproj_hid,
            proj_rstd,
            out_scale,
            proj,
            joined,
            branch,
            stats,
            scales,
            shifts,
            own,
            ha,
            rows,
            pixels,
        )
        dbranch, dpool, sums = branch_gradients(
            plane_parts(fourth), dhid, branch, stats, scales, weighted, pool, prows, rows, pixels
        )
        sums = jnp.concatenate([sums[:10], third[:2]])
    else:
        first = plane_sum(
            jnp.concatenate(
                [once * jnp.sum(branch, axis=1), once * jnp.sum(branch * branch, axis=1), pool_part]
            ),
            planes,
        )
        mean = first[0:4] / pixels
        rstd = lax.rsqrt(first[4:8] / pixels - mean * mean + EPS)
        pool_out = first[8:]
        norm = (branch - mean[:, None]) * rstd[:, None]
        hid = norm * scales[:4, None] + shifts[:4, None]
        act = silu(hid)
        weighted = counts[:, None]
        pool_mean = jnp.sum(weighted * pool_out, axis=0) / pixels
        pool_second = jnp.sum(weighted * pool_out * pool_out, axis=0) / pixels
        pool_rstd = lax.rsqrt(pool_second - pool_mean * pool_mean + EPS)
        pool_norm = (pool_out - pool_mean) * pool_rstd
        pool_hid = pool_norm * scales[4] + shifts[4]
        spread = jnp.dot(own, silu(pool_hid), precision=HIGHEST)
        spread = jnp.broadcast_to(spread[None], (valid, prows, out)).reshape(valid * prows, out)
        joined = jnp.concatenate([act[0], act[1], act[2], act[3], spread], axis=-1).astype(BF16)
        projected = jnp.dot(joined, proj, preferred_element_type=F32)

        held = projected * mask
        second = plane_sum(
            jnp.stack([jnp.sum(held, axis=0), jnp.sum(held * held, axis=0)]) * once, planes
        )
        proj_mean = second[0] / pixels
        proj_rstd = lax.rsqrt(second[1] / pixels - proj_mean * proj_mean + EPS)
        proj_norm = (projected - proj_mean) * proj_rstd
        proj_hid = proj_norm * out_scale + out_shift
        activation = silu(proj_hid).astype(BF16)
        dproj_hid = cot.astype(F32) * mask * silu_slope(proj_hid)
        third = plane_sum(
            jnp.stack([jnp.sum(dproj_hid, axis=0), jnp.sum(dproj_hid * proj_norm, axis=0)]) * once, planes
        )
        dproj = (
            out_scale * proj_rstd * (dproj_hid - (third[0] + proj_norm * third[1]) / pixels) * mask
        ).astype(BF16)
        djoined = lax.dot_general(dproj, proj, (((1,), (1,)), ((), ())), preferred_element_type=F32)
        grad_proj = dot(dproj, joined, TN)
        dact = jnp.stack([djoined[:, j * out : (j + 1) * out] for j in range(4)])
        dspread = jnp.sum(djoined[:, 4 * out :].reshape(valid, prows, out), axis=0)
        image_part = jnp.dot(own.T, dspread, precision=HIGHEST)
        dhid = dact * silu_slope(hid) * mask
        fourth = plane_sum(
            jnp.concatenate([jnp.sum(dhid, axis=1), jnp.sum(dhid * norm, axis=1), image_part]) * once,
            planes,
        )
        branch_shift, branch_scale, image_total = fourth[0:4], fourth[4:8], fourth[8:]
        dbranch = (
            (scales[:4] * rstd)[:, None]
            * (dhid - (branch_shift[:, None] + norm * branch_scale[:, None]) / pixels)
            * mask
        ).astype(BF16)
        dpool_hid = silu_slope(pool_hid) * image_total
        pool_shift = jnp.sum(dpool_hid, axis=0)
        pool_scale = jnp.sum(dpool_hid * pool_norm, axis=0)
        dpool = (
            scales[4] * pool_rstd * (dpool_hid - weighted * (pool_shift + pool_norm * pool_scale) / pixels)
        ).astype(BF16)
        sums = jnp.concatenate([branch_scale, pool_scale[None], branch_shift, pool_shift[None], third])
    grad_pool = dot(dpool, pooled, TN)
    dpooled = dot(dpool, wide_pool, NN)

    total = jnp.dot(member, dpooled / counts[:, None], precision=HIGHEST)
    if fast:
        pieces = gather_square(dbranch)
        tap_grads = weights_backward(x, group, pieces, wa, prows)
        back = features_backward(x, weights, group, pieces, total, h, unplace, fit, prows)
    else:
        total = jnp.broadcast_to(total[None], (valid,) + total.shape)
        near, far = gather_chunks(dbranch)
        every = jnp.stack([near, far], axis=1).reshape(ha, len(group), valid, prows, out)
        every = every.transpose(1, 2, 0, 3, 4).reshape(len(group), valid, pheight, out)
        found = []
        for (s, n, r, t), d in zip(group, every):
            grads, total = backward_plain(x, s, weights[n : n + len(t)], r, t, d, total)
            found.append(grads.reshape(len(t), wa, out // wa, deep).swapaxes(0, 1).astype(BF16))
        tap_grads = jnp.concatenate(found, axis=1)
        back = total.astype(BF16).reshape(valid, ha, prows, deep)[:, :, :rows]
        back = back.swapaxes(0, 1).reshape(ha, valid * rows, deep)
        back = by_distance(back)

    def in_place(grads):
        if planes == 1:
            return grads
        full = jnp.zeros(grads.shape[:-1] + (deep * planes,), grads.dtype)
        return lax.dynamic_update_slice_in_dim(full, grads, part * deep, grads.ndim - 1)

    if not fast:
        grad_proj = (grad_proj * once).reshape(out, ha, few).swapaxes(0, 1)
        grad_proj = jnp.pad(grad_proj, ((0, 0), (0, 0), (0, w_one.shape[0] - few))).astype(BF16)
    proj_chunk = lax.psum_scatter(grad_proj, "ha", scatter_dimension=0, tiled=False)
    grad_pool = in_place(grad_pool.astype(BF16)).reshape(wa, 1, out // wa, -1)
    proj_chunk = proj_chunk.reshape(wa, 1, out // wa, -1)
    tap_grads = line_scatter(in_place(tap_grads))
    rest = jnp.concatenate([grad_pool, proj_chunk], axis=1)
    if not fast:
        rest = line_scatter(rest)
    tap_out = [tap_grads[n : n + len(t)] for n, t in zip(ahead, taps)]
    blank = jnp.zeros((out // wa, w_one.shape[0]), F32)
    atrous = []
    for j in range(3):
        if len(taps[j]) == 9:
            atrous.append(tap_out[j])
        else:
            found = {3 * (a + 1) + b + 1: tap_out[j][t] for t, (a, b) in enumerate(taps[j])}
            atrous.append(jnp.stack([found.get(t, blank) for t in range(9)]))
    atrous = jnp.stack(atrous)
    atrous_out = atrous.swapaxes(2, 3)
    back = lax.all_to_all(back, "ha", 0, 0, tiled=True)

    def home(i, k):
        return i ^ k < blocks

    if fast:
        piece_spots = spots_of(block_rows(wa * tall, tall, rows, cols, valid, rows), np.arange(thick))
        chunk_spots = spots_of(block_rows(wa * tall, tall, rows, cols, valid, prows), np.arange(valid * prows))
        got = unchoose(
            back, activation, z, blocks, piece_spots.reshape(wa, tall, thick), chunk_spots.reshape(wa, tall, -1)
        )
        got = [got[0]] + [swap(got[k], "wa", k, partial(home, k=k)) for k in range(1, wa)]
        df, acts = interleave(got, z, blocks, rows, cols, out, [atrous])
        wide = jnp.broadcast_to(jnp.pad(sums, ((0, 4), (0, 0)))[None], (wa, 16, out))
        rest = jnp.concatenate([rest.astype(F32).reshape(wa, -1, out), wide], axis=1)
        rest = exchange_sum(after(rest, got[0]))
        sums = rest[-16:-4]
        rest = rest[:-16].reshape(2, -1, out)
    else:

        def send_home(array):
            array = jnp.pad(array, ((0, wa * size - valid * rows), (0, 0))).reshape(wa, size, -1)
            got = [take(array, z)]
            got += [swap(take(array, z ^ k), "wa", k, partial(home, k=k)) for k in range(1, wa)]
            got = jnp.stack(got)
            got = jnp.where(z < blocks, got, jnp.zeros((), got.dtype))
            return jnp.stack([take(got, z ^ t) for t in range(wa)])

        back = back.swapaxes(0, 1).reshape(valid * rows, ha * deep)
        df = send_home(back).reshape(micro, planes, cols, rows, ha, deep)
        df = df.transpose(0, 3, 2, 4, 1, 5).reshape(features.shape)
        activation = activation.reshape(valid, prows, out)[:, :rows].reshape(valid * rows, out)
        acts = send_home(activation).reshape(micro, planes, cols, rows, out)[:, 0].swapaxes(1, 2)
    if not fast:
        sums = sums * once
        sums = tree_sum([sums] + [swap(sums, "wa", k) for k in range(1, wa)])
    one_out, pool_grad_out, proj_out = tap_grads[0].T, rest[0].T, rest[1][:, :few].T
    return (
        acts,
        df,
        one_out,
        atrous_out,
        pool_grad_out,
        proj_out,
        sums[0:5],
        sums[5:10],
        sums[11],
        sums[10],
    )


def solution(mesh):
    specs = (
        P(None, "ha", "wa", None),
        P(),
        P(None, "ha", "wa", None),
        P("ha", "wa"),
        P(None, None, "ha", "wa"),
        P("ha", "wa"),
        P("ha", "wa"),
        P(),
        P(),
        P(),
        P(),
    )
    out_specs = (
        P(None, "ha", "wa", None),
        P(None, "ha", "wa", None),
        P("ha", "wa"),
        P(None, None, "ha", "wa"),
        P("ha", "wa"),
        P("ha", "wa"),
        P(),
        P(),
        P(),
        P(),
    )
    return jax.shard_map(local, mesh=mesh, in_specs=specs, out_specs=out_specs, check_vma=False)
```

```python
from functools import partial

import jax
import jax.numpy as jnp
import numpy as np
from jax import lax
from jax.experimental import pallas as pl
from jax.experimental.pallas import tpu as pltpu
from jax.sharding import PartitionSpec as P

PADC = 7
IMG_DEV = 2
RATES = (6, 12, 18)
EPS = 1e-05
HIGHEST = lax.Precision.HIGHEST
F32 = jnp.float32
BF16 = jnp.bfloat16


def silu(u):
    return u * jax.nn.sigmoid(u)


def silu_slope(u):
    s = jax.nn.sigmoid(u)
    return s * (1.0 + u * (1.0 - s))


def swap(array, axis, bits, sources=None):
    count = lax.axis_size(axis)
    pairs = [(i, i ^ bits) for i in range(count) if sources is None or sources(i)]
    return lax.ppermute(array, axis, pairs)


def after(value, *others):
    return lax.optimization_barrier((value, *others))[0]


def tree_sum(parts):
    while len(parts) > 1:
        parts = [parts[i] + parts[i + 1] for i in range(0, len(parts), 2)]
    return parts[0]


def plane_parts(array):
    pair = array + swap(array, "ha", 1)
    return [pair] + [swap(pair, "ha", k) for k in range(2, lax.axis_size("ha"), 2)]


def plane_sum(array, groups):
    total = tree_sum(plane_parts(array))
    bits = 1
    while bits < groups:
        total = total + swap(total, "wa", bits)
        bits *= 2
    return total


def take(array, index):
    return lax.dynamic_index_in_dim(array, index, 0, keepdims=False)


def by_distance(array):
    h = lax.axis_index("ha")
    return jnp.stack([take(array, h ^ k) for k in range(array.shape[0])])


def spread_chunks(even, odd):
    other = swap(odd, "ha", 1)
    both = [even[q].astype(F32) + other[q].astype(F32) for q in range(even.shape[0])]
    return both[:1] + [swap(both[q].astype(BF16), "ha", 2 * q) for q in range(1, len(both))]


def sum_chunks(parts, groups):
    total = tree_sum([part.astype(F32) for part in parts])
    bits = 1
    while bits < groups:
        total = total + swap(total.astype(BF16), "wa", bits).astype(F32)
        bits *= 2
    return total


def reduce_square(even, odd):
    other = swap(odd, "ha", 1)
    half = even.shape[1] // 2
    low = even[:, :half].astype(F32) + other[:, :half].astype(F32)
    high = even[:, half:].astype(F32) + other[:, half:].astype(F32)
    low_got = swap(low[1::2].astype(BF16), "ha", 2)
    high_got = swap(high[2:].astype(BF16), "ha", 4)
    low_last = swap((low[2] + low_got[1].astype(F32)).astype(BF16), "ha", 4)
    high_last = swap((high[1] + high_got[1].astype(F32)).astype(BF16), "ha", 2)
    return low[0], low_got, low_last, high[0], high_got, high_last


def gather_square(chunk):
    half = chunk.shape[0] // 2
    low, high = chunk[:half], chunk[half:]
    low_one = swap(low, "ha", 2)
    high_one = swap(high, "ha", 4)
    low_two = swap(jnp.stack([low, low_one]), "ha", 4)
    high_two = swap(jnp.stack([high, high_one]), "ha", 2)
    near = [chunk, low_one, high_one, low_two, high_two]
    return near + [swap(piece, "ha", 1) for piece in near]


def piece_of(k, branch, branches):
    q, half = k // 2, branches // 2
    first = 5 * (k % 2)
    low = branch < half
    inner = branch if low else branch - half
    if q == 0:
        return first, (branch,)
    if q == (1 if low else 2):
        return first + (1 if low else 2), (inner,)
    return first + (3 if low else 4), (int(q == 3), inner)


def gather_near(chunk):
    return [chunk] + [swap(chunk, "ha", 2 * q) for q in range(1, lax.axis_size("ha") // 2)]


def gather_chunks(chunk):
    near = jnp.stack(gather_near(chunk))
    return near, swap(near, "ha", 1)


def in_order(near, far):
    every = jnp.stack([near, far], axis=1)
    return by_distance(every.reshape((2 * near.shape[0],) + near.shape[1:]))


def gather_columns(own):
    gathered = lax.all_gather(own, "wa", axis=0, tiled=False)
    planes, count, few, rows = gathered.shape
    return gathered.swapaxes(0, 1).reshape(count, planes * few, rows)


def neighbour(array, pairs):
    return lax.ppermute(array, "wa", pairs)


def gather_early(own, others):
    right = neighbour(own, [(0, 1), (1, 2), (2, 3)])
    left = neighbour(own, [(1, 0), (2, 1), (3, 2)])
    right_two = neighbour(after(right, others), [(2, 3)])
    left_two = neighbour(after(left, others), [(1, 0), (2, 1)])
    return right, left, right_two, left_two


def gather_late(own, early, *others):
    z = lax.axis_index("wa")
    right, left, right_two, left_two = early
    left_three = neighbour(left_two, [(1, 0)])
    last_two = neighbour(after(right, *others), [(1, 2)])
    last_three = neighbour(last_two, [(2, 3)])
    found = [
        lax.select_n(z, own, right, last_two, last_three),
        lax.select_n(z, left, own, right, right_two),
        lax.select_n(z, left_two, left, own, right),
        lax.select_n(z, left_three, left_two, left, own),
    ]
    return jnp.concatenate(found, axis=1)


def exchange_sum(parts):
    z = lax.axis_index("wa")
    got = [swap(take(parts, z ^ k), "wa", k) for k in range(1, lax.axis_size("wa"))]
    return tree_sum([take(parts, z)] + got)


def line_scatter(parts):
    return lax.psum_scatter(parts, "wa", scatter_dimension=0, tiled=False).astype(F32)


def live_taps(rate, valid):
    return [(a, b) for a in (-1, 0, 1) for b in (-1, 0, 1) if b == 0 or valid > rate]


def span(b, rate, valid):
    return max(0, -b * rate), min(valid, valid - b * rate)


def moves(taps):
    return sorted({a for a, b in taps})


def forward_plain(x, shift, weights, rate, taps):
    valid = x.shape[0]
    moved = {
        a: x if a == 0 else jnp.einsum("pq,wqk->wpk", shift[(a + 1) // 2], x) for a in moves(taps)
    }
    out = jnp.zeros(x.shape[:2] + (weights.shape[1],), F32)
    for t, (a, b) in enumerate(taps):
        low, high = span(b, rate, valid)
        part = jnp.einsum(
            "wpk,ek->wpe", moved[a][low + b * rate : high + b * rate], weights[t], preferred_element_type=F32
        )
        out = out.at[low:high].add(part)
    return out


def backward_plain(x, shift, weights, rate, taps, grad, total):
    valid = x.shape[0]
    moved = {
        a: grad if a == 0 else jnp.einsum("pq,wqe->wpe", shift[(1 - a) // 2], grad)
        for a in moves(taps)
    }
    weight_grads = []
    for t, (a, b) in enumerate(taps):
        low, high = span(b, rate, valid)
        d = moved[a][low:high]
        source = slice(low + b * rate, high + b * rate)
        weight_grads.append(jnp.einsum("wpe,wpk->ek", d, x[source], preferred_element_type=F32))
        total = total.at[source].add(
            jnp.einsum("wpe,ek->wpk", d, weights[t], preferred_element_type=F32)
        )
    return jnp.stack(weight_grads), total


def dot(left, right, dims):
    return lax.dot_general(left, right, ((dims[0], dims[1]), ((), ())), preferred_element_type=F32)


NN = ((1,), (0,))
NT = ((1,), (1,))
TN = ((0,), (0,))
WHOLE = pl.BlockSpec(memory_space=pltpu.VMEM)
SCALAR = pl.BlockSpec(memory_space=pltpu.SMEM)
NO_COST = pl.CostEstimate(flops=0, bytes_accessed=0, transcendentals=0)
WIDE = pltpu.CompilerParams(vmem_limit_bytes=60 * 1024 * 1024)
PARAMS = pltpu.CompilerParams(vmem_limit_bytes=32 * 1024 * 1024)


def ceil_to(n, step):
    return -(-n // step) * step


def pack_weights(w_one, dilated, w_pool, w_proj, taps):
    rows, deep = w_one.shape
    order = [(j, 3 * (a + 1) + b + 1) for j in range(3) for a, b in taps[j]]

    def kernel(one_ref, dilated_ref, pool_ref, proj_ref, out_ref):
        out_ref[0] = one_ref[...]
        for at, (j, t) in enumerate(order):
            out_ref[at + 1] = dilated_ref[j, t]
        out_ref[len(order) + 1] = pool_ref[...]
        out_ref[len(order) + 2] = proj_ref[...]

    return pl.pallas_call(
        kernel,
        out_shape=jax.ShapeDtypeStruct((len(order) + 3, rows, deep), BF16),
        in_specs=[WHOLE] * 4,
        out_specs=WHOLE,
        compiler_params=PARAMS,
        name="pack_weights",
    )(w_one, dilated, w_pool, w_proj)


def spots_of(wanted, held):
    return ((wanted[:, None] == held[None, :]) & (wanted >= 0)[:, None]).astype(BF16)


def block_rows(count, tall, rows, cols, valid, pitch):
    row = np.arange(count)
    column = row // tall * cols + row % tall % cols
    real = (row % tall < rows * cols) & (column < valid)
    return np.where(real, column * pitch + row % tall // cols, -1)


def padded_rows(count, valid, prows, rows):
    row = np.arange(count)
    real = (row < valid * prows) & (row % prows < rows)
    return np.where(real, row // prows * rows + row % prows, -1)


def extract(features, cotangent, z):
    rows, cols, micro, channels = features.shape
    out = cotangent.shape[-1]
    size = rows * cols
    tall = ceil_to(size, 16)
    steps = channels // out

    def kernel(z_ref, f_ref, c_ref, *refs):
        outs, held_ref = refs[:-1], refs[-1]
        held_ref[:, size // 8 * 8 :] = jnp.zeros((micro, tall - size // 8 * 8, out), F32)

        def put(ref):
            values = ref[...]
            for m in range(micro):
                held_ref[m, :size] = values[:, m, :].astype(F32)
            for k in range(micro):
                outs[k][...] = held_ref[z_ref[0] ^ k].astype(BF16)

        @pl.when(pl.program_id(0) < steps)
        def _():
            put(f_ref)

        @pl.when(pl.program_id(0) == steps)
        def _():
            put(c_ref)

    return pl.pallas_call(
        kernel,
        grid=(steps + 1,),
        out_shape=[jax.ShapeDtypeStruct((tall, channels + out), BF16)] * micro,
        in_specs=[
            SCALAR,
            pl.BlockSpec((size, micro, out), lambda i: (0, 0, jnp.minimum(i, steps - 1))),
            pl.BlockSpec((size, micro, out), lambda i: (0, 0, 0)),
        ],
        out_specs=[pl.BlockSpec((tall, out), lambda i: (0, i))] * micro,
        scratch_shapes=[pltpu.VMEM((micro, tall, out), F32)],
        compiler_params=PARAMS,
        name="extract",
    )(z.reshape(1), features.reshape(size, micro, channels), cotangent.reshape(size, micro, out))


def choose(slots, z, blocks, spots, last_spots, lanes):
    tall, wide = slots[0].shape
    high = spots.shape[1]
    count = wide // lanes - 1

    def kernel(z_ref, *refs):
        spots_ref, last_ref, send_ref, own_ref, held_ref = refs[len(slots) :]
        for v in range(len(slots)):

            @pl.when(z_ref[0] == v)
            def _():
                for j in range(blocks):
                    held_ref[j * tall : (j + 1) * tall] = refs[v ^ j][...]

        held_ref[blocks * tall :] = jnp.zeros((high - blocks * tall, wide), BF16)
        for d in range(count):
            part = held_ref[:, d * lanes : (d + 1) * lanes]
            send_ref[d] = dot(spots_ref[...], part, NN).astype(BF16)
        own_ref[...] = dot(last_ref[...], held_ref[:, count * lanes :], NN).astype(BF16)

    return pl.pallas_call(
        kernel,
        out_shape=[
            jax.ShapeDtypeStruct((count, spots.shape[0], lanes), BF16),
            jax.ShapeDtypeStruct((last_spots.shape[0], lanes), BF16),
        ],
        in_specs=[SCALAR] + [WHOLE] * (len(slots) + 2),
        out_specs=[WHOLE] * 2,
        scratch_shapes=[pltpu.VMEM((high, wide), BF16)],
        compiler_params=PARAMS,
        name="choose",
    )(z.reshape(1), *slots, spots, last_spots)


def unchoose(pieces, last, z, blocks, spots, last_spots):
    ha, fit, out = pieces.shape
    planes, tall, thick = spots.shape
    wide = (ha + 1) * out

    def kernel(z_ref, pieces_ref, last_ref, spots_ref, last_spots_ref, *refs):
        outs, held_ref = refs[:-1], refs[-1]
        held_ref[fit:] = jnp.zeros((thick - fit, ha * out), BF16)
        for d in range(ha):
            held_ref[:fit, d * out : (d + 1) * out] = pieces_ref[d]
        for v in range(planes):

            @pl.when(z_ref[0] == v)
            def _():
                for j in range(planes):
                    if j < blocks:
                        outs[v ^ j][:, : ha * out] = dot(spots_ref[j], held_ref[...], NN).astype(BF16)
                        outs[v ^ j][:, ha * out :] = dot(last_spots_ref[j], last_ref[...], NN).astype(BF16)
                    else:
                        outs[v ^ j][...] = jnp.zeros((tall, wide), BF16)

    return pl.pallas_call(
        kernel,
        out_shape=[jax.ShapeDtypeStruct((tall, wide), BF16)] * planes,
        in_specs=[SCALAR] + [WHOLE] * 4,
        out_specs=[WHOLE] * planes,
        scratch_shapes=[pltpu.VMEM((thick, ha * out), BF16)],
        compiler_params=PARAMS,
        name="unchoose",
    )(z.reshape(1), pieces, last, spots, last_spots)


def order_chunks(near, far, h, few):
    half, out, _ = near.shape

    def kernel(h_ref, near_ref, far_ref, out_ref):
        for k in range(2 * half):
            chunk = (far_ref if k % 2 else near_ref)[k // 2]
            at = pl.multiple_of((h_ref[0] ^ k) * few, 16)
            out_ref[pl.ds(at, few), :] = chunk.T[:few]

    return pl.pallas_call(
        kernel,
        out_shape=jax.ShapeDtypeStruct((2 * half * few, out), BF16),
        in_specs=[SCALAR, WHOLE, WHOLE],
        out_specs=WHOLE,
        compiler_params=PARAMS,
        cost_estimate=NO_COST,
        name="order_chunks",
    )(h.reshape(1), near, far)


def interleave(got, z, blocks, rows, cols, out, others):
    micro = len(got)
    tall, channels = got[0].shape
    channels -= out
    size = rows * cols
    lanes = 2 * out

    def kernel(z_ref, *refs):
        df_ref, act_ref, held_ref = refs[-3:]

        def place(parts, wide):
            for k in range(micro):
                part = jnp.where(z_ref[0] < blocks, parts[k][...], jnp.zeros((), BF16))
                held_ref[z_ref[0] ^ k, :, :wide] = part
            return jnp.stack([held_ref[m, :, :wide][:size] for m in range(micro)], axis=1)

        @pl.when(pl.program_id(0) == 0)
        def _():
            act_ref[...] = place(refs[micro : 2 * micro], out)

        df_ref[...] = place(refs[:micro], lanes)

    df, act = pl.pallas_call(
        kernel,
        grid=(channels // lanes,),
        out_shape=[jax.ShapeDtypeStruct((size, micro, n), BF16) for n in (channels, out)],
        in_specs=[SCALAR]
        + [pl.BlockSpec((tall, lanes), lambda i: (0, i))] * micro
        + [pl.BlockSpec((tall, out), lambda i: (0, channels // out))] * micro
        + [pl.BlockSpec(memory_space=pl.ANY)] * len(others),
        out_specs=[
            pl.BlockSpec((size, micro, lanes), lambda i: (0, 0, i)),
            pl.BlockSpec((size, micro, out), lambda i: (0, 0, 0)),
        ],
        scratch_shapes=[pltpu.VMEM((micro, tall, lanes), BF16)],
        compiler_params=PARAMS,
        name="interleave",
    )(z.reshape(1), *got, *got, *others)
    return [a.reshape(rows, cols, micro, -1).transpose(2, 0, 1, 3) for a in (df, act)]


def arrange(raw, place, h, valid, prows):
    ha, tall, deep = raw.shape
    high = place.shape[1]

    def kernel(h_ref, raw_ref, place_ref, x_ref, sum_ref, held_ref):
        held_ref[tall:] = jnp.zeros((high - tall, deep), BF16)
        for k in range(ha):
            held_ref[:tall] = raw_ref[h_ref[0] ^ k]
            block = dot(place_ref[...], held_ref[...], NN).reshape(valid, prows, deep)
            x_ref[:, k * prows : (k + 1) * prows, :] = block.astype(BF16)
            sum_ref[k * prows : (k + 1) * prows] = jnp.sum(block, axis=0)

    return pl.pallas_call(
        kernel,
        out_shape=[
            jax.ShapeDtypeStruct((valid, ha * prows, deep), BF16),
            jax.ShapeDtypeStruct((ha * prows, deep), F32),
        ],
        in_specs=[SCALAR, WHOLE, WHOLE],
        out_specs=[WHOLE, WHOLE],
        scratch_shapes=[pltpu.VMEM((high, deep), BF16)],
        compiler_params=PARAMS,
        name="arrange",
    )(h.reshape(1), raw, place)


def sides_of(taps):
    return sorted({b for a, b in taps}, key=abs)


def in_steps(low, high, step, body):
    whole = (high - low) // step
    if whole:

        def one(i, carry):
            body(low + i * step, step)
            return carry

        lax.fori_loop(0, whole, one, 0)
    if (high - low) % step:
        body(low + whole * step, (high - low) % step)


def forward_kernel(x, weights, group, prows):
    valid, pheight, deep = x.shape
    out = weights.shape[1]
    half = pheight // prows // 2
    operands, flops = [x, weights], 0
    for shift, first, rate, taps in group:
        operands += [] if shift is None else [shift]
        spans = [span(b, rate, valid) for a, b in taps]
        flops += 2 * pheight * deep * out * sum(high - low for low, high in spans)
    most = max(len(moves(g[3])) for g in group)
    most_sides = max(len(sides_of(g[3])) for g in group)

    def kernel(x_ref, w_ref, *refs):
        ins = list(refs[: len(operands) - 2])
        even_ref, odd_ref, moved_ref, wide_ref, sum_ref = refs[len(operands) - 2 :]
        for g, (shift, first, rate, taps) in enumerate(group):
            steps, sides = moves(taps), sides_of(taps)
            for i, b in enumerate(sides):
                for n, a in enumerate(steps):
                    wide_ref[i, :, n * deep : (n + 1) * deep] = w_ref[first + taps.index((a, b))]
            source_ref = x_ref
            if shift is not None:
                s_ref = ins.pop(0)
                source_ref = moved_ref

                def move(w, carry):
                    values = x_ref[w]
                    both = dot(s_ref[...].reshape(2 * pheight, pheight), values, NN).astype(BF16)
                    moved_ref[w, :, :deep] = both[:pheight]
                    moved_ref[w, :, deep : 2 * deep] = values
                    moved_ref[w, :, 2 * deep :] = both[pheight:]
                    return carry

                lax.fori_loop(0, valid, move, 0, unroll=True)

            for i, b in enumerate(sides):

                def columns(w, count):
                    values = source_ref[pl.ds(w + b * rate, count)].reshape(count * pheight, -1)
                    part = dot(values, wide_ref[i, :, : len(steps) * deep], NT)
                    part = part.reshape(count, pheight, out)
                    if b == 0:
                        sum_ref[pl.ds(w, count)] = part
                    else:
                        sum_ref[pl.ds(w, count)] += part

                in_steps(*span(b, rate, valid), 7, columns)

            def store(w, carry):
                at = pl.multiple_of(w * prows, prows)
                for k in range(2 * half):
                    to = odd_ref if k % 2 else even_ref
                    to[k // 2, g, pl.ds(at, prows), :] = sum_ref[w, k * prows : (k + 1) * prows].astype(BF16)
                return carry

            lax.fori_loop(0, valid, store, 0, unroll=True)

    shape = jax.ShapeDtypeStruct((half, len(group), valid * prows, out), BF16)
    return pl.pallas_call(
        kernel,
        out_shape=[shape] * 2,
        in_specs=[WHOLE] * len(operands),
        out_specs=[WHOLE] * 2,
        scratch_shapes=[
            pltpu.VMEM((valid, pheight, most * deep), BF16),
            pltpu.VMEM((most_sides, out, most * deep), BF16),
            pltpu.VMEM((valid, pheight, out), F32),
        ],
        compiler_params=PARAMS,
        cost_estimate=NO_COST,
        name="forward",
    )(*operands)


def loaded(operands):
    return [
        pl.BlockSpec(a.shape, lambda i, n=a.ndim: (0,) * n, pipeline_mode=pl.Buffered(1)) for a in operands
    ]


def build_moved(pieces, moved_ref, s_ref, g, branches, valid, ha, prows, out):
    middle = 0 if s_ref is None else out

    def move(w, carry):
        at = pl.multiple_of(w * prows, prows)
        for k in range(ha):
            piece, index = piece_of(k, g, branches)
            rows = slice(k * prows, (k + 1) * prows)
            moved_ref[w, rows, middle : middle + out] = pieces[piece][(*index, pl.ds(at, prows))]
        if s_ref is not None:
            held = moved_ref[w, :, out : 2 * out]
            both = dot(s_ref[...].reshape(2 * ha * prows, ha * prows), held, NN).astype(BF16)
            moved_ref[w, :, :out] = both[ha * prows :]
            moved_ref[w, :, 2 * out :] = both[: ha * prows]
        return carry

    lax.fori_loop(0, valid, move, 0, unroll=True)


def weights_backward(x, group, pieces, wa, prows):
    valid, pheight, deep = x.shape
    out = pieces[0].shape[-1]
    few, ha, branches = out // wa, pheight // prows, len(group)
    shifts = [g[0] for g in group if g[0] is not None]
    operands = [x, *shifts, *pieces]
    shape = wa, sum(len(g[3]) for g in group), few, deep
    most = max(len(moves(g[3])) for g in group)

    def kernel(x_ref, *refs):
        shift_refs = list(refs[: len(shifts)])
        piece_refs = refs[len(shifts) : len(operands) - 1]
        grad_ref, moved_ref = refs[len(operands) - 1 :]
        done = 0
        for g, (shift, first, rate, taps) in enumerate(group):
            steps = moves(taps)
            s_ref = None if shift is None else shift_refs.pop(0)
            build_moved(piece_refs, moved_ref, s_ref, g, branches, valid, ha, prows, out)
            wide = len(steps) * out
            for b in sides_of(taps):
                low, high = span(b, rate, valid)
                left = moved_ref[low:high, :, :wide].reshape((high - low) * pheight, wide)
                right = x_ref[low + b * rate : high + b * rate].reshape((high - low) * pheight, deep)
                part = dot(left, right, TN).astype(BF16)
                for n, a in enumerate(steps):
                    t = done + taps.index((a, b))
                    for j in range(wa):
                        at = n * out + j * few
                        grad_ref[j, t] = part[at : at + few]
            done += len(taps)

    return pl.pallas_call(
        kernel,
        out_shape=jax.ShapeDtypeStruct(shape, BF16),
        grid=(1,),
        in_specs=loaded(operands),
        out_specs=pl.BlockSpec(shape, lambda i: (0, 0, 0, 0)),
        scratch_shapes=[pltpu.VMEM((valid, pheight, most * out), BF16)],
        compiler_params=WIDE,
        cost_estimate=NO_COST,
        name="weights_backward",
    )(*operands)


def features_backward(x, weights, group, pieces, start, h, place, fit, prows):
    valid, pheight, deep = x.shape
    out = weights.shape[1]
    ha, branches = pheight // prows, len(group)
    shifts = [g[0] for g in group if g[0] is not None]
    operands = [h.reshape(1), start, weights, place, *shifts, *pieces]
    high = place.shape[1]
    most = max(len(moves(g[3])) for g in group)
    most_sides = max(len(sides_of(g[3])) for g in group)

    def kernel(h_ref, start_ref, w_ref, place_ref, *refs):
        shift_refs = list(refs[: len(shifts)])
        piece_refs = refs[len(shifts) : len(operands) - 4]
        last_ref, moved_ref, wide_ref, total_ref, held_ref = refs[len(operands) - 4 :]
        for g, (shift, first, rate, taps) in enumerate(group):
            steps, sides = moves(taps), sides_of(taps)
            s_ref = None if shift is None else shift_refs.pop(0)
            build_moved(piece_refs, moved_ref, s_ref, g, branches, valid, ha, prows, out)
            for i, b in enumerate(sides):
                for n, a in enumerate(steps):
                    wide_ref[i, n * out : (n + 1) * out] = w_ref[first + taps.index((a, b))]
            wide = len(steps) * out
            for i, b in enumerate(sides):

                def columns(w, count):
                    values = moved_ref[pl.ds(w - b * rate, count), :, :wide].reshape(count * pheight, wide)
                    part = dot(values, wide_ref[i, :wide], NN).reshape(count, pheight, deep)
                    if g or b != 0:
                        total_ref[pl.ds(w, count)] += part
                    else:
                        total_ref[pl.ds(w, count)] = part + start_ref[...][None]

                in_steps(*span(-b, rate, valid), 4, columns)
        held_ref[valid * prows :] = jnp.zeros((high - valid * prows, deep), BF16)
        for k in range(ha):
            block = total_ref[:, k * prows : (k + 1) * prows, :].astype(BF16)
            held_ref[: valid * prows] = block.reshape(valid * prows, deep)
            last_ref[h_ref[0] ^ k] = dot(place_ref[...], held_ref[...], NN).astype(BF16)

    return pl.pallas_call(
        kernel,
        out_shape=jax.ShapeDtypeStruct((ha, fit, deep), BF16),
        grid=(1,),
        in_specs=[SCALAR] + loaded(operands[1:]),
        out_specs=pl.BlockSpec((ha, fit, deep), lambda i: (0, 0, 0)),
        scratch_shapes=[
            pltpu.VMEM((valid, pheight, most * out), BF16),
            pltpu.VMEM((most_sides, most * out, deep), BF16),
            pltpu.VMEM(x.shape, F32),
            pltpu.VMEM((high, deep), BF16),
        ],
        compiler_params=WIDE,
        cost_estimate=NO_COST,
        name="features_backward",
    )(*operands)


def real_rows(pixels, prows, rows):
    return (lax.broadcasted_iota(jnp.int32, (pixels, 1), 0) % prows < rows).astype(F32)


def total_of(refs):
    return tree_sum([r[...] for r in refs])


def column_sum(values):
    return jnp.sum(values, axis=0, keepdims=True)


def small_kernel(kernel, name, operands, shapes):
    return pl.pallas_call(
        kernel,
        out_shape=[jax.ShapeDtypeStruct(s, t) for s, t in shapes],
        in_specs=[WHOLE] * len(operands),
        out_specs=[WHOLE] * len(shapes),
        compiler_params=PARAMS,
        cost_estimate=NO_COST,
        name=name,
    )(*operands)


def branch_sums(parts, pool_part):
    _, pixels, out = parts[0].shape
    images = pool_part.shape[0]

    def kernel(low, low_got, low_last, high, high_got, high_last, pool_ref, branch_ref, sum_ref):
        for j in range(4):
            own, got, last = (low, low_got, low_last) if j < 2 else (high, high_got, high_last)
            value = own[j % 2] + got[0, j % 2].astype(F32) + last[j % 2].astype(F32)
            branch_ref[j] = value
            sum_ref[j : j + 1] = column_sum(value)
            sum_ref[4 + j : 5 + j] = column_sum(value * value)
        sum_ref[8:] = pool_ref[...]

    shapes = [((4, pixels, out), F32), ((8 + images, out), F32)]
    return small_kernel(kernel, "branch_sums", [*parts, pool_part], shapes)


def project(sums, branch, scales, shifts, counts, own, proj, rows, pixel_total):
    _, pixels, out = branch.shape
    images = counts.shape[0]
    prows = own.shape[0]
    many = len(sums)

    def kernel(*refs):
        branch_ref, scale_ref, shift_ref, count_ref, own_ref, proj_ref = refs[many : many + 6]
        joined_ref, projected_ref, second_ref, stat_ref, pool_ref = refs[many + 6 :]
        total = total_of(refs[:many])
        mean = total[0:4] / pixel_total
        rstd = lax.rsqrt(total[4:8] / pixel_total - mean * mean + EPS)
        stat_ref[0:4] = mean
        stat_ref[4:8] = rstd
        scale, shift = scale_ref[...], shift_ref[...]
        for j in range(4):
            norm = (branch_ref[j] - mean[j : j + 1]) * rstd[j : j + 1]
            hid = norm * scale[j : j + 1] + shift[j : j + 1]
            joined_ref[:, j * out : (j + 1) * out] = silu(hid).astype(BF16)
        pool_out = total[8:]
        weighted = count_ref[...]
        pool_mean = column_sum(weighted * pool_out) / pixel_total
        pool_second = column_sum(weighted * pool_out * pool_out) / pixel_total
        pool_rstd = lax.rsqrt(pool_second - pool_mean * pool_mean + EPS)
        pool_norm = (pool_out - pool_mean) * pool_rstd
        pool_hid = pool_norm * scale[4:5] + shift[4:5]
        pool_ref[0] = pool_norm
        pool_ref[1] = pool_hid
        pool_ref[2] = jnp.broadcast_to(pool_rstd, pool_out.shape)
        pool_act = silu(pool_hid)
        spread = jnp.zeros((prows, out), F32)
        for i in range(images):
            spread = spread + own_ref[:, i : i + 1] * pool_act[i : i + 1]
        spread = spread.astype(BF16)
        for w in range(pixels // prows):
            joined_ref[w * prows : (w + 1) * prows, 4 * out :] = spread
        projected = dot(joined_ref[...], proj_ref[...], NN)
        projected_ref[...] = projected
        held = projected * real_rows(pixels, prows, rows)
        second_ref[...] = jnp.zeros(second_ref.shape, F32)
        second_ref[0:1] = column_sum(held)
        second_ref[1:2] = column_sum(held * held)

    shapes = [((pixels, 5 * out), BF16), ((pixels, out), F32), ((8, out), F32), ((8, out), F32), ((3, images, out), F32)]
    return small_kernel(kernel, "project", [*sums, branch, scales, shifts, counts, own, proj], shapes)


def activate(sums, projected, cot, out_scale, out_shift, prows, rows, pixel_total):
    pixels, out = projected.shape
    many = len(sums)

    def kernel(*refs):
        projected_ref, cot_ref, scale_ref, shift_ref = refs[many : many + 4]
        act_ref, norm_ref, dhid_ref, third_ref, rstd_ref = refs[many + 4 :]
        total = total_of(refs[:many])
        mean = total[0:1] / pixel_total
        rstd = lax.rsqrt(total[1:2] / pixel_total - mean * mean + EPS)
        rstd_ref[...] = jnp.broadcast_to(rstd, rstd_ref.shape)
        norm = (projected_ref[...] - mean) * rstd
        norm_ref[...] = norm
        hid = norm * scale_ref[...] + shift_ref[...]
        act_ref[...] = silu(hid).astype(BF16)
        dhid = cot_ref[...].astype(F32) * real_rows(pixels, prows, rows) * silu_slope(hid)
        dhid_ref[...] = dhid
        third_ref[...] = jnp.zeros(third_ref.shape, F32)
        third_ref[0:1] = column_sum(dhid)
        third_ref[1:2] = column_sum(dhid * norm)

    shapes = [((pixels, out), BF16), ((pixels, out), F32), ((pixels, out), F32), ((8, out), F32), ((8, out), F32)]
    operands = [*sums, projected, cot, out_scale[None], out_shift[None]]
    return small_kernel(kernel, "activate", operands, shapes)


def unproject(sums, norm, dhid, rstd, out_scale, proj, joined, branch, stats, scales, shifts, own, ha, rows, pixel_total):
    _, pixels, out = branch.shape
    prows, images = own.shape
    many = len(sums)

    def kernel(*refs):
        norm_ref, dhid_ref, rstd_ref, oscale_ref, proj_ref, joined_ref = refs[many : many + 6]
        branch_ref, stat_ref, scale_ref, shift_ref, own_ref = refs[many + 6 : many + 11]
        third_ref, grad_ref, back_ref, fourth_ref = refs[many + 11 :]
        total = total_of(refs[:many])
        third_ref[...] = total
        mask = real_rows(pixels, prows, rows)
        dproj = dhid_ref[...] - (total[0:1] + norm_ref[...] * total[1:2]) / pixel_total
        dproj = (oscale_ref[...] * rstd_ref[0:1] * dproj * mask).astype(BF16)
        grad = dot(joined_ref[...], dproj, TN)
        grad_ref[...] = jnp.zeros(grad_ref.shape, BF16)
        few = 5 * out // ha
        for d in range(ha):
            grad_ref[d, :, :few] = grad[d * few : (d + 1) * few].T.astype(BF16)
        for j in range(5):
            dact = dot(dproj, proj_ref[j * out : (j + 1) * out], NT)
            if j < 4:
                branch_norm = (branch_ref[j] - stat_ref[j : j + 1]) * stat_ref[4 + j : 5 + j]
                hid = branch_norm * scale_ref[j : j + 1] + shift_ref[j : j + 1]
                back = dact * silu_slope(hid) * mask
                back_ref[j] = back
                fourth_ref[j : j + 1] = column_sum(back)
                fourth_ref[4 + j : 5 + j] = column_sum(back * branch_norm)
            else:
                across = jnp.sum(dact.reshape(pixels // prows, prows, out), axis=0)
                for i in range(images):
                    fourth_ref[8 + i : 9 + i] = column_sum(own_ref[:, i : i + 1] * across)

    shapes = [((8, out), F32), ((ha, out, out), BF16), ((4, pixels, out), F32), ((8 + images, out), F32)]
    operands = [*sums, norm, dhid, rstd, out_scale[None], proj, joined, branch, stats, scales, shifts, own]
    return small_kernel(kernel, "unproject", operands, shapes)


def branch_gradients(sums, back, branch, stats, scales, counts, pool, prows, rows, pixel_total):
    _, pixels, out = branch.shape
    images = counts.shape[0]
    many = len(sums)

    def kernel(*refs):
        back_ref, branch_ref, stat_ref, scale_ref, count_ref, pool_ref = refs[many : many + 6]
        grad_ref, dpool_ref, sum_ref = refs[many + 6 :]
        total = total_of(refs[:many])
        mask = real_rows(pixels, prows, rows)
        for j in range(4):
            rstd = stat_ref[4 + j : 5 + j]
            norm = (branch_ref[j] - stat_ref[j : j + 1]) * rstd
            value = back_ref[j] - (total[j : j + 1] + norm * total[4 + j : 5 + j]) / pixel_total
            grad_ref[j] = (scale_ref[j : j + 1] * rstd * value * mask).astype(BF16)
        dhid = silu_slope(pool_ref[1]) * total[8:]
        pool_shift = column_sum(dhid)
        pool_scale = column_sum(dhid * pool_ref[0])
        value = dhid - count_ref[...] * (pool_shift + pool_ref[0] * pool_scale) / pixel_total
        dpool_ref[...] = (scale_ref[4:5] * pool_ref[2] * value).astype(BF16)
        sum_ref[...] = jnp.zeros(sum_ref.shape, F32)
        sum_ref[0:4] = total[4:8]
        sum_ref[4:5] = pool_scale
        sum_ref[5:9] = total[0:4]
        sum_ref[9:10] = pool_shift

    shapes = [((4, pixels, out), BF16), ((images, out), BF16), ((16, out), F32)]
    operands = [*sums, back, branch, stats, scales, counts, pool]
    return small_kernel(kernel, "branch_gradients", operands, shapes)


def local(
    features,
    row_image,
    cotangent,
    w_one,
    dilated_weight,
    w_pool,
    w_proj,
    scales,
    shifts,
    out_scale,
    out_shift,
):
    micro, rows, cols, channels = features.shape
    ha, wa = lax.axis_size("ha"), lax.axis_size("wa")
    h, z = lax.axis_index("ha"), lax.axis_index("wa")
    planes = wa // micro
    batch, part = z // planes, z % planes
    deep = w_one.shape[0] // planes
    out = w_one.shape[1] * wa
    valid = cols * wa - PADC
    blocks = -(-valid // cols)
    prows = -(-rows // 16) * 16
    height, pheight = rows * ha, prows * ha
    images = IMG_DEV * ha
    pixels = float(height * valid)
    size = cols * rows

    fast = planes == 1 and wa == 4 and 6 * valid * pheight * out < (16 << 20) and channels % out == 0 and deep == out

    taps = [live_taps(r, valid) for r in RATES]
    few = w_proj.shape[0]
    side = jnp.pad(w_proj.T, ((0, 0), (0, w_one.shape[0] - few)))
    turned = dilated_weight.swapaxes(2, 3)
    if fast:
        weights = pack_weights(w_one.T, turned, w_pool.T, side, taps)
    else:
        picked = [turned[j, 3 * (a + 1) + b + 1] for j in range(3) for a, b in taps[j]]
        weights = gather_columns(jnp.stack([w_one.T, *picked, w_pool.T, side]))

    if fast:
        slots = extract(features.transpose(1, 2, 0, 3), cotangent.transpose(1, 2, 0, 3), z)
        tall, fit = slots[0].shape[0], ceil_to(valid * rows, 16)
        slots = [slots[0]] + [swap(slots[k], "wa", k, lambda i: i < blocks) for k in range(1, wa)]
        early = gather_early(weights, slots[1])
        high, thick = ceil_to(blocks * tall, 128), ceil_to(fit, 128)
        in_piece = block_rows(high, tall, rows, cols, valid, rows)
        in_chunk = block_rows(high, tall, rows, cols, valid, prows)
        spots = spots_of(np.arange(fit), in_piece)
        cot_spots = spots_of(np.arange(valid * prows), in_chunk)
        send, cot = choose(slots, z, blocks, spots, cot_spots, deep)
        raw = lax.all_to_all(send, "ha", 0, 0, tiled=True)
    else:
        f = features.transpose(0, 2, 1, 3).reshape(micro, size, ha, planes, deep)
        f = f.transpose(0, 3, 1, 2, 4).reshape(wa, size, ha * deep)
        c = cotangent.transpose(0, 2, 1, 3).reshape(micro, size, out)
        load = jnp.concatenate([f, jnp.repeat(c, planes, axis=0)], axis=-1)
        slots = [take(load, z)]
        for k in range(1, wa):
            slots.append(swap(take(load, z ^ k), "wa", k, lambda i: i < blocks))
        slots = jnp.stack(slots)
        block = jnp.concatenate([take(slots, z ^ j) for j in range(blocks)])[: valid * rows]
        raw = block[:, : ha * deep].reshape(valid * rows, ha, deep).swapaxes(0, 1)
        raw = lax.all_to_all(raw, "ha", 0, 0, tiled=True)
        cot = block[:, ha * deep :].reshape(valid, rows, out)
        cot = jnp.pad(cot, ((0, 0), (0, prows - rows), (0, 0))).reshape(valid * prows, out)
    if fast:
        weights = gather_late(weights, early, *slots)
    if fast:
        proj = order_chunks(*gather_chunks(weights[-1]), h, few)
    else:
        proj = in_order(*gather_chunks(weights[-1]))[..., :few].swapaxes(1, 2).reshape(ha * few, out)
    if planes > 1:
        weights = lax.dynamic_slice_in_dim(weights, part * deep, deep, 2)
    wide_pool = weights[-2]

    order = h ^ jnp.arange(ha, dtype=jnp.int32)
    labels = by_distance(take(row_image, batch).reshape(ha, rows))
    number = order[:, None] * rows + jnp.arange(rows, dtype=jnp.int32)[None, :]
    pad = ((0, 0), (0, prows - rows))
    labels = jnp.pad(labels, pad, constant_values=-1).reshape(pheight)
    number = jnp.pad(number, pad, constant_values=-(1 << 20)).reshape(pheight)
    same = (labels[:, None] == labels[None, :]) & (labels >= 0)[:, None]
    apart = number[None, :] - number[:, None]
    shift = [
        jnp.stack([(same & (apart == a * r)).astype(BF16) for a in (-1, 1)]) for r in RATES
    ]
    ids = jnp.arange(images, dtype=jnp.int32)
    member = (labels[:, None] == ids[None, :]).astype(F32)
    counts = jnp.sum(member, axis=0) * valid
    own = member[:prows]
    mask = jnp.tile(jnp.sum(own, axis=1), valid)[:, None]

    ahead = [1, 1 + len(taps[0]), 1 + len(taps[0]) + len(taps[1])]
    group = [(None, 0, 0, [(0, 0)])] + [(shift[j], ahead[j], RATES[j], taps[j]) for j in range(3)]
    if fast:
        place = spots_of(padded_rows(valid * prows, valid, prows, rows), np.arange(thick))
        x, row_sums = arrange(raw, place, h, valid, prows)
        unplace = spots_of(np.arange(fit), padded_rows(ceil_to(valid * prows, 128), valid, prows, rows))
    else:
        x = by_distance(raw).reshape(ha, valid, rows, deep)
        x = jnp.pad(x, ((0, 0), (0, 0), (0, prows - rows), (0, 0)))
        x = x.swapaxes(0, 1).reshape(valid, pheight, deep)
        row_sums = jnp.sum(x.astype(F32), axis=0)
    if fast:
        branch_parts = reduce_square(*forward_kernel(x, weights, group, prows))
    else:
        sums = jnp.stack([forward_plain(x, s, weights[n : n + len(t)], r, t) for s, n, r, t in group])
        sums = sums.astype(BF16).reshape(len(group), valid, ha // 2, 2, prows, out)
        sums = sums.transpose(3, 2, 0, 1, 4, 5).reshape(2, ha // 2, len(group), valid * prows, out)
        branch = sum_chunks(spread_chunks(sums[0], sums[1]), planes)
    pooled = (jnp.dot(member.T, row_sums, precision=HIGHEST) / counts[:, None]).astype(BF16)
    pool_part = dot(pooled, wide_pool, NT)

    weighted = counts[:, None]
    once = (part == 0).astype(F32)
    if fast:
        branch, first = branch_sums(branch_parts, pool_part)
        joined, projected, second, stats, pool = project(
            plane_parts(first), branch, scales, shifts, weighted, own, proj, rows, pixels
        )
        activation, proj_norm, dproj_hid, third, proj_rstd = activate(
            plane_parts(second), projected, cot, out_scale, out_shift, prows, rows, pixels
        )
        third, grad_proj, dhid, fourth = unproject(
            plane_parts(third),
            proj_norm,
            dproj_hid,
            proj_rstd,
            out_scale,
            proj,
            joined,
            branch,
            stats,
            scales,
            shifts,
            own,
            ha,
            rows,
            pixels,
        )
        dbranch, dpool, sums = branch_gradients(
            plane_parts(fourth), dhid, branch, stats, scales, weighted, pool, prows, rows, pixels
        )
        sums = jnp.concatenate([sums[:10], third[:2]])
    else:
        first = plane_sum(
            jnp.concatenate(
                [once * jnp.sum(branch, axis=1), once * jnp.sum(branch * branch, axis=1), pool_part]
            ),
            planes,
        )
        mean = first[0:4] / pixels
        rstd = lax.rsqrt(first[4:8] / pixels - mean * mean + EPS)
        pool_out = first[8:]
        norm = (branch - mean[:, None]) * rstd[:, None]
        hid = norm * scales[:4, None] + shifts[:4, None]
        act = silu(hid)
        weighted = counts[:, None]
        pool_mean = jnp.sum(weighted * pool_out, axis=0) / pixels
        pool_second = jnp.sum(weighted * pool_out * pool_out, axis=0) / pixels
        pool_rstd = lax.rsqrt(pool_second - pool_mean * pool_mean + EPS)
        pool_norm = (pool_out - pool_mean) * pool_rstd
        pool_hid = pool_norm * scales[4] + shifts[4]
        spread = jnp.dot(own, silu(pool_hid), precision=HIGHEST)
        spread = jnp.broadcast_to(spread[None], (valid, prows, out)).reshape(valid * prows, out)
        joined = jnp.concatenate([act[0], act[1], act[2], act[3], spread], axis=-1).astype(BF16)
        projected = jnp.dot(joined, proj, preferred_element_type=F32)

        held = projected * mask
        second = plane_sum(
            jnp.stack([jnp.sum(held, axis=0), jnp.sum(held * held, axis=0)]) * once, planes
        )
        proj_mean = second[0] / pixels
        proj_rstd = lax.rsqrt(second[1] / pixels - proj_mean * proj_mean + EPS)
        proj_norm = (projected - proj_mean) * proj_rstd
        proj_hid = proj_norm * out_scale + out_shift
        activation = silu(proj_hid).astype(BF16)
        dproj_hid = cot.astype(F32) * mask * silu_slope(proj_hid)
        third = plane_sum(
            jnp.stack([jnp.sum(dproj_hid, axis=0), jnp.sum(dproj_hid * proj_norm, axis=0)]) * once, planes
        )
        dproj = (
            out_scale * proj_rstd * (dproj_hid - (third[0] + proj_norm * third[1]) / pixels) * mask
        ).astype(BF16)
        djoined = lax.dot_general(dproj, proj, (((1,), (1,)), ((), ())), preferred_element_type=F32)
        grad_proj = dot(dproj, joined, TN)
        dact = jnp.stack([djoined[:, j * out : (j + 1) * out] for j in range(4)])
        dspread = jnp.sum(djoined[:, 4 * out :].reshape(valid, prows, out), axis=0)
        image_part = jnp.dot(own.T, dspread, precision=HIGHEST)
        dhid = dact * silu_slope(hid) * mask
        fourth = plane_sum(
            jnp.concatenate([jnp.sum(dhid, axis=1), jnp.sum(dhid * norm, axis=1), image_part]) * once,
            planes,
        )
        branch_shift, branch_scale, image_total = fourth[0:4], fourth[4:8], fourth[8:]
        dbranch = (
            (scales[:4] * rstd)[:, None]
            * (dhid - (branch_shift[:, None] + norm * branch_scale[:, None]) / pixels)
            * mask
        ).astype(BF16)
        dpool_hid = silu_slope(pool_hid) * image_total
        pool_shift = jnp.sum(dpool_hid, axis=0)
        pool_scale = jnp.sum(dpool_hid * pool_norm, axis=0)
        dpool = (
            scales[4] * pool_rstd * (dpool_hid - weighted * (pool_shift + pool_norm * pool_scale) / pixels)
        ).astype(BF16)
        sums = jnp.concatenate([branch_scale, pool_scale[None], branch_shift, pool_shift[None], third])
    grad_pool = dot(dpool, pooled, TN)
    dpooled = dot(dpool, wide_pool, NN)

    total = jnp.dot(member, dpooled / counts[:, None], precision=HIGHEST)
    if fast:
        pieces = gather_square(dbranch)
        tap_grads = weights_backward(x, group, pieces, wa, prows)
        back = features_backward(x, weights, group, pieces, total, h, unplace, fit, prows)
    else:
        total = jnp.broadcast_to(total[None], (valid,) + total.shape)
        near, far = gather_chunks(dbranch)
        every = jnp.stack([near, far], axis=1).reshape(ha, len(group), valid, prows, out)
        every = every.transpose(1, 2, 0, 3, 4).reshape(len(group), valid, pheight, out)
        found = []
        for (s, n, r, t), d in zip(group, every):
            grads, total = backward_plain(x, s, weights[n : n + len(t)], r, t, d, total)
            found.append(grads.reshape(len(t), wa, out // wa, deep).swapaxes(0, 1).astype(BF16))
        tap_grads = jnp.concatenate(found, axis=1)
        back = total.astype(BF16).reshape(valid, ha, prows, deep)[:, :, :rows]
        back = back.swapaxes(0, 1).reshape(ha, valid * rows, deep)
        back = by_distance(back)

    def in_place(grads):
        if planes == 1:
            return grads
        full = jnp.zeros(grads.shape[:-1] + (deep * planes,), grads.dtype)
        return lax.dynamic_update_slice_in_dim(full, grads, part * deep, grads.ndim - 1)

    if not fast:
        grad_proj = (grad_proj * once).reshape(out, ha, few).swapaxes(0, 1)
        grad_proj = jnp.pad(grad_proj, ((0, 0), (0, 0), (0, w_one.shape[0] - few))).astype(BF16)
    proj_chunk = lax.psum_scatter(grad_proj, "ha", scatter_dimension=0, tiled=False)
    grad_pool = in_place(grad_pool.astype(BF16)).reshape(wa, 1, out // wa, -1)
    proj_chunk = proj_chunk.reshape(wa, 1, out // wa, -1)
    tap_grads = line_scatter(in_place(tap_grads))
    rest = jnp.concatenate([grad_pool, proj_chunk], axis=1)
    if not fast:
        rest = line_scatter(rest)
    tap_out = [tap_grads[n : n + len(t)] for n, t in zip(ahead, taps)]
    blank = jnp.zeros((out // wa, w_one.shape[0]), F32)
    atrous = []
    for j in range(3):
        if len(taps[j]) == 9:
            atrous.append(tap_out[j])
        else:
            found = {3 * (a + 1) + b + 1: tap_out[j][t] for t, (a, b) in enumerate(taps[j])}
            atrous.append(jnp.stack([found.get(t, blank) for t in range(9)]))
    atrous = jnp.stack(atrous)
    atrous_out = atrous.swapaxes(2, 3)
    back = lax.all_to_all(back, "ha", 0, 0, tiled=True)

    def home(i, k):
        return i ^ k < blocks

    if fast:
        piece_spots = spots_of(block_rows(wa * tall, tall, rows, cols, valid, rows), np.arange(thick))
        chunk_spots = spots_of(block_rows(wa * tall, tall, rows, cols, valid, prows), np.arange(valid * prows))
        got = unchoose(
            back, activation, z, blocks, piece_spots.reshape(wa, tall, thick), chunk_spots.reshape(wa, tall, -1)
        )
        got = [got[0]] + [swap(got[k], "wa", k, partial(home, k=k)) for k in range(1, wa)]
        df, acts = interleave(got, z, blocks, rows, cols, out, [atrous])
        wide = jnp.broadcast_to(jnp.pad(sums, ((0, 4), (0, 0)))[None], (wa, 16, out))
        rest = jnp.concatenate([rest.astype(F32).reshape(wa, -1, out), wide], axis=1)
        rest = exchange_sum(after(rest, got[0]))
        sums = rest[-16:-4]
        rest = rest[:-16].reshape(2, -1, out)
    else:

        def send_home(array):
            array = jnp.pad(array, ((0, wa * size - valid * rows), (0, 0))).reshape(wa, size, -1)
            got = [take(array, z)]
            got += [swap(take(array, z ^ k), "wa", k, partial(home, k=k)) for k in range(1, wa)]
            got = jnp.stack(got)
            got = jnp.where(z < blocks, got, jnp.zeros((), got.dtype))
            return jnp.stack([take(got, z ^ t) for t in range(wa)])

        back = back.swapaxes(0, 1).reshape(valid * rows, ha * deep)
        df = send_home(back).reshape(micro, planes, cols, rows, ha, deep)
        df = df.transpose(0, 3, 2, 4, 1, 5).reshape(features.shape)
        activation = activation.reshape(valid, prows, out)[:, :rows].reshape(valid * rows, out)
        acts = send_home(activation).reshape(micro, planes, cols, rows, out)[:, 0].swapaxes(1, 2)
    if not fast:
        sums = sums * once
        sums = tree_sum([sums] + [swap(sums, "wa", k) for k in range(1, wa)])
    one_out, pool_grad_out, proj_out = tap_grads[0].T, rest[0].T, rest[1][:, :few].T
    return (
        acts,
        df,
        one_out,
        atrous_out,
        pool_grad_out,
        proj_out,
        sums[0:5],
        sums[5:10],
        sums[11],
        sums[10],
    )


def solution(mesh):
    specs = (
        P(None, "ha", "wa", None),
        P(),
        P(None, "ha", "wa", None),
        P("ha", "wa"),
        P(None, None, "ha", "wa"),
        P("ha", "wa"),
        P("ha", "wa"),
        P(),
        P(),
        P(),
        P(),
    )
    out_specs = (
        P(None, "ha", "wa", None),
        P(None, "ha", "wa", None),
        P("ha", "wa"),
        P(None, None, "ha", "wa"),
        P("ha", "wa"),
        P("ha", "wa"),
        P(),
        P(),
        P(),
        P(),
    )
    return jax.shard_map(local, mesh=mesh, in_specs=specs, out_specs=out_specs, check_vma=False)
```

```python
from functools import partial

import jax
import jax.numpy as jnp
import numpy as np
from jax import lax
from jax.experimental import pallas as pl
from jax.experimental.pallas import tpu as pltpu
from jax.sharding import PartitionSpec as P

PADC = 7
IMG_DEV = 2
RATES = (6, 12, 18)
EPS = 1e-05
HIGHEST = lax.Precision.HIGHEST
F32 = jnp.float32
BF16 = jnp.bfloat16


def silu(u):
    return u * jax.nn.sigmoid(u)


def silu_slope(u):
    s = jax.nn.sigmoid(u)
    return s * (1.0 + u * (1.0 - s))


def swap(array, axis, bits, sources=None):
    count = lax.axis_size(axis)
    pairs = [(i, i ^ bits) for i in range(count) if sources is None or sources(i)]
    return lax.ppermute(array, axis, pairs)


def after(value, *others):
    return lax.optimization_barrier((value, *others))[0]


def tree_sum(parts):
    while len(parts) > 1:
        parts = [parts[i] + parts[i + 1] for i in range(0, len(parts), 2)]
    return parts[0]


def plane_parts(array):
    pair = array + swap(array, "ha", 1)
    return [pair] + [swap(pair, "ha", k) for k in range(2, lax.axis_size("ha"), 2)]


def plane_sum(array, groups):
    total = tree_sum(plane_parts(array))
    bits = 1
    while bits < groups:
        total = total + swap(total, "wa", bits)
        bits *= 2
    return total


def take(array, index):
    return lax.dynamic_index_in_dim(array, index, 0, keepdims=False)


def by_distance(array):
    h = lax.axis_index("ha")
    return jnp.stack([take(array, h ^ k) for k in range(array.shape[0])])


def spread_chunks(even, odd):
    other = swap(odd, "ha", 1)
    both = [even[q].astype(F32) + other[q].astype(F32) for q in range(even.shape[0])]
    return both[:1] + [swap(both[q].astype(BF16), "ha", 2 * q) for q in range(1, len(both))]


def sum_chunks(parts, groups):
    total = tree_sum([part.astype(F32) for part in parts])
    bits = 1
    while bits < groups:
        total = total + swap(total.astype(BF16), "wa", bits).astype(F32)
        bits *= 2
    return total


def reduce_square(even, odd):
    other = swap(odd, "ha", 1)
    half = even.shape[1] // 2
    low = even[:, :half].astype(F32) + other[:, :half].astype(F32)
    high = even[:, half:].astype(F32) + other[:, half:].astype(F32)
    low_got = swap(low[1::2].astype(BF16), "ha", 2)
    high_got = swap(high[2:].astype(BF16), "ha", 4)
    low_last = swap((low[2] + low_got[1].astype(F32)).astype(BF16), "ha", 4)
    high_last = swap((high[1] + high_got[1].astype(F32)).astype(BF16), "ha", 2)
    return low[0], low_got, low_last, high[0], high_got, high_last


def gather_square(chunk):
    half = chunk.shape[0] // 2
    low, high = chunk[:half], chunk[half:]
    low_one = swap(low, "ha", 2)
    high_one = swap(high, "ha", 4)
    low_two = swap(jnp.stack([low, low_one]), "ha", 4)
    high_two = swap(jnp.stack([high, high_one]), "ha", 2)
    near = [chunk, low_one, high_one, low_two, high_two]
    return near + [swap(piece, "ha", 1) for piece in near]


def piece_of(k, branch, branches):
    q, half = k // 2, branches // 2
    first = 5 * (k % 2)
    low = branch < half
    inner = branch if low else branch - half
    if q == 0:
        return first, (branch,)
    if q == (1 if low else 2):
        return first + (1 if low else 2), (inner,)
    return first + (3 if low else 4), (int(q == 3), inner)


def gather_near(chunk):
    return [chunk] + [swap(chunk, "ha", 2 * q) for q in range(1, lax.axis_size("ha") // 2)]


def gather_chunks(chunk):
    near = jnp.stack(gather_near(chunk))
    return near, swap(near, "ha", 1)


def in_order(near, far):
    every = jnp.stack([near, far], axis=1)
    return by_distance(every.reshape((2 * near.shape[0],) + near.shape[1:]))


def gather_columns(own):
    gathered = lax.all_gather(own, "wa", axis=0, tiled=False)
    planes, count, few, rows = gathered.shape
    return gathered.swapaxes(0, 1).reshape(count, planes * few, rows)


def neighbour(array, pairs):
    return lax.ppermute(array, "wa", pairs)


def gather_early(own, others):
    right = neighbour(own, [(0, 1), (1, 2), (2, 3)])
    left = neighbour(own, [(1, 0), (2, 1), (3, 2)])
    right_two = neighbour(after(right, others), [(2, 3)])
    left_two = neighbour(after(left, others), [(1, 0), (2, 1)])
    return right, left, right_two, left_two


def gather_late(own, early, *others):
    z = lax.axis_index("wa")
    right, left, right_two, left_two = early
    left_three = neighbour(left_two, [(1, 0)])
    last_two = neighbour(after(right, *others), [(1, 2)])
    last_three = neighbour(last_two, [(2, 3)])
    found = [
        lax.select_n(z, own, right, last_two, last_three),
        lax.select_n(z, left, own, right, right_two),
        lax.select_n(z, left_two, left, own, right),
        lax.select_n(z, left_three, left_two, left, own),
    ]
    return jnp.concatenate(found, axis=1)


def exchange_sum(parts):
    z = lax.axis_index("wa")
    got = [swap(take(parts, z ^ k), "wa", k) for k in range(1, lax.axis_size("wa"))]
    return tree_sum([take(parts, z)] + got)


def line_scatter(parts):
    return lax.psum_scatter(parts, "wa", scatter_dimension=0, tiled=False).astype(F32)


def live_taps(rate, valid):
    return [(a, b) for a in (-1, 0, 1) for b in (-1, 0, 1) if b == 0 or valid > rate]


def span(b, rate, valid):
    return max(0, -b * rate), min(valid, valid - b * rate)


def moves(taps):
    return sorted({a for a, b in taps})


def forward_plain(x, shift, weights, rate, taps):
    valid = x.shape[0]
    moved = {
        a: x if a == 0 else jnp.einsum("pq,wqk->wpk", shift[(a + 1) // 2], x) for a in moves(taps)
    }
    out = jnp.zeros(x.shape[:2] + (weights.shape[1],), F32)
    for t, (a, b) in enumerate(taps):
        low, high = span(b, rate, valid)
        part = jnp.einsum(
            "wpk,ek->wpe", moved[a][low + b * rate : high + b * rate], weights[t], preferred_element_type=F32
        )
        out = out.at[low:high].add(part)
    return out


def backward_plain(x, shift, weights, rate, taps, grad, total):
    valid = x.shape[0]
    moved = {
        a: grad if a == 0 else jnp.einsum("pq,wqe->wpe", shift[(1 - a) // 2], grad)
        for a in moves(taps)
    }
    weight_grads = []
    for t, (a, b) in enumerate(taps):
        low, high = span(b, rate, valid)
        d = moved[a][low:high]
        source = slice(low + b * rate, high + b * rate)
        weight_grads.append(jnp.einsum("wpe,wpk->ek", d, x[source], preferred_element_type=F32))
        total = total.at[source].add(
            jnp.einsum("wpe,ek->wpk", d, weights[t], preferred_element_type=F32)
        )
    return jnp.stack(weight_grads), total


def dot(left, right, dims):
    return lax.dot_general(left, right, ((dims[0], dims[1]), ((), ())), preferred_element_type=F32)


NN = ((1,), (0,))
NT = ((1,), (1,))
TN = ((0,), (0,))
WHOLE = pl.BlockSpec(memory_space=pltpu.VMEM)
SCALAR = pl.BlockSpec(memory_space=pltpu.SMEM)
NO_COST = pl.CostEstimate(flops=0, bytes_accessed=0, transcendentals=0)
WIDE = pltpu.CompilerParams(vmem_limit_bytes=60 * 1024 * 1024)
PARAMS = pltpu.CompilerParams(vmem_limit_bytes=32 * 1024 * 1024)


def ceil_to(n, step):
    return -(-n // step) * step


def pack_weights(w_one, dilated, w_pool, w_proj, taps):
    rows, deep = w_one.shape
    order = [(j, 3 * (a + 1) + b + 1) for j in range(3) for a, b in taps[j]]

    def kernel(one_ref, dilated_ref, pool_ref, proj_ref, out_ref):
        out_ref[0] = one_ref[...]
        for at, (j, t) in enumerate(order):
            out_ref[at + 1] = dilated_ref[j, t]
        out_ref[len(order) + 1] = pool_ref[...]
        out_ref[len(order) + 2] = proj_ref[...]

    return pl.pallas_call(
        kernel,
        out_shape=jax.ShapeDtypeStruct((len(order) + 3, rows, deep), BF16),
        in_specs=[WHOLE] * 4,
        out_specs=WHOLE,
        compiler_params=PARAMS,
        name="pack_weights",
    )(w_one, dilated, w_pool, w_proj)


def spots_of(wanted, held):
    return ((wanted[:, None] == held[None, :]) & (wanted >= 0)[:, None]).astype(BF16)


def block_rows(count, tall, rows, cols, valid, pitch):
    row = np.arange(count)
    column = row // tall * cols + row % tall % cols
    real = (row % tall < rows * cols) & (column < valid)
    return np.where(real, column * pitch + row % tall // cols, -1)


def padded_rows(count, valid, prows, rows):
    row = np.arange(count)
    real = (row < valid * prows) & (row % prows < rows)
    return np.where(real, row // prows * rows + row % prows, -1)


def extract(features, cotangent, z):
    rows, cols, micro, channels = features.shape
    out = cotangent.shape[-1]
    size = rows * cols
    steps = channels // out

    def kernel(z_ref, f_ref, c_ref, *refs):
        outs, held_ref = refs[:-1], refs[-1]

        def put(ref):
            values = ref[...]
            for m in range(micro):
                held_ref[m] = values[:, m, :].astype(F32)
            for k in range(micro):
                outs[k][...] = held_ref[z_ref[0] ^ k].astype(BF16)

        @pl.when(pl.program_id(0) < steps)
        def _():
            put(f_ref)

        @pl.when(pl.program_id(0) == steps)
        def _():
            put(c_ref)

    return pl.pallas_call(
        kernel,
        grid=(steps + 1,),
        out_shape=[jax.ShapeDtypeStruct((size, channels + out), BF16)] * micro,
        in_specs=[
            SCALAR,
            pl.BlockSpec((size, micro, out), lambda i: (0, 0, jnp.minimum(i, steps - 1))),
            pl.BlockSpec((size, micro, out), lambda i: (0, 0, 0)),
        ],
        out_specs=[pl.BlockSpec((size, out), lambda i: (0, i))] * micro,
        scratch_shapes=[pltpu.VMEM((micro, size, out), F32)],
        compiler_params=PARAMS,
        name="extract",
    )(z.reshape(1), features.reshape(size, micro, channels), cotangent.reshape(size, micro, out))


def choose(slots, z, blocks, spots, last_spots, lanes):
    size, wide = slots[0].shape
    tall = ceil_to(size, 16)
    high = spots.shape[1]
    count = wide // lanes - 1

    def kernel(z_ref, *refs):
        spots_ref, last_ref, send_ref, own_ref, held_ref = refs[len(slots) :]
        held_ref[...] = jnp.zeros((high, wide), BF16)
        for v in range(len(slots)):

            @pl.when(z_ref[0] == v)
            def _():
                for j in range(blocks):
                    held_ref[j * tall : j * tall + size] = refs[v ^ j][...]

        for d in range(count):
            part = held_ref[:, d * lanes : (d + 1) * lanes]
            send_ref[d] = dot(spots_ref[...], part, NN).astype(BF16)
        own_ref[...] = dot(last_ref[...], held_ref[:, count * lanes :], NN).astype(BF16)

    return pl.pallas_call(
        kernel,
        out_shape=[
            jax.ShapeDtypeStruct((count, spots.shape[0], lanes), BF16),
            jax.ShapeDtypeStruct((last_spots.shape[0], lanes), BF16),
        ],
        in_specs=[SCALAR] + [WHOLE] * (len(slots) + 2),
        out_specs=[WHOLE] * 2,
        scratch_shapes=[pltpu.VMEM((high, wide), BF16)],
        compiler_params=PARAMS,
        name="choose",
    )(z.reshape(1), *slots, spots, last_spots)


def unchoose(pieces, last, z, blocks, size, spots, last_spots):
    ha, fit, out = pieces.shape
    planes, tall, thick = spots.shape
    wide = (ha + 1) * out

    def kernel(z_ref, pieces_ref, last_ref, spots_ref, last_spots_ref, *refs):
        outs, held_ref = refs[:-1], refs[-1]
        held_ref[fit:] = jnp.zeros((thick - fit, ha * out), BF16)
        for d in range(ha):
            held_ref[:fit, d * out : (d + 1) * out] = pieces_ref[d]
        for v in range(planes):

            @pl.when(z_ref[0] == v)
            def _():
                for j in range(planes):
                    if j < blocks:
                        block = dot(spots_ref[j], held_ref[...], NN).astype(BF16)
                        outs[v ^ j][:, : ha * out] = block[:size]
                        block = dot(last_spots_ref[j], last_ref[...], NN).astype(BF16)
                        outs[v ^ j][:, ha * out :] = block[:size]
                    else:
                        outs[v ^ j][...] = jnp.zeros((size, wide), BF16)

    return pl.pallas_call(
        kernel,
        out_shape=[jax.ShapeDtypeStruct((size, wide), BF16)] * planes,
        in_specs=[SCALAR] + [WHOLE] * 4,
        out_specs=[WHOLE] * planes,
        scratch_shapes=[pltpu.VMEM((thick, ha * out), BF16)],
        compiler_params=PARAMS,
        name="unchoose",
    )(z.reshape(1), pieces, last, spots, last_spots)


def order_chunks(near, far, h, few):
    half, out, _ = near.shape

    def kernel(h_ref, near_ref, far_ref, out_ref):
        for k in range(2 * half):
            chunk = (far_ref if k % 2 else near_ref)[k // 2]
            at = pl.multiple_of((h_ref[0] ^ k) * few, 16)
            out_ref[pl.ds(at, few), :] = chunk.T[:few]

    return pl.pallas_call(
        kernel,
        out_shape=jax.ShapeDtypeStruct((2 * half * few, out), BF16),
        in_specs=[SCALAR, WHOLE, WHOLE],
        out_specs=WHOLE,
        compiler_params=PARAMS,
        cost_estimate=NO_COST,
        name="order_chunks",
    )(h.reshape(1), near, far)


def interleave(got, z, blocks, rows, cols, out, others):
    micro = len(got)
    size, channels = got[0].shape
    channels -= out
    lanes = 2 * out

    def kernel(z_ref, *refs):
        df_ref, act_ref, held_ref = refs[-3:]

        def place(parts, wide):
            for k in range(micro):
                part = jnp.where(z_ref[0] < blocks, parts[k][...], jnp.zeros((), BF16))
                held_ref[z_ref[0] ^ k, :, :wide] = part
            return jnp.stack([held_ref[m, :, :wide] for m in range(micro)], axis=1)

        @pl.when(pl.program_id(0) == 0)
        def _():
            act_ref[...] = place(refs[micro : 2 * micro], out)

        df_ref[...] = place(refs[:micro], lanes)

    df, act = pl.pallas_call(
        kernel,
        grid=(channels // lanes,),
        out_shape=[jax.ShapeDtypeStruct((size, micro, n), BF16) for n in (channels, out)],
        in_specs=[SCALAR]
        + [pl.BlockSpec((size, lanes), lambda i: (0, i))] * micro
        + [pl.BlockSpec((size, out), lambda i: (0, channels // out))] * micro
        + [pl.BlockSpec(memory_space=pl.ANY)] * len(others),
        out_specs=[
            pl.BlockSpec((size, micro, lanes), lambda i: (0, 0, i)),
            pl.BlockSpec((size, micro, out), lambda i: (0, 0, 0)),
        ],
        scratch_shapes=[pltpu.VMEM((micro, size, lanes), BF16)],
        compiler_params=PARAMS,
        name="interleave",
    )(z.reshape(1), *got, *got, *others)
    return [a.reshape(rows, cols, micro, -1).transpose(2, 0, 1, 3) for a in (df, act)]


def arrange(raw, place, h, valid, prows):
    ha, tall, deep = raw.shape
    high = place.shape[1]

    def kernel(h_ref, raw_ref, place_ref, x_ref, sum_ref, held_ref):
        held_ref[tall:] = jnp.zeros((high - tall, deep), BF16)
        for k in range(ha):
            held_ref[:tall] = raw_ref[h_ref[0] ^ k]
            block = dot(place_ref[...], held_ref[...], NN).reshape(valid, prows, deep)
            x_ref[:, k * prows : (k + 1) * prows, :] = block.astype(BF16)
            sum_ref[k * prows : (k + 1) * prows] = jnp.sum(block, axis=0)

    return pl.pallas_call(
        kernel,
        out_shape=[
            jax.ShapeDtypeStruct((valid, ha * prows, deep), BF16),
            jax.ShapeDtypeStruct((ha * prows, deep), F32),
        ],
        in_specs=[SCALAR, WHOLE, WHOLE],
        out_specs=[WHOLE, WHOLE],
        scratch_shapes=[pltpu.VMEM((high, deep), BF16)],
        compiler_params=PARAMS,
        name="arrange",
    )(h.reshape(1), raw, place)


def sides_of(taps):
    return sorted({b for a, b in taps}, key=abs)


def in_steps(low, high, step, body):
    whole = (high - low) // step
    if whole:

        def one(i, carry):
            body(low + i * step, step)
            return carry

        lax.fori_loop(0, whole, one, 0)
    if (high - low) % step:
        body(low + whole * step, (high - low) % step)


def forward_kernel(x, weights, group, prows):
    valid, pheight, deep = x.shape
    out = weights.shape[1]
    half = pheight // prows // 2
    operands, flops = [x, weights], 0
    for shift, first, rate, taps in group:
        operands += [] if shift is None else [shift]
        spans = [span(b, rate, valid) for a, b in taps]
        flops += 2 * pheight * deep * out * sum(high - low for low, high in spans)
    most = max(len(moves(g[3])) for g in group)
    most_sides = max(len(sides_of(g[3])) for g in group)

    def kernel(x_ref, w_ref, *refs):
        ins = list(refs[: len(operands) - 2])
        even_ref, odd_ref, moved_ref, wide_ref, sum_ref = refs[len(operands) - 2 :]
        for g, (shift, first, rate, taps) in enumerate(group):
            steps, sides = moves(taps), sides_of(taps)
            for i, b in enumerate(sides):
                for n, a in enumerate(steps):
                    wide_ref[i, :, n * deep : (n + 1) * deep] = w_ref[first + taps.index((a, b))]
            source_ref = x_ref
            if shift is not None:
                s_ref = ins.pop(0)
                source_ref = moved_ref

                def move(w, carry):
                    values = x_ref[w]
                    both = dot(s_ref[...].reshape(2 * pheight, pheight), values, NN).astype(BF16)
                    moved_ref[w, :, :deep] = both[:pheight]
                    moved_ref[w, :, deep : 2 * deep] = values
                    moved_ref[w, :, 2 * deep :] = both[pheight:]
                    return carry

                lax.fori_loop(0, valid, move, 0, unroll=True)

            for i, b in enumerate(sides):

                def columns(w, count):
                    values = source_ref[pl.ds(w + b * rate, count)].reshape(count * pheight, -1)
                    part = dot(values, wide_ref[i, :, : len(steps) * deep], NT)
                    part = part.reshape(count, pheight, out)
                    if b == 0:
                        sum_ref[pl.ds(w, count)] = part
                    else:
                        sum_ref[pl.ds(w, count)] += part

                in_steps(*span(b, rate, valid), 7, columns)

            def store(w, carry):
                at = pl.multiple_of(w * prows, prows)
                for k in range(2 * half):
                    to = odd_ref if k % 2 else even_ref
                    to[k // 2, g, pl.ds(at, prows), :] = sum_ref[w, k * prows : (k + 1) * prows].astype(BF16)
                return carry

            lax.fori_loop(0, valid, store, 0, unroll=True)

    shape = jax.ShapeDtypeStruct((half, len(group), valid * prows, out), BF16)
    return pl.pallas_call(
        kernel,
        out_shape=[shape] * 2,
        in_specs=[WHOLE] * len(operands),
        out_specs=[WHOLE] * 2,
        scratch_shapes=[
            pltpu.VMEM((valid, pheight, most * deep), BF16),
            pltpu.VMEM((most_sides, out, most * deep), BF16),
            pltpu.VMEM((valid, pheight, out), F32),
        ],
        compiler_params=PARAMS,
        cost_estimate=NO_COST,
        name="forward",
    )(*operands)


def loaded(operands):
    return [
        pl.BlockSpec(a.shape, lambda i, n=a.ndim: (0,) * n, pipeline_mode=pl.Buffered(1)) for a in operands
    ]


def build_moved(pieces, moved_ref, s_ref, g, branches, valid, ha, prows, out):
    middle = 0 if s_ref is None else out

    def move(w, carry):
        at = pl.multiple_of(w * prows, prows)
        for k in range(ha):
            piece, index = piece_of(k, g, branches)
            rows = slice(k * prows, (k + 1) * prows)
            moved_ref[w, rows, middle : middle + out] = pieces[piece][(*index, pl.ds(at, prows))]
        if s_ref is not None:
            held = moved_ref[w, :, out : 2 * out]
            both = dot(s_ref[...].reshape(2 * ha * prows, ha * prows), held, NN).astype(BF16)
            moved_ref[w, :, :out] = both[ha * prows :]
            moved_ref[w, :, 2 * out :] = both[: ha * prows]
        return carry

    lax.fori_loop(0, valid, move, 0, unroll=True)


def weights_backward(x, group, pieces, wa, prows):
    valid, pheight, deep = x.shape
    out = pieces[0].shape[-1]
    few, ha, branches = out // wa, pheight // prows, len(group)
    shifts = [g[0] for g in group if g[0] is not None]
    operands = [x, *shifts, *pieces]
    shape = wa, sum(len(g[3]) for g in group), few, deep
    most = max(len(moves(g[3])) for g in group)

    def kernel(x_ref, *refs):
        shift_refs = list(refs[: len(shifts)])
        piece_refs = refs[len(shifts) : len(operands) - 1]
        grad_ref, moved_ref = refs[len(operands) - 1 :]
        done = 0
        for g, (shift, first, rate, taps) in enumerate(group):
            steps = moves(taps)
            s_ref = None if shift is None else shift_refs.pop(0)
            build_moved(piece_refs, moved_ref, s_ref, g, branches, valid, ha, prows, out)
            wide = len(steps) * out
            for b in sides_of(taps):
                low, high = span(b, rate, valid)
                left = moved_ref[low:high, :, :wide].reshape((high - low) * pheight, wide)
                right = x_ref[low + b * rate : high + b * rate].reshape((high - low) * pheight, deep)
                part = dot(left, right, TN).astype(BF16)
                for n, a in enumerate(steps):
                    t = done + taps.index((a, b))
                    for j in range(wa):
                        at = n * out + j * few
                        grad_ref[j, t] = part[at : at + few]
            done += len(taps)

    return pl.pallas_call(
        kernel,
        out_shape=jax.ShapeDtypeStruct(shape, BF16),
        grid=(1,),
        in_specs=loaded(operands),
        out_specs=pl.BlockSpec(shape, lambda i: (0, 0, 0, 0)),
        scratch_shapes=[pltpu.VMEM((valid, pheight, most * out), BF16)],
        compiler_params=WIDE,
        cost_estimate=NO_COST,
        name="weights_backward",
    )(*operands)


def features_backward(x, weights, group, pieces, start, h, place, fit, prows):
    valid, pheight, deep = x.shape
    out = weights.shape[1]
    ha, branches = pheight // prows, len(group)
    shifts = [g[0] for g in group if g[0] is not None]
    operands = [h.reshape(1), start, weights, place, *shifts, *pieces]
    high = place.shape[1]
    most = max(len(moves(g[3])) for g in group)
    most_sides = max(len(sides_of(g[3])) for g in group)

    def kernel(h_ref, start_ref, w_ref, place_ref, *refs):
        shift_refs = list(refs[: len(shifts)])
        piece_refs = refs[len(shifts) : len(operands) - 4]
        last_ref, moved_ref, wide_ref, total_ref, held_ref = refs[len(operands) - 4 :]
        for g, (shift, first, rate, taps) in enumerate(group):
            steps, sides = moves(taps), sides_of(taps)
            s_ref = None if shift is None else shift_refs.pop(0)
            build_moved(piece_refs, moved_ref, s_ref, g, branches, valid, ha, prows, out)
            for i, b in enumerate(sides):
                for n, a in enumerate(steps):
                    wide_ref[i, n * out : (n + 1) * out] = w_ref[first + taps.index((a, b))]
            wide = len(steps) * out
            for i, b in enumerate(sides):

                def columns(w, count):
                    values = moved_ref[pl.ds(w - b * rate, count), :, :wide].reshape(count * pheight, wide)
                    part = dot(values, wide_ref[i, :wide], NN).reshape(count, pheight, deep)
                    if g or b != 0:
                        total_ref[pl.ds(w, count)] += part
                    else:
                        total_ref[pl.ds(w, count)] = part + start_ref[...][None]

                in_steps(*span(-b, rate, valid), 4, columns)
        held_ref[valid * prows :] = jnp.zeros((high - valid * prows, deep), BF16)
        for k in range(ha):
            block = total_ref[:, k * prows : (k + 1) * prows, :].astype(BF16)
            held_ref[: valid * prows] = block.reshape(valid * prows, deep)
            last_ref[h_ref[0] ^ k] = dot(place_ref[...], held_ref[...], NN).astype(BF16)

    return pl.pallas_call(
        kernel,
        out_shape=jax.ShapeDtypeStruct((ha, fit, deep), BF16),
        grid=(1,),
        in_specs=[SCALAR] + loaded(operands[1:]),
        out_specs=pl.BlockSpec((ha, fit, deep), lambda i: (0, 0, 0)),
        scratch_shapes=[
            pltpu.VMEM((valid, pheight, most * out), BF16),
            pltpu.VMEM((most_sides, most * out, deep), BF16),
            pltpu.VMEM(x.shape, F32),
            pltpu.VMEM((high, deep), BF16),
        ],
        compiler_params=WIDE,
        cost_estimate=NO_COST,
        name="features_backward",
    )(*operands)


def real_rows(pixels, prows, rows):
    return (lax.broadcasted_iota(jnp.int32, (pixels, 1), 0) % prows < rows).astype(F32)


def total_of(refs):
    return tree_sum([r[...] for r in refs])


def column_sum(values):
    return jnp.sum(values, axis=0, keepdims=True)


def small_kernel(kernel, name, operands, shapes):
    return pl.pallas_call(
        kernel,
        out_shape=[jax.ShapeDtypeStruct(s, t) for s, t in shapes],
        in_specs=[WHOLE] * len(operands),
        out_specs=[WHOLE] * len(shapes),
        compiler_params=PARAMS,
        cost_estimate=NO_COST,
        name=name,
    )(*operands)


def branch_sums(parts, pool_part):
    _, pixels, out = parts[0].shape
    images = pool_part.shape[0]

    def kernel(low, low_got, low_last, high, high_got, high_last, pool_ref, branch_ref, sum_ref):
        for j in range(4):
            own, got, last = (low, low_got, low_last) if j < 2 else (high, high_got, high_last)
            value = own[j % 2] + got[0, j % 2].astype(F32) + last[j % 2].astype(F32)
            branch_ref[j] = value
            sum_ref[j : j + 1] = column_sum(value)
            sum_ref[4 + j : 5 + j] = column_sum(value * value)
        sum_ref[8:] = pool_ref[...]

    shapes = [((4, pixels, out), F32), ((8 + images, out), F32)]
    return small_kernel(kernel, "branch_sums", [*parts, pool_part], shapes)


def project(sums, branch, scales, shifts, counts, own, proj, rows, pixel_total):
    _, pixels, out = branch.shape
    images = counts.shape[0]
    prows = own.shape[0]
    many = len(sums)

    def kernel(*refs):
        branch_ref, scale_ref, shift_ref, count_ref, own_ref, proj_ref = refs[many : many + 6]
        joined_ref, projected_ref, second_ref, stat_ref, pool_ref = refs[many + 6 :]
        total = total_of(refs[:many])
        mean = total[0:4] / pixel_total
        rstd = lax.rsqrt(total[4:8] / pixel_total - mean * mean + EPS)
        stat_ref[0:4] = mean
        stat_ref[4:8] = rstd
        scale, shift = scale_ref[...], shift_ref[...]
        for j in range(4):
            norm = (branch_ref[j] - mean[j : j + 1]) * rstd[j : j + 1]
            hid = norm * scale[j : j + 1] + shift[j : j + 1]
            joined_ref[:, j * out : (j + 1) * out] = silu(hid).astype(BF16)
        pool_out = total[8:]
        weighted = count_ref[...]
        pool_mean = column_sum(weighted * pool_out) / pixel_total
        pool_second = column_sum(weighted * pool_out * pool_out) / pixel_total
        pool_rstd = lax.rsqrt(pool_second - pool_mean * pool_mean + EPS)
        pool_norm = (pool_out - pool_mean) * pool_rstd
        pool_hid = pool_norm * scale[4:5] + shift[4:5]
        pool_ref[0] = pool_norm
        pool_ref[1] = pool_hid
        pool_ref[2] = jnp.broadcast_to(pool_rstd, pool_out.shape)
        pool_act = silu(pool_hid)
        spread = jnp.zeros((prows, out), F32)
        for i in range(images):
            spread = spread + own_ref[:, i : i + 1] * pool_act[i : i + 1]
        spread = spread.astype(BF16)
        for w in range(pixels // prows):
            joined_ref[w * prows : (w + 1) * prows, 4 * out :] = spread
        projected = dot(joined_ref[...], proj_ref[...], NN)
        projected_ref[...] = projected
        held = projected * real_rows(pixels, prows, rows)
        second_ref[...] = jnp.zeros(second_ref.shape, F32)
        second_ref[0:1] = column_sum(held)
        second_ref[1:2] = column_sum(held * held)

    shapes = [((pixels, 5 * out), BF16), ((pixels, out), F32), ((8, out), F32), ((8, out), F32), ((3, images, out), F32)]
    return small_kernel(kernel, "project", [*sums, branch, scales, shifts, counts, own, proj], shapes)


def activate(sums, projected, cot, out_scale, out_shift, prows, rows, pixel_total):
    pixels, out = projected.shape
    many = len(sums)

    def kernel(*refs):
        projected_ref, cot_ref, scale_ref, shift_ref = refs[many : many + 4]
        act_ref, norm_ref, dhid_ref, third_ref, rstd_ref = refs[many + 4 :]
        total = total_of(refs[:many])
        mean = total[0:1] / pixel_total
        rstd = lax.rsqrt(total[1:2] / pixel_total - mean * mean + EPS)
        rstd_ref[...] = jnp.broadcast_to(rstd, rstd_ref.shape)
        norm = (projected_ref[...] - mean) * rstd
        norm_ref[...] = norm
        hid = norm * scale_ref[...] + shift_ref[...]
        act_ref[...] = silu(hid).astype(BF16)
        dhid = cot_ref[...].astype(F32) * real_rows(pixels, prows, rows) * silu_slope(hid)
        dhid_ref[...] = dhid
        third_ref[...] = jnp.zeros(third_ref.shape, F32)
        third_ref[0:1] = column_sum(dhid)
        third_ref[1:2] = column_sum(dhid * norm)

    shapes = [((pixels, out), BF16), ((pixels, out), F32), ((pixels, out), F32), ((8, out), F32), ((8, out), F32)]
    operands = [*sums, projected, cot, out_scale[None], out_shift[None]]
    return small_kernel(kernel, "activate", operands, shapes)


def unproject(sums, norm, dhid, rstd, out_scale, proj, joined, branch, stats, scales, shifts, own, ha, rows, pixel_total):
    _, pixels, out = branch.shape
    prows, images = own.shape
    many = len(sums)

    def kernel(*refs):
        norm_ref, dhid_ref, rstd_ref, oscale_ref, proj_ref, joined_ref = refs[many : many + 6]
        branch_ref, stat_ref, scale_ref, shift_ref, own_ref = refs[many + 6 : many + 11]
        third_ref, grad_ref, back_ref, fourth_ref = refs[many + 11 :]
        total = total_of(refs[:many])
        third_ref[...] = total
        mask = real_rows(pixels, prows, rows)
        dproj = dhid_ref[...] - (total[0:1] + norm_ref[...] * total[1:2]) / pixel_total
        dproj = (oscale_ref[...] * rstd_ref[0:1] * dproj * mask).astype(BF16)
        grad = dot(joined_ref[...], dproj, TN)
        grad_ref[...] = jnp.zeros(grad_ref.shape, BF16)
        few = 5 * out // ha
        for d in range(ha):
            grad_ref[d, :, :few] = grad[d * few : (d + 1) * few].T.astype(BF16)
        for j in range(5):
            dact = dot(dproj, proj_ref[j * out : (j + 1) * out], NT)
            if j < 4:
                branch_norm = (branch_ref[j] - stat_ref[j : j + 1]) * stat_ref[4 + j : 5 + j]
                hid = branch_norm * scale_ref[j : j + 1] + shift_ref[j : j + 1]
                back = dact * silu_slope(hid) * mask
                back_ref[j] = back
                fourth_ref[j : j + 1] = column_sum(back)
                fourth_ref[4 + j : 5 + j] = column_sum(back * branch_norm)
            else:
                across = jnp.sum(dact.reshape(pixels // prows, prows, out), axis=0)
                for i in range(images):
                    fourth_ref[8 + i : 9 + i] = column_sum(own_ref[:, i : i + 1] * across)

    shapes = [((8, out), F32), ((ha, out, out), BF16), ((4, pixels, out), F32), ((8 + images, out), F32)]
    operands = [*sums, norm, dhid, rstd, out_scale[None], proj, joined, branch, stats, scales, shifts, own]
    return small_kernel(kernel, "unproject", operands, shapes)


def branch_gradients(sums, back, branch, stats, scales, counts, pool, prows, rows, pixel_total):
    _, pixels, out = branch.shape
    images = counts.shape[0]
    many = len(sums)

    def kernel(*refs):
        back_ref, branch_ref, stat_ref, scale_ref, count_ref, pool_ref = refs[many : many + 6]
        grad_ref, dpool_ref, sum_ref = refs[many + 6 :]
        total = total_of(refs[:many])
        mask = real_rows(pixels, prows, rows)
        for j in range(4):
            rstd = stat_ref[4 + j : 5 + j]
            norm = (branch_ref[j] - stat_ref[j : j + 1]) * rstd
            value = back_ref[j] - (total[j : j + 1] + norm * total[4 + j : 5 + j]) / pixel_total
            grad_ref[j] = (scale_ref[j : j + 1] * rstd * value * mask).astype(BF16)
        dhid = silu_slope(pool_ref[1]) * total[8:]
        pool_shift = column_sum(dhid)
        pool_scale = column_sum(dhid * pool_ref[0])
        value = dhid - count_ref[...] * (pool_shift + pool_ref[0] * pool_scale) / pixel_total
        dpool_ref[...] = (scale_ref[4:5] * pool_ref[2] * value).astype(BF16)
        sum_ref[...] = jnp.zeros(sum_ref.shape, F32)
        sum_ref[0:4] = total[4:8]
        sum_ref[4:5] = pool_scale
        sum_ref[5:9] = total[0:4]
        sum_ref[9:10] = pool_shift

    shapes = [((4, pixels, out), BF16), ((images, out), BF16), ((16, out), F32)]
    operands = [*sums, back, branch, stats, scales, counts, pool]
    return small_kernel(kernel, "branch_gradients", operands, shapes)


def local(
    features,
    row_image,
    cotangent,
    w_one,
    dilated_weight,
    w_pool,
    w_proj,
    scales,
    shifts,
    out_scale,
    out_shift,
):
    micro, rows, cols, channels = features.shape
    ha, wa = lax.axis_size("ha"), lax.axis_size("wa")
    h, z = lax.axis_index("ha"), lax.axis_index("wa")
    planes = wa // micro
    batch, part = z // planes, z % planes
    deep = w_one.shape[0] // planes
    out = w_one.shape[1] * wa
    valid = cols * wa - PADC
    blocks = -(-valid // cols)
    prows = -(-rows // 16) * 16
    height, pheight = rows * ha, prows * ha
    images = IMG_DEV * ha
    pixels = float(height * valid)
    size = cols * rows

    fast = planes == 1 and wa == 4 and 6 * valid * pheight * out < (16 << 20) and channels % out == 0 and deep == out

    taps = [live_taps(r, valid) for r in RATES]
    few = w_proj.shape[0]
    side = jnp.pad(w_proj.T, ((0, 0), (0, w_one.shape[0] - few)))
    turned = dilated_weight.swapaxes(2, 3)
    if fast:
        weights = pack_weights(w_one.T, turned, w_pool.T, side, taps)
    else:
        picked = [turned[j, 3 * (a + 1) + b + 1] for j in range(3) for a, b in taps[j]]
        weights = gather_columns(jnp.stack([w_one.T, *picked, w_pool.T, side]))

    if fast:
        slots = extract(features.transpose(1, 2, 0, 3), cotangent.transpose(1, 2, 0, 3), z)
        tall, fit = ceil_to(size, 16), ceil_to(valid * rows, 16)
        slots = [slots[0]] + [swap(slots[k], "wa", k, lambda i: i < blocks) for k in range(1, wa)]
        early = gather_early(weights, slots[1])
        high, thick = ceil_to(blocks * tall, 128), ceil_to(fit, 128)
        in_piece = block_rows(high, tall, rows, cols, valid, rows)
        in_chunk = block_rows(high, tall, rows, cols, valid, prows)
        spots = spots_of(np.arange(fit), in_piece)
        cot_spots = spots_of(np.arange(valid * prows), in_chunk)
        send, cot = choose(slots, z, blocks, spots, cot_spots, deep)
        raw = lax.all_to_all(send, "ha", 0, 0, tiled=True)
    else:
        f = features.transpose(0, 2, 1, 3).reshape(micro, size, ha, planes, deep)
        f = f.transpose(0, 3, 1, 2, 4).reshape(wa, size, ha * deep)
        c = cotangent.transpose(0, 2, 1, 3).reshape(micro, size, out)
        load = jnp.concatenate([f, jnp.repeat(c, planes, axis=0)], axis=-1)
        slots = [take(load, z)]
        for k in range(1, wa):
            slots.append(swap(take(load, z ^ k), "wa", k, lambda i: i < blocks))
        slots = jnp.stack(slots)
        block = jnp.concatenate([take(slots, z ^ j) for j in range(blocks)])[: valid * rows]
        raw = block[:, : ha * deep].reshape(valid * rows, ha, deep).swapaxes(0, 1)
        raw = lax.all_to_all(raw, "ha", 0, 0, tiled=True)
        cot = block[:, ha * deep :].reshape(valid, rows, out)
        cot = jnp.pad(cot, ((0, 0), (0, prows - rows), (0, 0))).reshape(valid * prows, out)
    if fast:
        weights = gather_late(weights, early, *slots)
    if fast:
        proj = order_chunks(*gather_chunks(weights[-1]), h, few)
    else:
        proj = in_order(*gather_chunks(weights[-1]))[..., :few].swapaxes(1, 2).reshape(ha * few, out)
    if planes > 1:
        weights = lax.dynamic_slice_in_dim(weights, part * deep, deep, 2)
    wide_pool = weights[-2]

    order = h ^ jnp.arange(ha, dtype=jnp.int32)
    labels = by_distance(take(row_image, batch).reshape(ha, rows))
    number = order[:, None] * rows + jnp.arange(rows, dtype=jnp.int32)[None, :]
    pad = ((0, 0), (0, prows - rows))
    labels = jnp.pad(labels, pad, constant_values=-1).reshape(pheight)
    number = jnp.pad(number, pad, constant_values=-(1 << 20)).reshape(pheight)
    same = (labels[:, None] == labels[None, :]) & (labels >= 0)[:, None]
    apart = number[None, :] - number[:, None]
    shift = [
        jnp.stack([(same & (apart == a * r)).astype(BF16) for a in (-1, 1)]) for r in RATES
    ]
    ids = jnp.arange(images, dtype=jnp.int32)
    member = (labels[:, None] == ids[None, :]).astype(F32)
    counts = jnp.sum(member, axis=0) * valid
    own = member[:prows]
    mask = jnp.tile(jnp.sum(own, axis=1), valid)[:, None]

    ahead = [1, 1 + len(taps[0]), 1 + len(taps[0]) + len(taps[1])]
    group = [(None, 0, 0, [(0, 0)])] + [(shift[j], ahead[j], RATES[j], taps[j]) for j in range(3)]
    if fast:
        place = spots_of(padded_rows(valid * prows, valid, prows, rows), np.arange(thick))
        x, row_sums = arrange(raw, place, h, valid, prows)
        unplace = spots_of(np.arange(fit), padded_rows(ceil_to(valid * prows, 128), valid, prows, rows))
    else:
        x = by_distance(raw).reshape(ha, valid, rows, deep)
        x = jnp.pad(x, ((0, 0), (0, 0), (0, prows - rows), (0, 0)))
        x = x.swapaxes(0, 1).reshape(valid, pheight, deep)
        row_sums = jnp.sum(x.astype(F32), axis=0)
    if fast:
        branch_parts = reduce_square(*forward_kernel(x, weights, group, prows))
    else:
        sums = jnp.stack([forward_plain(x, s, weights[n : n + len(t)], r, t) for s, n, r, t in group])
        sums = sums.astype(BF16).reshape(len(group), valid, ha // 2, 2, prows, out)
        sums = sums.transpose(3, 2, 0, 1, 4, 5).reshape(2, ha // 2, len(group), valid * prows, out)
        branch = sum_chunks(spread_chunks(sums[0], sums[1]), planes)
    pooled = (jnp.dot(member.T, row_sums, precision=HIGHEST) / counts[:, None]).astype(BF16)
    pool_part = dot(pooled, wide_pool, NT)

    weighted = counts[:, None]
    once = (part == 0).astype(F32)
    if fast:
        branch, first = branch_sums(branch_parts, pool_part)
        joined, projected, second, stats, pool = project(
            plane_parts(first), branch, scales, shifts, weighted, own, proj, rows, pixels
        )
        activation, proj_norm, dproj_hid, third, proj_rstd = activate(
            plane_parts(second), projected, cot, out_scale, out_shift, prows, rows, pixels
        )
        third, grad_proj, dhid, fourth = unproject(
            plane_parts(third),
            proj_norm,
            dproj_hid,
            proj_rstd,
            out_scale,
            proj,
            joined,
            branch,
            stats,
            scales,
            shifts,
            own,
            ha,
            rows,
            pixels,
        )
        dbranch, dpool, sums = branch_gradients(
            plane_parts(fourth), dhid, branch, stats, scales, weighted, pool, prows, rows, pixels
        )
        sums = jnp.concatenate([sums[:10], third[:2]])
    else:
        first = plane_sum(
            jnp.concatenate(
                [once * jnp.sum(branch, axis=1), once * jnp.sum(branch * branch, axis=1), pool_part]
            ),
            planes,
        )
        mean = first[0:4] / pixels
        rstd = lax.rsqrt(first[4:8] / pixels - mean * mean + EPS)
        pool_out = first[8:]
        norm = (branch - mean[:, None]) * rstd[:, None]
        hid = norm * scales[:4, None] + shifts[:4, None]
        act = silu(hid)
        weighted = counts[:, None]
        pool_mean = jnp.sum(weighted * pool_out, axis=0) / pixels
        pool_second = jnp.sum(weighted * pool_out * pool_out, axis=0) / pixels
        pool_rstd = lax.rsqrt(pool_second - pool_mean * pool_mean + EPS)
        pool_norm = (pool_out - pool_mean) * pool_rstd
        pool_hid = pool_norm * scales[4] + shifts[4]
        spread = jnp.dot(own, silu(pool_hid), precision=HIGHEST)
        spread = jnp.broadcast_to(spread[None], (valid, prows, out)).reshape(valid * prows, out)
        joined = jnp.concatenate([act[0], act[1], act[2], act[3], spread], axis=-1).astype(BF16)
        projected = jnp.dot(joined, proj, preferred_element_type=F32)

        held = projected * mask
        second = plane_sum(
            jnp.stack([jnp.sum(held, axis=0), jnp.sum(held * held, axis=0)]) * once, planes
        )
        proj_mean = second[0] / pixels
        proj_rstd = lax.rsqrt(second[1] / pixels - proj_mean * proj_mean + EPS)
        proj_norm = (projected - proj_mean) * proj_rstd
        proj_hid = proj_norm * out_scale + out_shift
        activation = silu(proj_hid).astype(BF16)
        dproj_hid = cot.astype(F32) * mask * silu_slope(proj_hid)
        third = plane_sum(
            jnp.stack([jnp.sum(dproj_hid, axis=0), jnp.sum(dproj_hid * proj_norm, axis=0)]) * once, planes
        )
        dproj = (
            out_scale * proj_rstd * (dproj_hid - (third[0] + proj_norm * third[1]) / pixels) * mask
        ).astype(BF16)
        djoined = lax.dot_general(dproj, proj, (((1,), (1,)), ((), ())), preferred_element_type=F32)
        grad_proj = dot(dproj, joined, TN)
        dact = jnp.stack([djoined[:, j * out : (j + 1) * out] for j in range(4)])
        dspread = jnp.sum(djoined[:, 4 * out :].reshape(valid, prows, out), axis=0)
        image_part = jnp.dot(own.T, dspread, precision=HIGHEST)
        dhid = dact * silu_slope(hid) * mask
        fourth = plane_sum(
            jnp.concatenate([jnp.sum(dhid, axis=1), jnp.sum(dhid * norm, axis=1), image_part]) * once,
            planes,
        )
        branch_shift, branch_scale, image_total = fourth[0:4], fourth[4:8], fourth[8:]
        dbranch = (
            (scales[:4] * rstd)[:, None]
            * (dhid - (branch_shift[:, None] + norm * branch_scale[:, None]) / pixels)
            * mask
        ).astype(BF16)
        dpool_hid = silu_slope(pool_hid) * image_total
        pool_shift = jnp.sum(dpool_hid, axis=0)
        pool_scale = jnp.sum(dpool_hid * pool_norm, axis=0)
        dpool = (
            scales[4] * pool_rstd * (dpool_hid - weighted * (pool_shift + pool_norm * pool_scale) / pixels)
        ).astype(BF16)
        sums = jnp.concatenate([branch_scale, pool_scale[None], branch_shift, pool_shift[None], third])
    grad_pool = dot(dpool, pooled, TN)
    dpooled = dot(dpool, wide_pool, NN)

    total = jnp.dot(member, dpooled / counts[:, None], precision=HIGHEST)
    if fast:
        pieces = gather_square(dbranch)
        tap_grads = weights_backward(x, group, pieces, wa, prows)
        back = features_backward(x, weights, group, pieces, total, h, unplace, fit, prows)
    else:
        total = jnp.broadcast_to(total[None], (valid,) + total.shape)
        near, far = gather_chunks(dbranch)
        every = jnp.stack([near, far], axis=1).reshape(ha, len(group), valid, prows, out)
        every = every.transpose(1, 2, 0, 3, 4).reshape(len(group), valid, pheight, out)
        found = []
        for (s, n, r, t), d in zip(group, every):
            grads, total = backward_plain(x, s, weights[n : n + len(t)], r, t, d, total)
            found.append(grads.reshape(len(t), wa, out // wa, deep).swapaxes(0, 1).astype(BF16))
        tap_grads = jnp.concatenate(found, axis=1)
        back = total.astype(BF16).reshape(valid, ha, prows, deep)[:, :, :rows]
        back = back.swapaxes(0, 1).reshape(ha, valid * rows, deep)
        back = by_distance(back)

    def in_place(grads):
        if planes == 1:
            return grads
        full = jnp.zeros(grads.shape[:-1] + (deep * planes,), grads.dtype)
        return lax.dynamic_update_slice_in_dim(full, grads, part * deep, grads.ndim - 1)

    if not fast:
        grad_proj = (grad_proj * once).reshape(out, ha, few).swapaxes(0, 1)
        grad_proj = jnp.pad(grad_proj, ((0, 0), (0, 0), (0, w_one.shape[0] - few))).astype(BF16)
    proj_chunk = lax.psum_scatter(grad_proj, "ha", scatter_dimension=0, tiled=False)
    grad_pool = in_place(grad_pool.astype(BF16)).reshape(wa, 1, out // wa, -1)
    proj_chunk = proj_chunk.reshape(wa, 1, out // wa, -1)
    tap_grads = line_scatter(in_place(tap_grads))
    rest = jnp.concatenate([grad_pool, proj_chunk], axis=1)
    if not fast:
        rest = line_scatter(rest)
    tap_out = [tap_grads[n : n + len(t)] for n, t in zip(ahead, taps)]
    blank = jnp.zeros((out // wa, w_one.shape[0]), F32)
    atrous = []
    for j in range(3):
        if len(taps[j]) == 9:
            atrous.append(tap_out[j])
        else:
            found = {3 * (a + 1) + b + 1: tap_out[j][t] for t, (a, b) in enumerate(taps[j])}
            atrous.append(jnp.stack([found.get(t, blank) for t in range(9)]))
    atrous = jnp.stack(atrous)
    atrous_out = atrous.swapaxes(2, 3)
    back = lax.all_to_all(back, "ha", 0, 0, tiled=True)

    def home(i, k):
        return i ^ k < blocks

    if fast:
        piece_spots = spots_of(block_rows(wa * tall, tall, rows, cols, valid, rows), np.arange(thick))
        chunk_spots = spots_of(block_rows(wa * tall, tall, rows, cols, valid, prows), np.arange(valid * prows))
        got = unchoose(
            back, activation, z, blocks, size, piece_spots.reshape(wa, tall, thick), chunk_spots.reshape(wa, tall, -1)
        )
        got = [got[0]] + [swap(got[k], "wa", k, partial(home, k=k)) for k in range(1, wa)]
        df, acts = interleave(got, z, blocks, rows, cols, out, [atrous])
        wide = jnp.broadcast_to(jnp.pad(sums, ((0, 4), (0, 0)))[None], (wa, 16, out))
        rest = jnp.concatenate([rest.astype(F32).reshape(wa, -1, out), wide], axis=1)
        rest = exchange_sum(after(rest, got[0]))
        sums = rest[-16:-4]
        rest = rest[:-16].reshape(2, -1, out)
    else:

        def send_home(array):
            array = jnp.pad(array, ((0, wa * size - valid * rows), (0, 0))).reshape(wa, size, -1)
            got = [take(array, z)]
            got += [swap(take(array, z ^ k), "wa", k, partial(home, k=k)) for k in range(1, wa)]
            got = jnp.stack(got)
            got = jnp.where(z < blocks, got, jnp.zeros((), got.dtype))
            return jnp.stack([take(got, z ^ t) for t in range(wa)])

        back = back.swapaxes(0, 1).reshape(valid * rows, ha * deep)
        df = send_home(back).reshape(micro, planes, cols, rows, ha, deep)
        df = df.transpose(0, 3, 2, 4, 1, 5).reshape(features.shape)
        activation = activation.reshape(valid, prows, out)[:, :rows].reshape(valid * rows, out)
        acts = send_home(activation).reshape(micro, planes, cols, rows, out)[:, 0].swapaxes(1, 2)
    if not fast:
        sums = sums * once
        sums = tree_sum([sums] + [swap(sums, "wa", k) for k in range(1, wa)])
    one_out, pool_grad_out, proj_out = tap_grads[0].T, rest[0].T, rest[1][:, :few].T
    return (
        acts,
        df,
        one_out,
        atrous_out,
        pool_grad_out,
        proj_out,
        sums[0:5],
        sums[5:10],
        sums[11],
        sums[10],
    )


def solution(mesh):
    specs = (
        P(None, "ha", "wa", None),
        P(),
        P(None, "ha", "wa", None),
        P("ha", "wa"),
        P(None, None, "ha", "wa"),
        P("ha", "wa"),
        P("ha", "wa"),
        P(),
        P(),
        P(),
        P(),
    )
    out_specs = (
        P(None, "ha", "wa", None),
        P(None, "ha", "wa", None),
        P("ha", "wa"),
        P(None, None, "ha", "wa"),
        P("ha", "wa"),
        P("ha", "wa"),
        P(),
        P(),
        P(),
        P(),
    )
    return jax.shard_map(local, mesh=mesh, in_specs=specs, out_specs=out_specs, check_vma=False)
```

```python
from functools import partial

import jax
import jax.numpy as jnp
import numpy as np
from jax import lax
from jax.experimental import pallas as pl
from jax.experimental.pallas import tpu as pltpu
from jax.sharding import PartitionSpec as P

PADC = 7
IMG_DEV = 2
RATES = (6, 12, 18)
EPS = 1e-05
HIGHEST = lax.Precision.HIGHEST
F32 = jnp.float32
BF16 = jnp.bfloat16


def silu(u):
    return u * jax.nn.sigmoid(u)


def silu_slope(u):
    s = jax.nn.sigmoid(u)
    return s * (1.0 + u * (1.0 - s))


def swap(array, axis, bits, sources=None):
    count = lax.axis_size(axis)
    pairs = [(i, i ^ bits) for i in range(count) if sources is None or sources(i)]
    return lax.ppermute(array, axis, pairs)


def after(value, *others):
    return lax.optimization_barrier((value, *others))[0]


def tree_sum(parts):
    while len(parts) > 1:
        parts = [parts[i] + parts[i + 1] for i in range(0, len(parts), 2)]
    return parts[0]


def plane_parts(array):
    pair = array + swap(array, "ha", 1)
    return [pair] + [swap(pair, "ha", k) for k in range(2, lax.axis_size("ha"), 2)]


def plane_sum(array, groups):
    total = tree_sum(plane_parts(array))
    bits = 1
    while bits < groups:
        total = total + swap(total, "wa", bits)
        bits *= 2
    return total


def take(array, index):
    return lax.dynamic_index_in_dim(array, index, 0, keepdims=False)


def by_distance(array):
    h = lax.axis_index("ha")
    return jnp.stack([take(array, h ^ k) for k in range(array.shape[0])])


def spread_chunks(even, odd):
    other = swap(odd, "ha", 1)
    both = [even[q].astype(F32) + other[q].astype(F32) for q in range(even.shape[0])]
    return both[:1] + [swap(both[q].astype(BF16), "ha", 2 * q) for q in range(1, len(both))]


def sum_chunks(parts, groups):
    total = tree_sum([part.astype(F32) for part in parts])
    bits = 1
    while bits < groups:
        total = total + swap(total.astype(BF16), "wa", bits).astype(F32)
        bits *= 2
    return total


def reduce_square(even, odd):
    other = swap(odd, "ha", 1)
    half = even.shape[1] // 2
    low = even[:, :half].astype(F32) + other[:, :half].astype(F32)
    high = even[:, half:].astype(F32) + other[:, half:].astype(F32)
    low_got = swap(low[1::2].astype(BF16), "ha", 2)
    high_got = swap(high[2:].astype(BF16), "ha", 4)
    low_last = swap((low[2] + low_got[1].astype(F32)).astype(BF16), "ha", 4)
    high_last = swap((high[1] + high_got[1].astype(F32)).astype(BF16), "ha", 2)
    return low[0], low_got, low_last, high[0], high_got, high_last


def gather_square(chunk):
    half = chunk.shape[0] // 2
    low, high = chunk[:half], chunk[half:]
    low_one = swap(low, "ha", 2)
    high_one = swap(high, "ha", 4)
    low_two = swap(jnp.stack([low, low_one]), "ha", 4)
    high_two = swap(jnp.stack([high, high_one]), "ha", 2)
    near = [chunk, low_one, high_one, low_two, high_two]
    return near + [swap(piece, "ha", 1) for piece in near]


def piece_of(k, branch, branches):
    q, half = k // 2, branches // 2
    first = 5 * (k % 2)
    low = branch < half
    inner = branch if low else branch - half
    if q == 0:
        return first, (branch,)
    if q == (1 if low else 2):
        return first + (1 if low else 2), (inner,)
    return first + (3 if low else 4), (int(q == 3), inner)


def gather_near(chunk):
    return [chunk] + [swap(chunk, "ha", 2 * q) for q in range(1, lax.axis_size("ha") // 2)]


def gather_chunks(chunk):
    near = jnp.stack(gather_near(chunk))
    return near, swap(near, "ha", 1)


def in_order(near, far):
    every = jnp.stack([near, far], axis=1)
    return by_distance(every.reshape((2 * near.shape[0],) + near.shape[1:]))


def gather_columns(own):
    gathered = lax.all_gather(own, "wa", axis=0, tiled=False)
    planes, count, few, rows = gathered.shape
    return gathered.swapaxes(0, 1).reshape(count, planes * few, rows)


def neighbour(array, pairs):
    return lax.ppermute(array, "wa", pairs)


def gather_early(own, others):
    right = neighbour(own, [(0, 1), (1, 2), (2, 3)])
    left = neighbour(own, [(1, 0), (2, 1), (3, 2)])
    right_two = neighbour(after(right, others), [(2, 3)])
    left_two = neighbour(after(left, others), [(1, 0), (2, 1)])
    return right, left, right_two, left_two


def gather_late(own, early, *others):
    z = lax.axis_index("wa")
    right, left, right_two, left_two = early
    left_three = neighbour(left_two, [(1, 0)])
    last_two = neighbour(after(right, *others), [(1, 2)])
    last_three = neighbour(last_two, [(2, 3)])
    found = [
        lax.select_n(z, own, right, last_two, last_three),
        lax.select_n(z, left, own, right, right_two),
        lax.select_n(z, left_two, left, own, right),
        lax.select_n(z, left_three, left_two, left, own),
    ]
    return jnp.concatenate(found, axis=1)


def exchange_sum(parts):
    z = lax.axis_index("wa")
    got = [swap(take(parts, z ^ k), "wa", k) for k in range(1, lax.axis_size("wa"))]
    return tree_sum([take(parts, z)] + got)


def line_scatter(parts):
    return lax.psum_scatter(parts, "wa", scatter_dimension=0, tiled=False).astype(F32)


def live_taps(rate, valid):
    return [(a, b) for a in (-1, 0, 1) for b in (-1, 0, 1) if b == 0 or valid > rate]


def span(b, rate, valid):
    return max(0, -b * rate), min(valid, valid - b * rate)


def moves(taps):
    return sorted({a for a, b in taps})


def forward_plain(x, shift, weights, rate, taps):
    valid = x.shape[0]
    moved = {
        a: x if a == 0 else jnp.einsum("pq,wqk->wpk", shift[(a + 1) // 2], x) for a in moves(taps)
    }
    out = jnp.zeros(x.shape[:2] + (weights.shape[1],), F32)
    for t, (a, b) in enumerate(taps):
        low, high = span(b, rate, valid)
        part = jnp.einsum(
            "wpk,ek->wpe", moved[a][low + b * rate : high + b * rate], weights[t], preferred_element_type=F32
        )
        out = out.at[low:high].add(part)
    return out


def backward_plain(x, shift, weights, rate, taps, grad, total):
    valid = x.shape[0]
    moved = {
        a: grad if a == 0 else jnp.einsum("pq,wqe->wpe", shift[(1 - a) // 2], grad)
        for a in moves(taps)
    }
    weight_grads = []
    for t, (a, b) in enumerate(taps):
        low, high = span(b, rate, valid)
        d = moved[a][low:high]
        source = slice(low + b * rate, high + b * rate)
        weight_grads.append(jnp.einsum("wpe,wpk->ek", d, x[source], preferred_element_type=F32))
        total = total.at[source].add(
            jnp.einsum("wpe,ek->wpk", d, weights[t], preferred_element_type=F32)
        )
    return jnp.stack(weight_grads), total


def dot(left, right, dims):
    return lax.dot_general(left, right, ((dims[0], dims[1]), ((), ())), preferred_element_type=F32)


NN = ((1,), (0,))
NT = ((1,), (1,))
TN = ((0,), (0,))
WHOLE = pl.BlockSpec(memory_space=pltpu.VMEM)
SCALAR = pl.BlockSpec(memory_space=pltpu.SMEM)
NO_COST = pl.CostEstimate(flops=0, bytes_accessed=0, transcendentals=0)
WIDE = pltpu.CompilerParams(vmem_limit_bytes=60 * 1024 * 1024)
PARAMS = pltpu.CompilerParams(vmem_limit_bytes=32 * 1024 * 1024)


def ceil_to(n, step):
    return -(-n // step) * step


def pack_weights(w_one, dilated, w_pool, w_proj, taps):
    rows, deep = w_one.shape
    order = [(j, 3 * (a + 1) + b + 1) for j in range(3) for a, b in taps[j]]

    def kernel(one_ref, dilated_ref, pool_ref, proj_ref, out_ref):
        out_ref[0] = one_ref[...]
        for at, (j, t) in enumerate(order):
            out_ref[at + 1] = dilated_ref[j, t]
        out_ref[len(order) + 1] = pool_ref[...]
        out_ref[len(order) + 2] = proj_ref[...]

    return pl.pallas_call(
        kernel,
        out_shape=jax.ShapeDtypeStruct((len(order) + 3, rows, deep), BF16),
        in_specs=[WHOLE] * 4,
        out_specs=WHOLE,
        compiler_params=PARAMS,
        name="pack_weights",
    )(w_one, dilated, w_pool, w_proj)


def spots_of(wanted, held):
    return ((wanted[:, None] == held[None, :]) & (wanted >= 0)[:, None]).astype(BF16)


def block_rows(count, tall, rows, cols, valid, pitch):
    row = np.arange(count)
    column = row // tall * cols + row % tall % cols
    real = (row % tall < rows * cols) & (column < valid)
    return np.where(real, column * pitch + row % tall // cols, -1)


def padded_rows(count, valid, prows, rows):
    row = np.arange(count)
    real = (row < valid * prows) & (row % prows < rows)
    return np.where(real, row // prows * rows + row % prows, -1)


def extract(features, cotangent, z):
    rows, cols, micro, channels = features.shape
    out = cotangent.shape[-1]
    size = rows * cols
    steps = channels // out

    def kernel(z_ref, f_ref, c_ref, *refs):
        outs, held_ref = refs[:-1], refs[-1]

        def put(ref):
            values = ref[...]
            for m in range(micro):
                held_ref[m] = values[:, m, :].astype(F32)
            for k in range(micro):
                outs[k][...] = held_ref[z_ref[0] ^ k].astype(BF16)

        @pl.when(pl.program_id(0) < steps)
        def _():
            put(f_ref)

        @pl.when(pl.program_id(0) == steps)
        def _():
            put(c_ref)

    return pl.pallas_call(
        kernel,
        grid=(steps + 1,),
        out_shape=[jax.ShapeDtypeStruct((size, channels + out), BF16)] * micro,
        in_specs=[
            SCALAR,
            pl.BlockSpec((size, micro, out), lambda i: (0, 0, jnp.minimum(i, steps - 1))),
            pl.BlockSpec((size, micro, out), lambda i: (0, 0, 0)),
        ],
        out_specs=[pl.BlockSpec((size, out), lambda i: (0, i))] * micro,
        scratch_shapes=[pltpu.VMEM((micro, size, out), F32)],
        compiler_params=PARAMS,
        name="extract",
    )(z.reshape(1), features.reshape(size, micro, channels), cotangent.reshape(size, micro, out))


def choose(slots, z, blocks, spots, last_spots, lanes):
    size, wide = slots[0].shape
    tall = ceil_to(size, 16)
    high = spots.shape[1]
    count = wide // lanes - 1

    def kernel(z_ref, *refs):
        spots_ref, last_ref, send_ref, own_ref, held_ref = refs[len(slots) :]
        held_ref[...] = jnp.zeros((high, wide), BF16)
        for v in range(len(slots)):

            @pl.when(z_ref[0] == v)
            def _():
                for j in range(blocks):
                    held_ref[j * tall : j * tall + size] = refs[v ^ j][...]

        for d in range(count):
            part = held_ref[:, d * lanes : (d + 1) * lanes]
            send_ref[d] = dot(spots_ref[...], part, NN).astype(BF16)
        own_ref[...] = dot(last_ref[...], held_ref[:, count * lanes :], NN).astype(BF16)

    return pl.pallas_call(
        kernel,
        out_shape=[
            jax.ShapeDtypeStruct((count, spots.shape[0], lanes), BF16),
            jax.ShapeDtypeStruct((last_spots.shape[0], lanes), BF16),
        ],
        in_specs=[SCALAR] + [WHOLE] * (len(slots) + 2),
        out_specs=[WHOLE] * 2,
        scratch_shapes=[pltpu.VMEM((high, wide), BF16)],
        compiler_params=PARAMS,
        name="choose",
    )(z.reshape(1), *slots, spots, last_spots)


def unchoose(pieces, last, z, blocks, size, spots, last_spots):
    ha, fit, out = pieces.shape
    planes, tall, thick = spots.shape
    wide = (ha + 1) * out

    def kernel(z_ref, pieces_ref, last_ref, spots_ref, last_spots_ref, *refs):
        outs, held_ref = refs[:-1], refs[-1]
        held_ref[fit:] = jnp.zeros((thick - fit, ha * out), BF16)
        for d in range(ha):
            held_ref[:fit, d * out : (d + 1) * out] = pieces_ref[d]
        for v in range(planes):

            @pl.when(z_ref[0] == v)
            def _():
                for j in range(planes):
                    if j < blocks:
                        block = dot(spots_ref[j], held_ref[...], NN).astype(BF16)
                        outs[v ^ j][:, : ha * out] = block[:size]
                        block = dot(last_spots_ref[j], last_ref[...], NN).astype(BF16)
                        outs[v ^ j][:, ha * out :] = block[:size]
                    else:
                        outs[v ^ j][...] = jnp.zeros((size, wide), BF16)

    return pl.pallas_call(
        kernel,
        out_shape=[jax.ShapeDtypeStruct((size, wide), BF16)] * planes,
        in_specs=[SCALAR] + [WHOLE] * 4,
        out_specs=[WHOLE] * planes,
        scratch_shapes=[pltpu.VMEM((thick, ha * out), BF16)],
        compiler_params=PARAMS,
        name="unchoose",
    )(z.reshape(1), pieces, last, spots, last_spots)


def order_chunks(near, far, h, few):
    half, out, _ = near.shape

    def kernel(h_ref, near_ref, far_ref, out_ref):
        for k in range(2 * half):
            chunk = (far_ref if k % 2 else near_ref)[k // 2]
            at = pl.multiple_of((h_ref[0] ^ k) * few, 16)
            out_ref[pl.ds(at, few), :] = chunk.T[:few]

    return pl.pallas_call(
        kernel,
        out_shape=jax.ShapeDtypeStruct((2 * half * few, out), BF16),
        in_specs=[SCALAR, WHOLE, WHOLE],
        out_specs=WHOLE,
        compiler_params=PARAMS,
        cost_estimate=NO_COST,
        name="order_chunks",
    )(h.reshape(1), near, far)


def interleave(got, z, blocks, rows, cols, out, others):
    micro = len(got)
    size, channels = got[0].shape
    channels -= out
    lanes = 2 * out

    def kernel(z_ref, *refs):
        df_ref, act_ref, held_ref = refs[-3:]

        def place(parts, wide):
            for k in range(micro):
                part = jnp.where(z_ref[0] < blocks, parts[k][...], jnp.zeros((), BF16))
                held_ref[z_ref[0] ^ k, :, :wide] = part
            return jnp.stack([held_ref[m, :, :wide] for m in range(micro)], axis=1)

        @pl.when(pl.program_id(0) == 0)
        def _():
            act_ref[...] = place(refs[micro : 2 * micro], out)

        df_ref[...] = place(refs[:micro], lanes)

    df, act = pl.pallas_call(
        kernel,
        grid=(channels // lanes,),
        out_shape=[jax.ShapeDtypeStruct((size, micro, n), BF16) for n in (channels, out)],
        in_specs=[SCALAR]
        + [pl.BlockSpec((size, lanes), lambda i: (0, i))] * micro
        + [pl.BlockSpec((size, out), lambda i: (0, channels // out))] * micro
        + [pl.BlockSpec(memory_space=pl.ANY)] * len(others),
        out_specs=[
            pl.BlockSpec((size, micro, lanes), lambda i: (0, 0, i)),
            pl.BlockSpec((size, micro, out), lambda i: (0, 0, 0)),
        ],
        scratch_shapes=[pltpu.VMEM((micro, size, lanes), BF16)],
        compiler_params=PARAMS,
        name="interleave",
    )(z.reshape(1), *got, *got, *others)
    return [a.reshape(rows, cols, micro, -1).transpose(2, 0, 1, 3) for a in (df, act)]


def arrange(raw, place, h, valid, prows):
    ha, tall, deep = raw.shape
    high = place.shape[1]

    def kernel(h_ref, raw_ref, place_ref, x_ref, sum_ref, held_ref):
        held_ref[tall:] = jnp.zeros((high - tall, deep), BF16)
        for k in range(ha):
            held_ref[:tall] = raw_ref[h_ref[0] ^ k]
            block = dot(place_ref[...], held_ref[...], NN).reshape(valid, prows, deep)
            x_ref[:, k * prows : (k + 1) * prows, :] = block.astype(BF16)
            sum_ref[k * prows : (k + 1) * prows] = jnp.sum(block, axis=0)

    return pl.pallas_call(
        kernel,
        out_shape=[
            jax.ShapeDtypeStruct((valid, ha * prows, deep), BF16),
            jax.ShapeDtypeStruct((ha * prows, deep), F32),
        ],
        in_specs=[SCALAR, WHOLE, WHOLE],
        out_specs=[WHOLE, WHOLE],
        scratch_shapes=[pltpu.VMEM((high, deep), BF16)],
        compiler_params=PARAMS,
        name="arrange",
    )(h.reshape(1), raw, place)


def sides_of(taps):
    return sorted({b for a, b in taps}, key=abs)


def in_steps(low, high, step, body):
    whole = (high - low) // step
    if whole:

        def one(i, carry):
            body(low + i * step, step)
            return carry

        lax.fori_loop(0, whole, one, 0)
    if (high - low) % step:
        body(low + whole * step, (high - low) % step)


def forward_kernel(x, weights, group, prows):
    valid, pheight, deep = x.shape
    out = weights.shape[1]
    half = pheight // prows // 2
    operands, flops = [x, weights], 0
    for shift, first, rate, taps in group:
        operands += [] if shift is None else [shift]
        spans = [span(b, rate, valid) for a, b in taps]
        flops += 2 * pheight * deep * out * sum(high - low for low, high in spans)
    most = max(len(moves(g[3])) for g in group)
    most_sides = max(len(sides_of(g[3])) for g in group)

    def kernel(x_ref, w_ref, *refs):
        ins = list(refs[: len(operands) - 2])
        even_ref, odd_ref, moved_ref, wide_ref, sum_ref = refs[len(operands) - 2 :]
        for g, (shift, first, rate, taps) in enumerate(group):
            steps, sides = moves(taps), sides_of(taps)
            for i, b in enumerate(sides):
                for n, a in enumerate(steps):
                    wide_ref[i, :, n * deep : (n + 1) * deep] = w_ref[first + taps.index((a, b))]
            source_ref = x_ref
            if shift is not None:
                s_ref = ins.pop(0)
                source_ref = moved_ref

                def move(w, carry):
                    values = x_ref[w]
                    both = dot(s_ref[...].reshape(2 * pheight, pheight), values, NN).astype(BF16)
                    moved_ref[w, :, :deep] = both[:pheight]
                    moved_ref[w, :, deep : 2 * deep] = values
                    moved_ref[w, :, 2 * deep :] = both[pheight:]
                    return carry

                lax.fori_loop(0, valid, move, 0, unroll=True)

            for i, b in enumerate(sides):

                def columns(w, count):
                    values = source_ref[pl.ds(w + b * rate, count)].reshape(count * pheight, -1)
                    part = dot(values, wide_ref[i, :, : len(steps) * deep], NT)
                    part = part.reshape(count, pheight, out)
                    if b == 0:
                        sum_ref[pl.ds(w, count)] = part
                    else:
                        sum_ref[pl.ds(w, count)] += part

                in_steps(*span(b, rate, valid), 7, columns)

            def store(w, carry):
                at = pl.multiple_of(w * prows, prows)
                for k in range(2 * half):
                    to = odd_ref if k % 2 else even_ref
                    to[k // 2, g, pl.ds(at, prows), :] = sum_ref[w, k * prows : (k + 1) * prows].astype(BF16)
                return carry

            lax.fori_loop(0, valid, store, 0, unroll=True)

    shape = jax.ShapeDtypeStruct((half, len(group), valid * prows, out), BF16)
    return pl.pallas_call(
        kernel,
        out_shape=[shape] * 2,
        in_specs=[WHOLE] * len(operands),
        out_specs=[WHOLE] * 2,
        scratch_shapes=[
            pltpu.VMEM((valid, pheight, most * deep), BF16),
            pltpu.VMEM((most_sides, out, most * deep), BF16),
            pltpu.VMEM((valid, pheight, out), F32),
        ],
        compiler_params=PARAMS,
        cost_estimate=NO_COST,
        name="forward",
    )(*operands)


def loaded(operands):
    return [
        pl.BlockSpec(a.shape, lambda i, n=a.ndim: (0,) * n, pipeline_mode=pl.Buffered(1)) for a in operands
    ]


def build_moved(pieces, moved_ref, s_ref, g, branches, valid, ha, prows, out):
    middle = 0 if s_ref is None else out

    def move(w, carry):
        at = pl.multiple_of(w * prows, prows)
        for k in range(ha):
            piece, index = piece_of(k, g, branches)
            rows = slice(k * prows, (k + 1) * prows)
            moved_ref[w, rows, middle : middle + out] = pieces[piece][(*index, pl.ds(at, prows))]
        if s_ref is not None:
            held = moved_ref[w, :, out : 2 * out]
            both = dot(s_ref[...].reshape(2 * ha * prows, ha * prows), held, NN).astype(BF16)
            moved_ref[w, :, :out] = both[ha * prows :]
            moved_ref[w, :, 2 * out :] = both[: ha * prows]
        return carry

    lax.fori_loop(0, valid, move, 0, unroll=True)


def weights_backward(x, group, pieces, wa, prows):
    valid, pheight, deep = x.shape
    out = pieces[0].shape[-1]
    few, ha, branches = out // wa, pheight // prows, len(group)
    shifts = [g[0] for g in group if g[0] is not None]
    operands = [x, *shifts, *pieces]
    shape = wa, sum(len(g[3]) for g in group), few, deep
    most = max(len(moves(g[3])) for g in group)

    def kernel(x_ref, *refs):
        shift_refs = list(refs[: len(shifts)])
        piece_refs = refs[len(shifts) : len(operands) - 1]
        grad_ref, moved_ref = refs[len(operands) - 1 :]
        done = 0
        for g, (shift, first, rate, taps) in enumerate(group):
            steps = moves(taps)
            s_ref = None if shift is None else shift_refs.pop(0)
            build_moved(piece_refs, moved_ref, s_ref, g, branches, valid, ha, prows, out)
            wide = len(steps) * out
            for b in sides_of(taps):
                low, high = span(b, rate, valid)
                left = moved_ref[low:high, :, :wide].reshape((high - low) * pheight, wide)
                right = x_ref[low + b * rate : high + b * rate].reshape((high - low) * pheight, deep)
                part = dot(left, right, TN).astype(BF16)
                for n, a in enumerate(steps):
                    t = done + taps.index((a, b))
                    for j in range(wa):
                        at = n * out + j * few
                        grad_ref[j, t] = part[at : at + few]
            done += len(taps)

    return pl.pallas_call(
        kernel,
        out_shape=jax.ShapeDtypeStruct(shape, BF16),
        grid=(1,),
        in_specs=loaded(operands),
        out_specs=pl.BlockSpec(shape, lambda i: (0, 0, 0, 0)),
        scratch_shapes=[pltpu.VMEM((valid, pheight, most * out), BF16)],
        compiler_params=WIDE,
        cost_estimate=NO_COST,
        name="weights_backward",
    )(*operands)


def features_backward(x, weights, group, pieces, start, h, place, fit, prows):
    valid, pheight, deep = x.shape
    out = weights.shape[1]
    ha, branches = pheight // prows, len(group)
    shifts = [g[0] for g in group if g[0] is not None]
    operands = [h.reshape(1), start, weights, place, *shifts, *pieces]
    high = place.shape[1]
    most = max(len(moves(g[3])) for g in group)
    most_sides = max(len(sides_of(g[3])) for g in group)

    def kernel(h_ref, start_ref, w_ref, place_ref, *refs):
        shift_refs = list(refs[: len(shifts)])
        piece_refs = refs[len(shifts) : len(operands) - 4]
        last_ref, moved_ref, wide_ref, total_ref, held_ref = refs[len(operands) - 4 :]
        for g, (shift, first, rate, taps) in enumerate(group):
            steps, sides = moves(taps), sides_of(taps)
            s_ref = None if shift is None else shift_refs.pop(0)
            build_moved(piece_refs, moved_ref, s_ref, g, branches, valid, ha, prows, out)
            for i, b in enumerate(sides):
                for n, a in enumerate(steps):
                    wide_ref[i, n * out : (n + 1) * out] = w_ref[first + taps.index((a, b))]
            wide = len(steps) * out
            for i, b in enumerate(sides):

                def columns(w, count):
                    values = moved_ref[pl.ds(w - b * rate, count), :, :wide].reshape(count * pheight, wide)
                    part = dot(values, wide_ref[i, :wide], NN).reshape(count, pheight, deep)
                    if g or b != 0:
                        total_ref[pl.ds(w, count)] += part
                    else:
                        total_ref[pl.ds(w, count)] = part + start_ref[...][None]

                in_steps(*span(-b, rate, valid), 4, columns)
        held_ref[valid * prows :] = jnp.zeros((high - valid * prows, deep), BF16)
        for k in range(ha):
            block = total_ref[:, k * prows : (k + 1) * prows, :].astype(BF16)
            held_ref[: valid * prows] = block.reshape(valid * prows, deep)
            last_ref[h_ref[0] ^ k] = dot(place_ref[...], held_ref[...], NN).astype(BF16)

    return pl.pallas_call(
        kernel,
        out_shape=jax.ShapeDtypeStruct((ha, fit, deep), BF16),
        grid=(1,),
        in_specs=[SCALAR] + loaded(operands[1:]),
        out_specs=pl.BlockSpec((ha, fit, deep), lambda i: (0, 0, 0)),
        scratch_shapes=[
            pltpu.VMEM((valid, pheight, most * out), BF16),
            pltpu.VMEM((most_sides, most * out, deep), BF16),
            pltpu.VMEM(x.shape, F32),
            pltpu.VMEM((high, deep), BF16),
        ],
        compiler_params=WIDE,
        cost_estimate=NO_COST,
        name="features_backward",
    )(*operands)


def real_rows(pixels, prows, rows):
    return (lax.broadcasted_iota(jnp.int32, (pixels, 1), 0) % prows < rows).astype(F32)


def total_of(refs):
    return tree_sum([r[...] for r in refs])


def column_sum(values):
    return jnp.sum(values, axis=0, keepdims=True)


def small_kernel(kernel, name, operands, shapes):
    return pl.pallas_call(
        kernel,
        out_shape=[jax.ShapeDtypeStruct(s, t) for s, t in shapes],
        in_specs=[WHOLE] * len(operands),
        out_specs=[WHOLE] * len(shapes),
        compiler_params=PARAMS,
        cost_estimate=NO_COST,
        name=name,
    )(*operands)


def branch_sums(parts, pool_part):
    _, pixels, out = parts[0].shape
    images = pool_part.shape[0]

    def kernel(low, low_got, low_last, high, high_got, high_last, pool_ref, branch_ref, sum_ref):
        for j in range(4):
            own, got, last = (low, low_got, low_last) if j < 2 else (high, high_got, high_last)
            value = own[j % 2] + got[0, j % 2].astype(F32) + last[j % 2].astype(F32)
            branch_ref[j] = value
            sum_ref[j : j + 1] = column_sum(value)
            sum_ref[4 + j : 5 + j] = column_sum(value * value)
        sum_ref[8:] = pool_ref[...]

    shapes = [((4, pixels, out), F32), ((8 + images, out), F32)]
    return small_kernel(kernel, "branch_sums", [*parts, pool_part], shapes)


def project(sums, branch, scales, shifts, counts, own, proj, rows, pixel_total):
    _, pixels, out = branch.shape
    images = counts.shape[0]
    prows = own.shape[0]
    many = len(sums)

    def kernel(*refs):
        branch_ref, scale_ref, shift_ref, count_ref, own_ref, proj_ref = refs[many : many + 6]
        joined_ref, projected_ref, second_ref, stat_ref, pool_ref = refs[many + 6 :]
        total = total_of(refs[:many])
        mean = total[0:4] / pixel_total
        rstd = lax.rsqrt(total[4:8] / pixel_total - mean * mean + EPS)
        stat_ref[0:4] = mean
        stat_ref[4:8] = rstd
        scale, shift = scale_ref[...], shift_ref[...]
        for j in range(4):
            norm = (branch_ref[j] - mean[j : j + 1]) * rstd[j : j + 1]
            hid = norm * scale[j : j + 1] + shift[j : j + 1]
            joined_ref[:, j * out : (j + 1) * out] = silu(hid).astype(BF16)
        pool_out = total[8:]
        weighted = count_ref[...]
        pool_mean = column_sum(weighted * pool_out) / pixel_total
        pool_second = column_sum(weighted * pool_out * pool_out) / pixel_total
        pool_rstd = lax.rsqrt(pool_second - pool_mean * pool_mean + EPS)
        pool_norm = (pool_out - pool_mean) * pool_rstd
        pool_hid = pool_norm * scale[4:5] + shift[4:5]
        pool_ref[0] = pool_norm
        pool_ref[1] = pool_hid
        pool_ref[2] = jnp.broadcast_to(pool_rstd, pool_out.shape)
        pool_act = silu(pool_hid)
        spread = jnp.zeros((prows, out), F32)
        for i in range(images):
            spread = spread + own_ref[:, i : i + 1] * pool_act[i : i + 1]
        spread = spread.astype(BF16)
        for w in range(pixels // prows):
            joined_ref[w * prows : (w + 1) * prows, 4 * out :] = spread
        projected = dot(joined_ref[...], proj_ref[...], NN)
        projected_ref[...] = projected
        held = projected * real_rows(pixels, prows, rows)
        second_ref[...] = jnp.zeros(second_ref.shape, F32)
        second_ref[0:1] = column_sum(held)
        second_ref[1:2] = column_sum(held * held)

    shapes = [((pixels, 5 * out), BF16), ((pixels, out), F32), ((8, out), F32), ((8, out), F32), ((3, images, out), F32)]
    return small_kernel(kernel, "project", [*sums, branch, scales, shifts, counts, own, proj], shapes)


def activate(sums, projected, cot, out_scale, out_shift, prows, rows, pixel_total):
    pixels, out = projected.shape
    many = len(sums)

    def kernel(*refs):
        projected_ref, cot_ref, scale_ref, shift_ref = refs[many : many + 4]
        act_ref, norm_ref, dhid_ref, third_ref, rstd_ref = refs[many + 4 :]
        total = total_of(refs[:many])
        mean = total[0:1] / pixel_total
        rstd = lax.rsqrt(total[1:2] / pixel_total - mean * mean + EPS)
        rstd_ref[...] = jnp.broadcast_to(rstd, rstd_ref.shape)
        norm = (projected_ref[...] - mean) * rstd
        norm_ref[...] = norm
        hid = norm * scale_ref[...] + shift_ref[...]
        act_ref[...] = silu(hid).astype(BF16)
        dhid = cot_ref[...].astype(F32) * real_rows(pixels, prows, rows) * silu_slope(hid)
        dhid_ref[...] = dhid
        third_ref[...] = jnp.zeros(third_ref.shape, F32)
        third_ref[0:1] = column_sum(dhid)
        third_ref[1:2] = column_sum(dhid * norm)

    shapes = [((pixels, out), BF16), ((pixels, out), F32), ((pixels, out), F32), ((8, out), F32), ((8, out), F32)]
    operands = [*sums, projected, cot, out_scale[None], out_shift[None]]
    return small_kernel(kernel, "activate", operands, shapes)


def unproject(sums, norm, dhid, rstd, out_scale, proj, joined, branch, stats, scales, shifts, own, ha, rows, pixel_total):
    _, pixels, out = branch.shape
    prows, images = own.shape
    many = len(sums)

    def kernel(*refs):
        norm_ref, dhid_ref, rstd_ref, oscale_ref, proj_ref, joined_ref = refs[many : many + 6]
        branch_ref, stat_ref, scale_ref, shift_ref, own_ref = refs[many + 6 : many + 11]
        third_ref, grad_ref, back_ref, fourth_ref = refs[many + 11 :]
        total = total_of(refs[:many])
        third_ref[...] = total
        mask = real_rows(pixels, prows, rows)
        dproj = dhid_ref[...] - (total[0:1] + norm_ref[...] * total[1:2]) / pixel_total
        dproj = (oscale_ref[...] * rstd_ref[0:1] * dproj * mask).astype(BF16)
        grad = dot(joined_ref[...], dproj, TN)
        grad_ref[...] = jnp.zeros(grad_ref.shape, BF16)
        few = 5 * out // ha
        for d in range(ha):
            grad_ref[d, :, :few] = grad[d * few : (d + 1) * few].T.astype(BF16)
        for j in range(5):
            dact = dot(dproj, proj_ref[j * out : (j + 1) * out], NT)
            if j < 4:
                branch_norm = (branch_ref[j] - stat_ref[j : j + 1]) * stat_ref[4 + j : 5 + j]
                hid = branch_norm * scale_ref[j : j + 1] + shift_ref[j : j + 1]
                back = dact * silu_slope(hid) * mask
                back_ref[j] = back
                fourth_ref[j : j + 1] = column_sum(back)
                fourth_ref[4 + j : 5 + j] = column_sum(back * branch_norm)
            else:
                across = jnp.sum(dact.reshape(pixels // prows, prows, out), axis=0)
                for i in range(images):
                    fourth_ref[8 + i : 9 + i] = column_sum(own_ref[:, i : i + 1] * across)

    shapes = [((8, out), F32), ((ha, out, out), BF16), ((4, pixels, out), F32), ((8 + images, out), F32)]
    operands = [*sums, norm, dhid, rstd, out_scale[None], proj, joined, branch, stats, scales, shifts, own]
    return small_kernel(kernel, "unproject", operands, shapes)


def branch_gradients(sums, back, branch, stats, scales, counts, pool, prows, rows, pixel_total):
    _, pixels, out = branch.shape
    images = counts.shape[0]
    many = len(sums)

    def kernel(*refs):
        back_ref, branch_ref, stat_ref, scale_ref, count_ref, pool_ref = refs[many : many + 6]
        grad_ref, dpool_ref, sum_ref = refs[many + 6 :]
        total = total_of(refs[:many])
        mask = real_rows(pixels, prows, rows)
        for j in range(4):
            rstd = stat_ref[4 + j : 5 + j]
            norm = (branch_ref[j] - stat_ref[j : j + 1]) * rstd
            value = back_ref[j] - (total[j : j + 1] + norm * total[4 + j : 5 + j]) / pixel_total
            grad_ref[j] = (scale_ref[j : j + 1] * rstd * value * mask).astype(BF16)
        dhid = silu_slope(pool_ref[1]) * total[8:]
        pool_shift = column_sum(dhid)
        pool_scale = column_sum(dhid * pool_ref[0])
        value = dhid - count_ref[...] * (pool_shift + pool_ref[0] * pool_scale) / pixel_total
        dpool_ref[...] = (scale_ref[4:5] * pool_ref[2] * value).astype(BF16)
        sum_ref[...] = jnp.zeros(sum_ref.shape, F32)
        sum_ref[0:4] = total[4:8]
        sum_ref[4:5] = pool_scale
        sum_ref[5:9] = total[0:4]
        sum_ref[9:10] = pool_shift

    shapes = [((4, pixels, out), BF16), ((images, out), BF16), ((16, out), F32)]
    operands = [*sums, back, branch, stats, scales, counts, pool]
    return small_kernel(kernel, "branch_gradients", operands, shapes)


def local(
    features,
    row_image,
    cotangent,
    w_one,
    dilated_weight,
    w_pool,
    w_proj,
    scales,
    shifts,
    out_scale,
    out_shift,
):
    micro, rows, cols, channels = features.shape
    ha, wa = lax.axis_size("ha"), lax.axis_size("wa")
    h, z = lax.axis_index("ha"), lax.axis_index("wa")
    planes = wa // micro
    batch, part = z // planes, z % planes
    deep = w_one.shape[0] // planes
    out = w_one.shape[1] * wa
    valid = cols * wa - PADC
    blocks = -(-valid // cols)
    prows = -(-rows // 16) * 16
    height, pheight = rows * ha, prows * ha
    images = IMG_DEV * ha
    pixels = float(height * valid)
    size = cols * rows

    fast = planes == 1 and wa == 4 and 6 * valid * pheight * out < (16 << 20) and channels % out == 0 and deep == out

    taps = [live_taps(r, valid) for r in RATES]
    few = w_proj.shape[0]
    side = jnp.pad(w_proj.T, ((0, 0), (0, w_one.shape[0] - few)))
    turned = dilated_weight.swapaxes(2, 3)
    if fast:
        weights = pack_weights(w_one.T, turned, w_pool.T, side, taps)
    else:
        picked = [turned[j, 3 * (a + 1) + b + 1] for j in range(3) for a, b in taps[j]]
        weights = gather_columns(jnp.stack([w_one.T, *picked, w_pool.T, side]))

    if fast:
        slots = extract(features.transpose(1, 2, 0, 3), cotangent.transpose(1, 2, 0, 3), z)
        tall, fit = ceil_to(size, 16), ceil_to(valid * rows, 16)
        slots = [slots[0]] + [swap(slots[k], "wa", k, lambda i: i < blocks) for k in range(1, wa)]
        early = gather_early(weights, slots[1])
        high, thick = ceil_to(blocks * tall, 128), ceil_to(fit, 128)
        in_piece = block_rows(high, tall, rows, cols, valid, rows)
        in_chunk = block_rows(high, tall, rows, cols, valid, prows)
        spots = spots_of(np.arange(fit), in_piece)
        cot_spots = spots_of(np.arange(valid * prows), in_chunk)
        send, cot = choose(slots, z, blocks, spots, cot_spots, deep)
        raw = lax.all_to_all(send, "ha", 0, 0, tiled=True)
    else:
        f = features.transpose(0, 2, 1, 3).reshape(micro, size, ha, planes, deep)
        f = f.transpose(0, 3, 1, 2, 4).reshape(wa, size, ha * deep)
        c = cotangent.transpose(0, 2, 1, 3).reshape(micro, size, out)
        load = jnp.concatenate([f, jnp.repeat(c, planes, axis=0)], axis=-1)
        slots = [take(load, z)]
        for k in range(1, wa):
            slots.append(swap(take(load, z ^ k), "wa", k, lambda i: i < blocks))
        slots = jnp.stack(slots)
        block = jnp.concatenate([take(slots, z ^ j) for j in range(blocks)])[: valid * rows]
        raw = block[:, : ha * deep].reshape(valid * rows, ha, deep).swapaxes(0, 1)
        raw = lax.all_to_all(raw, "ha", 0, 0, tiled=True)
        cot = block[:, ha * deep :].reshape(valid, rows, out)
        cot = jnp.pad(cot, ((0, 0), (0, prows - rows), (0, 0))).reshape(valid * prows, out)
    if fast:
        weights = gather_late(weights, early, *slots)
    if fast:
        proj = order_chunks(*gather_chunks(weights[-1]), h, few)
    else:
        proj = in_order(*gather_chunks(weights[-1]))[..., :few].swapaxes(1, 2).reshape(ha * few, out)
    if planes > 1:
        weights = lax.dynamic_slice_in_dim(weights, part * deep, deep, 2)
    wide_pool = weights[-2]

    order = h ^ jnp.arange(ha, dtype=jnp.int32)
    labels = by_distance(take(row_image, batch).reshape(ha, rows))
    number = order[:, None] * rows + jnp.arange(rows, dtype=jnp.int32)[None, :]
    pad = ((0, 0), (0, prows - rows))
    labels = jnp.pad(labels, pad, constant_values=-1).reshape(pheight)
    number = jnp.pad(number, pad, constant_values=-(1 << 20)).reshape(pheight)
    same = (labels[:, None] == labels[None, :]) & (labels >= 0)[:, None]
    apart = number[None, :] - number[:, None]
    shift = [
        jnp.stack([(same & (apart == a * r)).astype(BF16) for a in (-1, 1)]) for r in RATES
    ]
    ids = jnp.arange(images, dtype=jnp.int32)
    member = (labels[:, None] == ids[None, :]).astype(F32)
    counts = jnp.sum(member, axis=0) * valid
    own = member[:prows]
    mask = jnp.tile(jnp.sum(own, axis=1), valid)[:, None]

    ahead = [1, 1 + len(taps[0]), 1 + len(taps[0]) + len(taps[1])]
    group = [(None, 0, 0, [(0, 0)])] + [(shift[j], ahead[j], RATES[j], taps[j]) for j in range(3)]
    if fast:
        place = spots_of(padded_rows(valid * prows, valid, prows, rows), np.arange(thick))
        x, row_sums = arrange(raw, place, h, valid, prows)
        unplace = spots_of(np.arange(fit), padded_rows(ceil_to(valid * prows, 128), valid, prows, rows))
    else:
        x = by_distance(raw).reshape(ha, valid, rows, deep)
        x = jnp.pad(x, ((0, 0), (0, 0), (0, prows - rows), (0, 0)))
        x = x.swapaxes(0, 1).reshape(valid, pheight, deep)
        row_sums = jnp.sum(x.astype(F32), axis=0)
    if fast:
        branch_parts = reduce_square(*forward_kernel(x, weights, group, prows))
    else:
        sums = jnp.stack([forward_plain(x, s, weights[n : n + len(t)], r, t) for s, n, r, t in group])
        sums = sums.astype(BF16).reshape(len(group), valid, ha // 2, 2, prows, out)
        sums = sums.transpose(3, 2, 0, 1, 4, 5).reshape(2, ha // 2, len(group), valid * prows, out)
        branch = sum_chunks(spread_chunks(sums[0], sums[1]), planes)
    pooled = (jnp.dot(member.T, row_sums, precision=HIGHEST) / counts[:, None]).astype(BF16)
    pool_part = dot(pooled, wide_pool, NT)

    weighted = counts[:, None]
    once = (part == 0).astype(F32)
    if fast:
        branch, first = branch_sums(branch_parts, pool_part)
        joined, projected, second, stats, pool = project(
            plane_parts(first), branch, scales, shifts, weighted, own, proj, rows, pixels
        )
        activation, proj_norm, dproj_hid, third, proj_rstd = activate(
            plane_parts(second), projected, cot, out_scale, out_shift, prows, rows, pixels
        )
        third, grad_proj, dhid, fourth = unproject(
            plane_parts(third),
            proj_norm,
            dproj_hid,
            proj_rstd,
            out_scale,
            proj,
            joined,
            branch,
            stats,
            scales,
            shifts,
            own,
            ha,
            rows,
            pixels,
        )
        dbranch, dpool, sums = branch_gradients(
            plane_parts(fourth), dhid, branch, stats, scales, weighted, pool, prows, rows, pixels
        )
        sums = jnp.concatenate([sums[:10], third[:2]])
    else:
        first = plane_sum(
            jnp.concatenate(
                [once * jnp.sum(branch, axis=1), once * jnp.sum(branch * branch, axis=1), pool_part]
            ),
            planes,
        )
        mean = first[0:4] / pixels
        rstd = lax.rsqrt(first[4:8] / pixels - mean * mean + EPS)
        pool_out = first[8:]
        norm = (branch - mean[:, None]) * rstd[:, None]
        hid = norm * scales[:4, None] + shifts[:4, None]
        act = silu(hid)
        weighted = counts[:, None]
        pool_mean = jnp.sum(weighted * pool_out, axis=0) / pixels
        pool_second = jnp.sum(weighted * pool_out * pool_out, axis=0) / pixels
        pool_rstd = lax.rsqrt(pool_second - pool_mean * pool_mean + EPS)
        pool_norm = (pool_out - pool_mean) * pool_rstd
        pool_hid = pool_norm * scales[4] + shifts[4]
        spread = jnp.dot(own, silu(pool_hid), precision=HIGHEST)
        spread = jnp.broadcast_to(spread[None], (valid, prows, out)).reshape(valid * prows, out)
        joined = jnp.concatenate([act[0], act[1], act[2], act[3], spread], axis=-1).astype(BF16)
        projected = jnp.dot(joined, proj, preferred_element_type=F32)

        held = projected * mask
        second = plane_sum(
            jnp.stack([jnp.sum(held, axis=0), jnp.sum(held * held, axis=0)]) * once, planes
        )
        proj_mean = second[0] / pixels
        proj_rstd = lax.rsqrt(second[1] / pixels - proj_mean * proj_mean + EPS)
        proj_norm = (projected - proj_mean) * proj_rstd
        proj_hid = proj_norm * out_scale + out_shift
        activation = silu(proj_hid).astype(BF16)
        dproj_hid = cot.astype(F32) * mask * silu_slope(proj_hid)
        third = plane_sum(
            jnp.stack([jnp.sum(dproj_hid, axis=0), jnp.sum(dproj_hid * proj_norm, axis=0)]) * once, planes
        )
        dproj = (
            out_scale * proj_rstd * (dproj_hid - (third[0] + proj_norm * third[1]) / pixels) * mask
        ).astype(BF16)
        djoined = lax.dot_general(dproj, proj, (((1,), (1,)), ((), ())), preferred_element_type=F32)
        grad_proj = dot(dproj, joined, TN)
        dact = jnp.stack([djoined[:, j * out : (j + 1) * out] for j in range(4)])
        dspread = jnp.sum(djoined[:, 4 * out :].reshape(valid, prows, out), axis=0)
        image_part = jnp.dot(own.T, dspread, precision=HIGHEST)
        dhid = dact * silu_slope(hid) * mask
        fourth = plane_sum(
            jnp.concatenate([jnp.sum(dhid, axis=1), jnp.sum(dhid * norm, axis=1), image_part]) * once,
            planes,
        )
        branch_shift, branch_scale, image_total = fourth[0:4], fourth[4:8], fourth[8:]
        dbranch = (
            (scales[:4] * rstd)[:, None]
            * (dhid - (branch_shift[:, None] + norm * branch_scale[:, None]) / pixels)
            * mask
        ).astype(BF16)
        dpool_hid = silu_slope(pool_hid) * image_total
        pool_shift = jnp.sum(dpool_hid, axis=0)
        pool_scale = jnp.sum(dpool_hid * pool_norm, axis=0)
        dpool = (
            scales[4] * pool_rstd * (dpool_hid - weighted * (pool_shift + pool_norm * pool_scale) / pixels)
        ).astype(BF16)
        sums = jnp.concatenate([branch_scale, pool_scale[None], branch_shift, pool_shift[None], third])
    grad_pool = dot(dpool, pooled, TN)
    dpooled = dot(dpool, wide_pool, NN)

    total = jnp.dot(member, dpooled / counts[:, None], precision=HIGHEST)
    if fast:
        pieces = gather_square(dbranch)
        tap_grads = weights_backward(x, group, pieces, wa, prows)
        back = features_backward(x, weights, group, pieces, total, h, unplace, fit, prows)
    else:
        total = jnp.broadcast_to(total[None], (valid,) + total.shape)
        near, far = gather_chunks(dbranch)
        every = jnp.stack([near, far], axis=1).reshape(ha, len(group), valid, prows, out)
        every = every.transpose(1, 2, 0, 3, 4).reshape(len(group), valid, pheight, out)
        found = []
        for (s, n, r, t), d in zip(group, every):
            grads, total = backward_plain(x, s, weights[n : n + len(t)], r, t, d, total)
            found.append(grads.reshape(len(t), wa, out // wa, deep).swapaxes(0, 1).astype(BF16))
        tap_grads = jnp.concatenate(found, axis=1)
        back = total.astype(BF16).reshape(valid, ha, prows, deep)[:, :, :rows]
        back = back.swapaxes(0, 1).reshape(ha, valid * rows, deep)
        back = by_distance(back)

    def in_place(grads):
        if planes == 1:
            return grads
        full = jnp.zeros(grads.shape[:-1] + (deep * planes,), grads.dtype)
        return lax.dynamic_update_slice_in_dim(full, grads, part * deep, grads.ndim - 1)

    if not fast:
        grad_proj = (grad_proj * once).reshape(out, ha, few).swapaxes(0, 1)
        grad_proj = jnp.pad(grad_proj, ((0, 0), (0, 0), (0, w_one.shape[0] - few))).astype(BF16)
    proj_chunk = lax.psum_scatter(grad_proj, "ha", scatter_dimension=0, tiled=False)
    grad_pool = in_place(grad_pool.astype(BF16)).reshape(wa, 1, out // wa, -1)
    proj_chunk = proj_chunk.reshape(wa, 1, out // wa, -1)
    tap_grads = line_scatter(in_place(tap_grads))
    rest = jnp.concatenate([grad_pool, proj_chunk], axis=1)
    if not fast:
        rest = line_scatter(rest)
    tap_out = [tap_grads[n : n + len(t)] for n, t in zip(ahead, taps)]
    blank = jnp.zeros((out // wa, w_one.shape[0]), F32)
    atrous = []
    for j in range(3):
        if len(taps[j]) == 9:
            atrous.append(tap_out[j])
        else:
            found = {3 * (a + 1) + b + 1: tap_out[j][t] for t, (a, b) in enumerate(taps[j])}
            atrous.append(jnp.stack([found.get(t, blank) for t in range(9)]))
    atrous = jnp.stack(atrous)
    atrous_out = atrous.swapaxes(2, 3)
    back = lax.all_to_all(back, "ha", 0, 0, tiled=True)

    def home(i, k):
        return i ^ k < blocks

    if fast:
        piece_spots = spots_of(block_rows(wa * tall, tall, rows, cols, valid, rows), np.arange(thick))
        chunk_spots = spots_of(block_rows(wa * tall, tall, rows, cols, valid, prows), np.arange(valid * prows))
        got = unchoose(
            back, activation, z, blocks, size, piece_spots.reshape(wa, tall, thick), chunk_spots.reshape(wa, tall, -1)
        )
        got = [got[0]] + [swap(got[k], "wa", k, partial(home, k=k)) for k in range(1, wa)]
        df, acts = interleave(got, z, blocks, rows, cols, out, [atrous])
        wide = jnp.broadcast_to(jnp.pad(sums, ((0, 4), (0, 0)))[None], (wa, 16, out))
        rest = jnp.concatenate([rest.astype(F32).reshape(wa, -1, out), wide], axis=1)
        rest = exchange_sum(rest)
        sums = rest[-16:-4]
        rest = rest[:-16].reshape(2, -1, out)
    else:

        def send_home(array):
            array = jnp.pad(array, ((0, wa * size - valid * rows), (0, 0))).reshape(wa, size, -1)
            got = [take(array, z)]
            got += [swap(take(array, z ^ k), "wa", k, partial(home, k=k)) for k in range(1, wa)]
            got = jnp.stack(got)
            got = jnp.where(z < blocks, got, jnp.zeros((), got.dtype))
            return jnp.stack([take(got, z ^ t) for t in range(wa)])

        back = back.swapaxes(0, 1).reshape(valid * rows, ha * deep)
        df = send_home(back).reshape(micro, planes, cols, rows, ha, deep)
        df = df.transpose(0, 3, 2, 4, 1, 5).reshape(features.shape)
        activation = activation.reshape(valid, prows, out)[:, :rows].reshape(valid * rows, out)
        acts = send_home(activation).reshape(micro, planes, cols, rows, out)[:, 0].swapaxes(1, 2)
    if not fast:
        sums = sums * once
        sums = tree_sum([sums] + [swap(sums, "wa", k) for k in range(1, wa)])
    one_out, pool_grad_out, proj_out = tap_grads[0].T, rest[0].T, rest[1][:, :few].T
    return (
        acts,
        df,
        one_out,
        atrous_out,
        pool_grad_out,
        proj_out,
        sums[0:5],
        sums[5:10],
        sums[11],
        sums[10],
    )


def solution(mesh):
    specs = (
        P(None, "ha", "wa", None),
        P(),
        P(None, "ha", "wa", None),
        P("ha", "wa"),
        P(None, None, "ha", "wa"),
        P("ha", "wa"),
        P("ha", "wa"),
        P(),
        P(),
        P(),
        P(),
    )
    out_specs = (
        P(None, "ha", "wa", None),
        P(None, "ha", "wa", None),
        P("ha", "wa"),
        P(None, None, "ha", "wa"),
        P("ha", "wa"),
        P("ha", "wa"),
        P(),
        P(),
        P(),
        P(),
    )
    return jax.shard_map(local, mesh=mesh, in_specs=specs, out_specs=out_specs, check_vma=False)
```

```python
from functools import partial

import jax
import jax.numpy as jnp
import numpy as np
from jax import lax
from jax.experimental import pallas as pl
from jax.experimental.pallas import tpu as pltpu
from jax.sharding import PartitionSpec as P

PADC = 7
IMG_DEV = 2
RATES = (6, 12, 18)
EPS = 1e-05
HIGHEST = lax.Precision.HIGHEST
F32 = jnp.float32
BF16 = jnp.bfloat16


def silu(u):
    return u * jax.nn.sigmoid(u)


def silu_slope(u):
    s = jax.nn.sigmoid(u)
    return s * (1.0 + u * (1.0 - s))


def swap(array, axis, bits, sources=None):
    count = lax.axis_size(axis)
    pairs = [(i, i ^ bits) for i in range(count) if sources is None or sources(i)]
    return lax.ppermute(array, axis, pairs)


def after(value, *others):
    return lax.optimization_barrier((value, *others))[0]


def tree_sum(parts):
    while len(parts) > 1:
        parts = [parts[i] + parts[i + 1] for i in range(0, len(parts), 2)]
    return parts[0]


def plane_parts(array):
    pair = array + swap(array, "ha", 1)
    return [pair] + [swap(pair, "ha", k) for k in range(2, lax.axis_size("ha"), 2)]


def plane_sum(array, groups):
    total = tree_sum(plane_parts(array))
    bits = 1
    while bits < groups:
        total = total + swap(total, "wa", bits)
        bits *= 2
    return total


def take(array, index):
    return lax.dynamic_index_in_dim(array, index, 0, keepdims=False)


def by_distance(array):
    h = lax.axis_index("ha")
    return jnp.stack([take(array, h ^ k) for k in range(array.shape[0])])


def spread_chunks(even, odd):
    other = swap(odd, "ha", 1)
    both = [even[q].astype(F32) + other[q].astype(F32) for q in range(even.shape[0])]
    return both[:1] + [swap(both[q].astype(BF16), "ha", 2 * q) for q in range(1, len(both))]


def sum_chunks(parts, groups):
    total = tree_sum([part.astype(F32) for part in parts])
    bits = 1
    while bits < groups:
        total = total + swap(total.astype(BF16), "wa", bits).astype(F32)
        bits *= 2
    return total


def reduce_square(even, odd):
    other = swap(odd, "ha", 1)
    half = even.shape[1] // 2
    low = even[:, :half].astype(F32) + other[:, :half].astype(F32)
    high = even[:, half:].astype(F32) + other[:, half:].astype(F32)
    low_got = swap(low[1::2].astype(BF16), "ha", 2)
    high_got = swap(high[2:].astype(BF16), "ha", 4)
    low_last = swap((low[2] + low_got[1].astype(F32)).astype(BF16), "ha", 4)
    high_last = swap((high[1] + high_got[1].astype(F32)).astype(BF16), "ha", 2)
    return low[0], low_got, low_last, high[0], high_got, high_last


def gather_square(chunk):
    half = chunk.shape[0] // 2
    low, high = chunk[:half], chunk[half:]
    low_one = swap(low, "ha", 2)
    high_one = swap(high, "ha", 4)
    low_two = swap(jnp.stack([low, low_one]), "ha", 4)
    high_two = swap(jnp.stack([high, high_one]), "ha", 2)
    near = [chunk, low_one, high_one, low_two, high_two]
    return near + [swap(piece, "ha", 1) for piece in near]


def piece_of(k, branch, branches):
    q, half = k // 2, branches // 2
    first = 5 * (k % 2)
    low = branch < half
    inner = branch if low else branch - half
    if q == 0:
        return first, (branch,)
    if q == (1 if low else 2):
        return first + (1 if low else 2), (inner,)
    return first + (3 if low else 4), (int(q == 3), inner)


def gather_near(chunk):
    return [chunk] + [swap(chunk, "ha", 2 * q) for q in range(1, lax.axis_size("ha") // 2)]


def gather_chunks(chunk):
    near = jnp.stack(gather_near(chunk))
    return near, swap(near, "ha", 1)


def in_order(near, far):
    every = jnp.stack([near, far], axis=1)
    return by_distance(every.reshape((2 * near.shape[0],) + near.shape[1:]))


def gather_columns(own):
    gathered = lax.all_gather(own, "wa", axis=0, tiled=False)
    planes, count, few, rows = gathered.shape
    return gathered.swapaxes(0, 1).reshape(count, planes * few, rows)


def neighbour(array, pairs):
    return lax.ppermute(array, "wa", pairs)


def gather_early(own, others):
    right = neighbour(own, [(0, 1), (1, 2), (2, 3)])
    left = neighbour(own, [(1, 0), (2, 1), (3, 2)])
    right_two = neighbour(after(right, others), [(2, 3)])
    left_two = neighbour(after(left, others), [(1, 0), (2, 1)])
    return right, left, right_two, left_two


def gather_late(own, early, *others):
    z = lax.axis_index("wa")
    right, left, right_two, left_two = early
    left_three = neighbour(left_two, [(1, 0)])
    last_two = neighbour(after(right, *others), [(1, 2)])
    last_three = neighbour(last_two, [(2, 3)])
    found = [
        lax.select_n(z, own, right, last_two, last_three),
        lax.select_n(z, left, own, right, right_two),
        lax.select_n(z, left_two, left, own, right),
        lax.select_n(z, left_three, left_two, left, own),
    ]
    return jnp.concatenate(found, axis=1)


def exchange_sum(parts):
    z = lax.axis_index("wa")
    got = [swap(take(parts, z ^ k), "wa", k) for k in range(1, lax.axis_size("wa"))]
    return tree_sum([take(parts, z)] + got)


def line_scatter(parts):
    return lax.psum_scatter(parts, "wa", scatter_dimension=0, tiled=False).astype(F32)


def live_taps(rate, valid):
    return [(a, b) for a in (-1, 0, 1) for b in (-1, 0, 1) if b == 0 or valid > rate]


def span(b, rate, valid):
    return max(0, -b * rate), min(valid, valid - b * rate)


def moves(taps):
    return sorted({a for a, b in taps})


def forward_plain(x, shift, weights, rate, taps):
    valid = x.shape[0]
    moved = {
        a: x if a == 0 else jnp.einsum("pq,wqk->wpk", shift[(a + 1) // 2], x) for a in moves(taps)
    }
    out = jnp.zeros(x.shape[:2] + (weights.shape[1],), F32)
    for t, (a, b) in enumerate(taps):
        low, high = span(b, rate, valid)
        part = jnp.einsum(
            "wpk,ek->wpe", moved[a][low + b * rate : high + b * rate], weights[t], preferred_element_type=F32
        )
        out = out.at[low:high].add(part)
    return out


def backward_plain(x, shift, weights, rate, taps, grad, total):
    valid = x.shape[0]
    moved = {
        a: grad if a == 0 else jnp.einsum("pq,wqe->wpe", shift[(1 - a) // 2], grad)
        for a in moves(taps)
    }
    weight_grads = []
    for t, (a, b) in enumerate(taps):
        low, high = span(b, rate, valid)
        d = moved[a][low:high]
        source = slice(low + b * rate, high + b * rate)
        weight_grads.append(jnp.einsum("wpe,wpk->ek", d, x[source], preferred_element_type=F32))
        total = total.at[source].add(
            jnp.einsum("wpe,ek->wpk", d, weights[t], preferred_element_type=F32)
        )
    return jnp.stack(weight_grads), total


def dot(left, right, dims):
    return lax.dot_general(left, right, ((dims[0], dims[1]), ((), ())), preferred_element_type=F32)


NN = ((1,), (0,))
NT = ((1,), (1,))
TN = ((0,), (0,))
WHOLE = pl.BlockSpec(memory_space=pltpu.VMEM)
SCALAR = pl.BlockSpec(memory_space=pltpu.SMEM)
NO_COST = pl.CostEstimate(flops=0, bytes_accessed=0, transcendentals=0)
WIDE = pltpu.CompilerParams(vmem_limit_bytes=60 * 1024 * 1024)
PARAMS = pltpu.CompilerParams(vmem_limit_bytes=32 * 1024 * 1024)


def ceil_to(n, step):
    return -(-n // step) * step


def pack_weights(w_one, dilated, w_pool, w_proj, taps):
    rows, deep = w_one.shape
    order = [(j, 3 * (a + 1) + b + 1) for j in range(3) for a, b in taps[j]]

    def kernel(one_ref, dilated_ref, pool_ref, proj_ref, out_ref):
        out_ref[0] = one_ref[...]
        for at, (j, t) in enumerate(order):
            out_ref[at + 1] = dilated_ref[j, t]
        out_ref[len(order) + 1] = pool_ref[...]
        out_ref[len(order) + 2] = proj_ref[...]

    return pl.pallas_call(
        kernel,
        out_shape=jax.ShapeDtypeStruct((len(order) + 3, rows, deep), BF16),
        in_specs=[WHOLE] * 4,
        out_specs=WHOLE,
        compiler_params=PARAMS,
        name="pack_weights",
    )(w_one, dilated, w_pool, w_proj)


def spots_of(wanted, held):
    return ((wanted[:, None] == held[None, :]) & (wanted >= 0)[:, None]).astype(BF16)


def block_rows(count, tall, rows, cols, valid, pitch):
    row = np.arange(count)
    column = row // tall * cols + row % tall % cols
    real = (row % tall < rows * cols) & (column < valid)
    return np.where(real, column * pitch + row % tall // cols, -1)


def padded_rows(count, valid, prows, rows):
    row = np.arange(count)
    real = (row < valid * prows) & (row % prows < rows)
    return np.where(real, row // prows * rows + row % prows, -1)


def extract(features, cotangent, z):
    rows, cols, micro, channels = features.shape
    out = cotangent.shape[-1]
    size = rows * cols
    steps = channels // out

    def kernel(z_ref, f_ref, c_ref, *refs):
        outs, held_ref = refs[:-1], refs[-1]

        def put(ref):
            values = ref[...]
            for m in range(micro):
                held_ref[m] = values[:, m, :].astype(F32)
            for k in range(micro):
                outs[k][...] = held_ref[z_ref[0] ^ k].astype(BF16)

        @pl.when(pl.program_id(0) < steps)
        def _():
            put(f_ref)

        @pl.when(pl.program_id(0) == steps)
        def _():
            put(c_ref)

    return pl.pallas_call(
        kernel,
        grid=(steps + 1,),
        out_shape=[jax.ShapeDtypeStruct((size, channels + out), BF16)] * micro,
        in_specs=[
            SCALAR,
            pl.BlockSpec((size, micro, out), lambda i: (0, 0, jnp.minimum(i, steps - 1))),
            pl.BlockSpec((size, micro, out), lambda i: (0, 0, 0)),
        ],
        out_specs=[pl.BlockSpec((size, out), lambda i: (0, i))] * micro,
        scratch_shapes=[pltpu.VMEM((micro, size, out), F32)],
        compiler_params=PARAMS,
        name="extract",
    )(z.reshape(1), features.reshape(size, micro, channels), cotangent.reshape(size, micro, out))


def choose(slots, z, blocks, spots, last_spots, lanes):
    size, wide = slots[0].shape
    tall = ceil_to(size, 16)
    high = spots.shape[1]
    count = wide // lanes - 1

    def kernel(z_ref, *refs):
        spots_ref, last_ref, send_ref, own_ref, held_ref = refs[len(slots) :]
        held_ref[...] = jnp.zeros((high, wide), BF16)
        for v in range(len(slots)):

            @pl.when(z_ref[0] == v)
            def _():
                for j in range(blocks):
                    held_ref[j * tall : j * tall + size] = refs[v ^ j][...]

        for d in range(count):
            part = held_ref[:, d * lanes : (d + 1) * lanes]
            send_ref[d] = dot(spots_ref[...], part, NN).astype(BF16)
        own_ref[...] = dot(last_ref[...], held_ref[:, count * lanes :], NN).astype(BF16)

    return pl.pallas_call(
        kernel,
        out_shape=[
            jax.ShapeDtypeStruct((count, spots.shape[0], lanes), BF16),
            jax.ShapeDtypeStruct((last_spots.shape[0], lanes), BF16),
        ],
        in_specs=[SCALAR] + [WHOLE] * (len(slots) + 2),
        out_specs=[WHOLE] * 2,
        scratch_shapes=[pltpu.VMEM((high, wide), BF16)],
        compiler_params=PARAMS,
        name="choose",
    )(z.reshape(1), *slots, spots, last_spots)


def unchoose(pieces, last, z, blocks, size, spots, last_spots):
    ha, fit, out = pieces.shape
    planes, tall, thick = spots.shape
    wide = (ha + 1) * out

    def kernel(z_ref, pieces_ref, last_ref, spots_ref, last_spots_ref, *refs):
        outs, held_ref = refs[:-1], refs[-1]
        held_ref[fit:] = jnp.zeros((thick - fit, ha * out), BF16)
        for d in range(ha):
            held_ref[:fit, d * out : (d + 1) * out] = pieces_ref[d]
        for v in range(planes):

            @pl.when(z_ref[0] == v)
            def _():
                for j in range(planes):
                    if j < blocks:
                        block = dot(spots_ref[j], held_ref[...], NN).astype(BF16)
                        outs[v ^ j][:, : ha * out] = block[:size]
                        block = dot(last_spots_ref[j], last_ref[...], NN).astype(BF16)
                        outs[v ^ j][:, ha * out :] = block[:size]
                    else:
                        outs[v ^ j][...] = jnp.zeros((size, wide), BF16)

    return pl.pallas_call(
        kernel,
        out_shape=[jax.ShapeDtypeStruct((size, wide), BF16)] * planes,
        in_specs=[SCALAR] + [WHOLE] * 4,
        out_specs=[WHOLE] * planes,
        scratch_shapes=[pltpu.VMEM((thick, ha * out), BF16)],
        compiler_params=PARAMS,
        name="unchoose",
    )(z.reshape(1), pieces, last, spots, last_spots)


def order_chunks(near, far, h, few):
    half, out, _ = near.shape

    def kernel(h_ref, near_ref, far_ref, out_ref):
        for k in range(2 * half):
            chunk = (far_ref if k % 2 else near_ref)[k // 2]
            at = pl.multiple_of((h_ref[0] ^ k) * few, 16)
            out_ref[pl.ds(at, few), :] = chunk.T[:few]

    return pl.pallas_call(
        kernel,
        out_shape=jax.ShapeDtypeStruct((2 * half * few, out), BF16),
        in_specs=[SCALAR, WHOLE, WHOLE],
        out_specs=WHOLE,
        compiler_params=PARAMS,
        cost_estimate=NO_COST,
        name="order_chunks",
    )(h.reshape(1), near, far)


def interleave(got, z, blocks, rows, cols, out, others):
    micro = len(got)
    size, channels = got[0].shape
    channels -= out
    lanes = 2 * out

    def kernel(z_ref, *refs):
        df_ref, act_ref = refs[-2:]

        def place(parts, to_ref):
            for v in range(micro):

                @pl.when(z_ref[0] == v)
                def _():
                    if v < blocks:
                        to_ref[...] = jnp.stack([parts[m ^ v][...] for m in range(micro)], axis=1)
                    else:
                        to_ref[...] = jnp.zeros(to_ref.shape, BF16)

        @pl.when(pl.program_id(0) == 0)
        def _():
            place(refs[micro : 2 * micro], act_ref)

        place(refs[:micro], df_ref)

    df, act = pl.pallas_call(
        kernel,
        grid=(channels // lanes,),
        out_shape=[jax.ShapeDtypeStruct((size, micro, n), BF16) for n in (channels, out)],
        in_specs=[SCALAR]
        + [pl.BlockSpec((size, lanes), lambda i: (0, i))] * micro
        + [pl.BlockSpec((size, out), lambda i: (0, channels // out))] * micro
        + [pl.BlockSpec(memory_space=pl.ANY)] * len(others),
        out_specs=[
            pl.BlockSpec((size, micro, lanes), lambda i: (0, 0, i)),
            pl.BlockSpec((size, micro, out), lambda i: (0, 0, 0)),
        ],
        compiler_params=PARAMS,
        name="interleave",
    )(z.reshape(1), *got, *got, *others)
    return [a.reshape(rows, cols, micro, -1).transpose(2, 0, 1, 3) for a in (df, act)]


def arrange(raw, place, h, valid, prows):
    ha, tall, deep = raw.shape
    high = place.shape[1]

    def kernel(h_ref, raw_ref, place_ref, x_ref, sum_ref, held_ref):
        held_ref[tall:] = jnp.zeros((high - tall, deep), BF16)
        for k in range(ha):
            held_ref[:tall] = raw_ref[h_ref[0] ^ k]
            block = dot(place_ref[...], held_ref[...], NN).reshape(valid, prows, deep)
            x_ref[:, k * prows : (k + 1) * prows, :] = block.astype(BF16)
            sum_ref[k * prows : (k + 1) * prows] = jnp.sum(block, axis=0)

    return pl.pallas_call(
        kernel,
        out_shape=[
            jax.ShapeDtypeStruct((valid, ha * prows, deep), BF16),
            jax.ShapeDtypeStruct((ha * prows, deep), F32),
        ],
        in_specs=[SCALAR, WHOLE, WHOLE],
        out_specs=[WHOLE, WHOLE],
        scratch_shapes=[pltpu.VMEM((high, deep), BF16)],
        compiler_params=PARAMS,
        name="arrange",
    )(h.reshape(1), raw, place)


def sides_of(taps):
    return sorted({b for a, b in taps}, key=abs)


def in_steps(low, high, step, body):
    whole = (high - low) // step
    if whole:

        def one(i, carry):
            body(low + i * step, step)
            return carry

        lax.fori_loop(0, whole, one, 0)
    if (high - low) % step:
        body(low + whole * step, (high - low) % step)


def forward_kernel(x, weights, group, prows):
    valid, pheight, deep = x.shape
    out = weights.shape[1]
    half = pheight // prows // 2
    operands, flops = [x, weights], 0
    for shift, first, rate, taps in group:
        operands += [] if shift is None else [shift]
        spans = [span(b, rate, valid) for a, b in taps]
        flops += 2 * pheight * deep * out * sum(high - low for low, high in spans)
    most = max(len(moves(g[3])) for g in group)
    most_sides = max(len(sides_of(g[3])) for g in group)

    def kernel(x_ref, w_ref, *refs):
        ins = list(refs[: len(operands) - 2])
        even_ref, odd_ref, moved_ref, wide_ref, sum_ref = refs[len(operands) - 2 :]
        for g, (shift, first, rate, taps) in enumerate(group):
            steps, sides = moves(taps), sides_of(taps)
            for i, b in enumerate(sides):
                for n, a in enumerate(steps):
                    wide_ref[i, :, n * deep : (n + 1) * deep] = w_ref[first + taps.index((a, b))]
            source_ref = x_ref
            if shift is not None:
                s_ref = ins.pop(0)
                source_ref = moved_ref

                def move(w, carry):
                    values = x_ref[w]
                    both = dot(s_ref[...].reshape(2 * pheight, pheight), values, NN).astype(BF16)
                    moved_ref[w, :, :deep] = both[:pheight]
                    moved_ref[w, :, deep : 2 * deep] = values
                    moved_ref[w, :, 2 * deep :] = both[pheight:]
                    return carry

                lax.fori_loop(0, valid, move, 0, unroll=True)

            for i, b in enumerate(sides):

                def columns(w, count):
                    values = source_ref[pl.ds(w + b * rate, count)].reshape(count * pheight, -1)
                    part = dot(values, wide_ref[i, :, : len(steps) * deep], NT)
                    part = part.reshape(count, pheight, out)
                    if b == 0:
                        sum_ref[pl.ds(w, count)] = part
                    else:
                        sum_ref[pl.ds(w, count)] += part

                in_steps(*span(b, rate, valid), 7, columns)

            def store(w, carry):
                at = pl.multiple_of(w * prows, prows)
                for k in range(2 * half):
                    to = odd_ref if k % 2 else even_ref
                    to[k // 2, g, pl.ds(at, prows), :] = sum_ref[w, k * prows : (k + 1) * prows].astype(BF16)
                return carry

            lax.fori_loop(0, valid, store, 0, unroll=True)

    shape = jax.ShapeDtypeStruct((half, len(group), valid * prows, out), BF16)
    return pl.pallas_call(
        kernel,
        out_shape=[shape] * 2,
        in_specs=[WHOLE] * len(operands),
        out_specs=[WHOLE] * 2,
        scratch_shapes=[
            pltpu.VMEM((valid, pheight, most * deep), BF16),
            pltpu.VMEM((most_sides, out, most * deep), BF16),
            pltpu.VMEM((valid, pheight, out), F32),
        ],
        compiler_params=PARAMS,
        cost_estimate=NO_COST,
        name="forward",
    )(*operands)


def loaded(operands):
    return [
        pl.BlockSpec(a.shape, lambda i, n=a.ndim: (0,) * n, pipeline_mode=pl.Buffered(1)) for a in operands
    ]


def build_moved(pieces, moved_ref, s_ref, g, branches, valid, ha, prows, out):
    middle = 0 if s_ref is None else out

    def move(w, carry):
        at = pl.multiple_of(w * prows, prows)
        for k in range(ha):
            piece, index = piece_of(k, g, branches)
            rows = slice(k * prows, (k + 1) * prows)
            moved_ref[w, rows, middle : middle + out] = pieces[piece][(*index, pl.ds(at, prows))]
        if s_ref is not None:
            held = moved_ref[w, :, out : 2 * out]
            both = dot(s_ref[...].reshape(2 * ha * prows, ha * prows), held, NN).astype(BF16)
            moved_ref[w, :, :out] = both[ha * prows :]
            moved_ref[w, :, 2 * out :] = both[: ha * prows]
        return carry

    lax.fori_loop(0, valid, move, 0, unroll=True)


def weights_backward(x, group, pieces, wa, prows):
    valid, pheight, deep = x.shape
    out = pieces[0].shape[-1]
    few, ha, branches = out // wa, pheight // prows, len(group)
    shifts = [g[0] for g in group if g[0] is not None]
    operands = [x, *shifts, *pieces]
    shape = wa, sum(len(g[3]) for g in group), few, deep
    most = max(len(moves(g[3])) for g in group)

    def kernel(x_ref, *refs):
        shift_refs = list(refs[: len(shifts)])
        piece_refs = refs[len(shifts) : len(operands) - 1]
        grad_ref, moved_ref = refs[len(operands) - 1 :]
        done = 0
        for g, (shift, first, rate, taps) in enumerate(group):
            steps = moves(taps)
            s_ref = None if shift is None else shift_refs.pop(0)
            build_moved(piece_refs, moved_ref, s_ref, g, branches, valid, ha, prows, out)
            wide = len(steps) * out
            for b in sides_of(taps):
                low, high = span(b, rate, valid)
                left = moved_ref[low:high, :, :wide].reshape((high - low) * pheight, wide)
                right = x_ref[low + b * rate : high + b * rate].reshape((high - low) * pheight, deep)
                part = dot(left, right, TN).astype(BF16)
                for n, a in enumerate(steps):
                    t = done + taps.index((a, b))
                    for j in range(wa):
                        at = n * out + j * few
                        grad_ref[j, t] = part[at : at + few]
            done += len(taps)

    return pl.pallas_call(
        kernel,
        out_shape=jax.ShapeDtypeStruct(shape, BF16),
        grid=(1,),
        in_specs=loaded(operands),
        out_specs=pl.BlockSpec(shape, lambda i: (0, 0, 0, 0)),
        scratch_shapes=[pltpu.VMEM((valid, pheight, most * out), BF16)],
        compiler_params=WIDE,
        cost_estimate=NO_COST,
        name="weights_backward",
    )(*operands)


def features_backward(x, weights, group, pieces, start, h, place, fit, prows):
    valid, pheight, deep = x.shape
    out = weights.shape[1]
    ha, branches = pheight // prows, len(group)
    shifts = [g[0] for g in group if g[0] is not None]
    operands = [h.reshape(1), start, weights, place, *shifts, *pieces]
    high = place.shape[1]
    most = max(len(moves(g[3])) for g in group)
    most_sides = max(len(sides_of(g[3])) for g in group)

    def kernel(h_ref, start_ref, w_ref, place_ref, *refs):
        shift_refs = list(refs[: len(shifts)])
        piece_refs = refs[len(shifts) : len(operands) - 4]
        last_ref, moved_ref, wide_ref, total_ref, held_ref = refs[len(operands) - 4 :]
        for g, (shift, first, rate, taps) in enumerate(group):
            steps, sides = moves(taps), sides_of(taps)
            s_ref = None if shift is None else shift_refs.pop(0)
            build_moved(piece_refs, moved_ref, s_ref, g, branches, valid, ha, prows, out)
            for i, b in enumerate(sides):
                for n, a in enumerate(steps):
                    wide_ref[i, n * out : (n + 1) * out] = w_ref[first + taps.index((a, b))]
            wide = len(steps) * out
            for i, b in enumerate(sides):

                def columns(w, count):
                    values = moved_ref[pl.ds(w - b * rate, count), :, :wide].reshape(count * pheight, wide)
                    part = dot(values, wide_ref[i, :wide], NN).reshape(count, pheight, deep)
                    if g or b != 0:
                        total_ref[pl.ds(w, count)] += part
                    else:
                        total_ref[pl.ds(w, count)] = part + start_ref[...][None]

                in_steps(*span(-b, rate, valid), 4, columns)
        held_ref[valid * prows :] = jnp.zeros((high - valid * prows, deep), BF16)
        for k in range(ha):
            block = total_ref[:, k * prows : (k + 1) * prows, :].astype(BF16)
            held_ref[: valid * prows] = block.reshape(valid * prows, deep)
            last_ref[h_ref[0] ^ k] = dot(place_ref[...], held_ref[...], NN).astype(BF16)

    return pl.pallas_call(
        kernel,
        out_shape=jax.ShapeDtypeStruct((ha, fit, deep), BF16),
        grid=(1,),
        in_specs=[SCALAR] + loaded(operands[1:]),
        out_specs=pl.BlockSpec((ha, fit, deep), lambda i: (0, 0, 0)),
        scratch_shapes=[
            pltpu.VMEM((valid, pheight, most * out), BF16),
            pltpu.VMEM((most_sides, most * out, deep), BF16),
            pltpu.VMEM(x.shape, F32),
            pltpu.VMEM((high, deep), BF16),
        ],
        compiler_params=WIDE,
        cost_estimate=NO_COST,
        name="features_backward",
    )(*operands)


def real_rows(pixels, prows, rows):
    return (lax.broadcasted_iota(jnp.int32, (pixels, 1), 0) % prows < rows).astype(F32)


def total_of(refs):
    return tree_sum([r[...] for r in refs])


def column_sum(values):
    return jnp.sum(values, axis=0, keepdims=True)


def small_kernel(kernel, name, operands, shapes):
    return pl.pallas_call(
        kernel,
        out_shape=[jax.ShapeDtypeStruct(s, t) for s, t in shapes],
        in_specs=[WHOLE] * len(operands),
        out_specs=[WHOLE] * len(shapes),
        compiler_params=PARAMS,
        cost_estimate=NO_COST,
        name=name,
    )(*operands)


def branch_sums(parts, pool_part):
    _, pixels, out = parts[0].shape
    images = pool_part.shape[0]

    def kernel(low, low_got, low_last, high, high_got, high_last, pool_ref, branch_ref, sum_ref):
        for j in range(4):
            own, got, last = (low, low_got, low_last) if j < 2 else (high, high_got, high_last)
            value = own[j % 2] + got[0, j % 2].astype(F32) + last[j % 2].astype(F32)
            branch_ref[j] = value
            sum_ref[j : j + 1] = column_sum(value)
            sum_ref[4 + j : 5 + j] = column_sum(value * value)
        sum_ref[8:] = pool_ref[...]

    shapes = [((4, pixels, out), F32), ((8 + images, out), F32)]
    return small_kernel(kernel, "branch_sums", [*parts, pool_part], shapes)


def project(sums, branch, scales, shifts, counts, own, proj, rows, pixel_total):
    _, pixels, out = branch.shape
    images = counts.shape[0]
    prows = own.shape[0]
    many = len(sums)

    def kernel(*refs):
        branch_ref, scale_ref, shift_ref, count_ref, own_ref, proj_ref = refs[many : many + 6]
        joined_ref, projected_ref, second_ref, stat_ref, pool_ref = refs[many + 6 :]
        total = total_of(refs[:many])
        mean = total[0:4] / pixel_total
        rstd = lax.rsqrt(total[4:8] / pixel_total - mean * mean + EPS)
        stat_ref[0:4] = mean
        stat_ref[4:8] = rstd
        scale, shift = scale_ref[...], shift_ref[...]
        for j in range(4):
            norm = (branch_ref[j] - mean[j : j + 1]) * rstd[j : j + 1]
            hid = norm * scale[j : j + 1] + shift[j : j + 1]
            joined_ref[:, j * out : (j + 1) * out] = silu(hid).astype(BF16)
        pool_out = total[8:]
        weighted = count_ref[...]
        pool_mean = column_sum(weighted * pool_out) / pixel_total
        pool_second = column_sum(weighted * pool_out * pool_out) / pixel_total
        pool_rstd = lax.rsqrt(pool_second - pool_mean * pool_mean + EPS)
        pool_norm = (pool_out - pool_mean) * pool_rstd
        pool_hid = pool_norm * scale[4:5] + shift[4:5]
        pool_ref[0] = pool_norm
        pool_ref[1] = pool_hid
        pool_ref[2] = jnp.broadcast_to(pool_rstd, pool_out.shape)
        pool_act = silu(pool_hid)
        spread = jnp.zeros((prows, out), F32)
        for i in range(images):
            spread = spread + own_ref[:, i : i + 1] * pool_act[i : i + 1]
        spread = spread.astype(BF16)
        for w in range(pixels // prows):
            joined_ref[w * prows : (w + 1) * prows, 4 * out :] = spread
        projected = dot(joined_ref[...], proj_ref[...], NN)
        projected_ref[...] = projected
        held = projected * real_rows(pixels, prows, rows)
        second_ref[...] = jnp.zeros(second_ref.shape, F32)
        second_ref[0:1] = column_sum(held)
        second_ref[1:2] = column_sum(held * held)

    shapes = [((pixels, 5 * out), BF16), ((pixels, out), F32), ((8, out), F32), ((8, out), F32), ((3, images, out), F32)]
    return small_kernel(kernel, "project", [*sums, branch, scales, shifts, counts, own, proj], shapes)


def activate(sums, projected, cot, out_scale, out_shift, prows, rows, pixel_total):
    pixels, out = projected.shape
    many = len(sums)

    def kernel(*refs):
        projected_ref, cot_ref, scale_ref, shift_ref = refs[many : many + 4]
        act_ref, norm_ref, dhid_ref, third_ref, rstd_ref = refs[many + 4 :]
        total = total_of(refs[:many])
        mean = total[0:1] / pixel_total
        rstd = lax.rsqrt(total[1:2] / pixel_total - mean * mean + EPS)
        rstd_ref[...] = jnp.broadcast_to(rstd, rstd_ref.shape)
        norm = (projected_ref[...] - mean) * rstd
        norm_ref[...] = norm
        hid = norm * scale_ref[...] + shift_ref[...]
        act_ref[...] = silu(hid).astype(BF16)
        dhid = cot_ref[...].astype(F32) * real_rows(pixels, prows, rows) * silu_slope(hid)
        dhid_ref[...] = dhid
        third_ref[...] = jnp.zeros(third_ref.shape, F32)
        third_ref[0:1] = column_sum(dhid)
        third_ref[1:2] = column_sum(dhid * norm)

    shapes = [((pixels, out), BF16), ((pixels, out), F32), ((pixels, out), F32), ((8, out), F32), ((8, out), F32)]
    operands = [*sums, projected, cot, out_scale[None], out_shift[None]]
    return small_kernel(kernel, "activate", operands, shapes)


def unproject(sums, norm, dhid, rstd, out_scale, proj, joined, branch, stats, scales, shifts, own, ha, rows, pixel_total):
    _, pixels, out = branch.shape
    prows, images = own.shape
    many = len(sums)

    def kernel(*refs):
        norm_ref, dhid_ref, rstd_ref, oscale_ref, proj_ref, joined_ref = refs[many : many + 6]
        branch_ref, stat_ref, scale_ref, shift_ref, own_ref = refs[many + 6 : many + 11]
        third_ref, grad_ref, back_ref, fourth_ref = refs[many + 11 :]
        total = total_of(refs[:many])
        third_ref[...] = total
        mask = real_rows(pixels, prows, rows)
        dproj = dhid_ref[...] - (total[0:1] + norm_ref[...] * total[1:2]) / pixel_total
        dproj = (oscale_ref[...] * rstd_ref[0:1] * dproj * mask).astype(BF16)
        grad = dot(joined_ref[...], dproj, TN)
        grad_ref[...] = jnp.zeros(grad_ref.shape, BF16)
        few = 5 * out // ha
        for d in range(ha):
            grad_ref[d, :, :few] = grad[d * few : (d + 1) * few].T.astype(BF16)
        for j in range(5):
            dact = dot(dproj, proj_ref[j * out : (j + 1) * out], NT)
            if j < 4:
                branch_norm = (branch_ref[j] - stat_ref[j : j + 1]) * stat_ref[4 + j : 5 + j]
                hid = branch_norm * scale_ref[j : j + 1] + shift_ref[j : j + 1]
                back = dact * silu_slope(hid) * mask
                back_ref[j] = back
                fourth_ref[j : j + 1] = column_sum(back)
                fourth_ref[4 + j : 5 + j] = column_sum(back * branch_norm)
            else:
                across = jnp.sum(dact.reshape(pixels // prows, prows, out), axis=0)
                for i in range(images):
                    fourth_ref[8 + i : 9 + i] = column_sum(own_ref[:, i : i + 1] * across)

    shapes = [((8, out), F32), ((ha, out, out), BF16), ((4, pixels, out), F32), ((8 + images, out), F32)]
    operands = [*sums, norm, dhid, rstd, out_scale[None], proj, joined, branch, stats, scales, shifts, own]
    return small_kernel(kernel, "unproject", operands, shapes)


def branch_gradients(sums, back, branch, stats, scales, counts, pool, prows, rows, pixel_total):
    _, pixels, out = branch.shape
    images = counts.shape[0]
    many = len(sums)

    def kernel(*refs):
        back_ref, branch_ref, stat_ref, scale_ref, count_ref, pool_ref = refs[many : many + 6]
        grad_ref, dpool_ref, sum_ref = refs[many + 6 :]
        total = total_of(refs[:many])
        mask = real_rows(pixels, prows, rows)
        for j in range(4):
            rstd = stat_ref[4 + j : 5 + j]
            norm = (branch_ref[j] - stat_ref[j : j + 1]) * rstd
            value = back_ref[j] - (total[j : j + 1] + norm * total[4 + j : 5 + j]) / pixel_total
            grad_ref[j] = (scale_ref[j : j + 1] * rstd * value * mask).astype(BF16)
        dhid = silu_slope(pool_ref[1]) * total[8:]
        pool_shift = column_sum(dhid)
        pool_scale = column_sum(dhid * pool_ref[0])
        value = dhid - count_ref[...] * (pool_shift + pool_ref[0] * pool_scale) / pixel_total
        dpool_ref[...] = (scale_ref[4:5] * pool_ref[2] * value).astype(BF16)
        sum_ref[...] = jnp.zeros(sum_ref.shape, F32)
        sum_ref[0:4] = total[4:8]
        sum_ref[4:5] = pool_scale
        sum_ref[5:9] = total[0:4]
        sum_ref[9:10] = pool_shift

    shapes = [((4, pixels, out), BF16), ((images, out), BF16), ((16, out), F32)]
    operands = [*sums, back, branch, stats, scales, counts, pool]
    return small_kernel(kernel, "branch_gradients", operands, shapes)


def local(
    features,
    row_image,
    cotangent,
    w_one,
    dilated_weight,
    w_pool,
    w_proj,
    scales,
    shifts,
    out_scale,
    out_shift,
):
    micro, rows, cols, channels = features.shape
    ha, wa = lax.axis_size("ha"), lax.axis_size("wa")
    h, z = lax.axis_index("ha"), lax.axis_index("wa")
    planes = wa // micro
    batch, part = z // planes, z % planes
    deep = w_one.shape[0] // planes
    out = w_one.shape[1] * wa
    valid = cols * wa - PADC
    blocks = -(-valid // cols)
    prows = -(-rows // 16) * 16
    height, pheight = rows * ha, prows * ha
    images = IMG_DEV * ha
    pixels = float(height * valid)
    size = cols * rows

    fast = planes == 1 and wa == 4 and 6 * valid * pheight * out < (16 << 20) and channels % out == 0 and deep == out

    taps = [live_taps(r, valid) for r in RATES]
    few = w_proj.shape[0]
    side = jnp.pad(w_proj.T, ((0, 0), (0, w_one.shape[0] - few)))
    turned = dilated_weight.swapaxes(2, 3)
    if fast:
        weights = pack_weights(w_one.T, turned, w_pool.T, side, taps)
    else:
        picked = [turned[j, 3 * (a + 1) + b + 1] for j in range(3) for a, b in taps[j]]
        weights = gather_columns(jnp.stack([w_one.T, *picked, w_pool.T, side]))

    if fast:
        slots = extract(features.transpose(1, 2, 0, 3), cotangent.transpose(1, 2, 0, 3), z)
        tall, fit = ceil_to(size, 16), ceil_to(valid * rows, 16)
        slots = [slots[0]] + [swap(slots[k], "wa", k, lambda i: i < blocks) for k in range(1, wa)]
        early = gather_early(weights, slots[1])
        high, thick = ceil_to(blocks * tall, 128), ceil_to(fit, 128)
        in_piece = block_rows(high, tall, rows, cols, valid, rows)
        in_chunk = block_rows(high, tall, rows, cols, valid, prows)
        spots = spots_of(np.arange(fit), in_piece)
        cot_spots = spots_of(np.arange(valid * prows), in_chunk)
        send, cot = choose(slots, z, blocks, spots, cot_spots, deep)
        raw = lax.all_to_all(send, "ha", 0, 0, tiled=True)
    else:
        f = features.transpose(0, 2, 1, 3).reshape(micro, size, ha, planes, deep)
        f = f.transpose(0, 3, 1, 2, 4).reshape(wa, size, ha * deep)
        c = cotangent.transpose(0, 2, 1, 3).reshape(micro, size, out)
        load = jnp.concatenate([f, jnp.repeat(c, planes, axis=0)], axis=-1)
        slots = [take(load, z)]
        for k in range(1, wa):
            slots.append(swap(take(load, z ^ k), "wa", k, lambda i: i < blocks))
        slots = jnp.stack(slots)
        block = jnp.concatenate([take(slots, z ^ j) for j in range(blocks)])[: valid * rows]
        raw = block[:, : ha * deep].reshape(valid * rows, ha, deep).swapaxes(0, 1)
        raw = lax.all_to_all(raw, "ha", 0, 0, tiled=True)
        cot = block[:, ha * deep :].reshape(valid, rows, out)
        cot = jnp.pad(cot, ((0, 0), (0, prows - rows), (0, 0))).reshape(valid * prows, out)
    if fast:
        weights = gather_late(weights, early, *slots)
    if fast:
        proj = order_chunks(*gather_chunks(weights[-1]), h, few)
    else:
        proj = in_order(*gather_chunks(weights[-1]))[..., :few].swapaxes(1, 2).reshape(ha * few, out)
    if planes > 1:
        weights = lax.dynamic_slice_in_dim(weights, part * deep, deep, 2)
    wide_pool = weights[-2]

    order = h ^ jnp.arange(ha, dtype=jnp.int32)
    labels = by_distance(take(row_image, batch).reshape(ha, rows))
    number = order[:, None] * rows + jnp.arange(rows, dtype=jnp.int32)[None, :]
    pad = ((0, 0), (0, prows - rows))
    labels = jnp.pad(labels, pad, constant_values=-1).reshape(pheight)
    number = jnp.pad(number, pad, constant_values=-(1 << 20)).reshape(pheight)
    same = (labels[:, None] == labels[None, :]) & (labels >= 0)[:, None]
    apart = number[None, :] - number[:, None]
    shift = [
        jnp.stack([(same & (apart == a * r)).astype(BF16) for a in (-1, 1)]) for r in RATES
    ]
    ids = jnp.arange(images, dtype=jnp.int32)
    member = (labels[:, None] == ids[None, :]).astype(F32)
    counts = jnp.sum(member, axis=0) * valid
    own = member[:prows]
    mask = jnp.tile(jnp.sum(own, axis=1), valid)[:, None]

    ahead = [1, 1 + len(taps[0]), 1 + len(taps[0]) + len(taps[1])]
    group = [(None, 0, 0, [(0, 0)])] + [(shift[j], ahead[j], RATES[j], taps[j]) for j in range(3)]
    if fast:
        place = spots_of(padded_rows(valid * prows, valid, prows, rows), np.arange(thick))
        x, row_sums = arrange(raw, place, h, valid, prows)
        unplace = spots_of(np.arange(fit), padded_rows(ceil_to(valid * prows, 128), valid, prows, rows))
    else:
        x = by_distance(raw).reshape(ha, valid, rows, deep)
        x = jnp.pad(x, ((0, 0), (0, 0), (0, prows - rows), (0, 0)))
        x = x.swapaxes(0, 1).reshape(valid, pheight, deep)
        row_sums = jnp.sum(x.astype(F32), axis=0)
    if fast:
        branch_parts = reduce_square(*forward_kernel(x, weights, group, prows))
    else:
        sums = jnp.stack([forward_plain(x, s, weights[n : n + len(t)], r, t) for s, n, r, t in group])
        sums = sums.astype(BF16).reshape(len(group), valid, ha // 2, 2, prows, out)
        sums = sums.transpose(3, 2, 0, 1, 4, 5).reshape(2, ha // 2, len(group), valid * prows, out)
        branch = sum_chunks(spread_chunks(sums[0], sums[1]), planes)
    pooled = (jnp.dot(member.T, row_sums, precision=HIGHEST) / counts[:, None]).astype(BF16)
    pool_part = dot(pooled, wide_pool, NT)

    weighted = counts[:, None]
    once = (part == 0).astype(F32)
    if fast:
        branch, first = branch_sums(branch_parts, pool_part)
        joined, projected, second, stats, pool = project(
            plane_parts(first), branch, scales, shifts, weighted, own, proj, rows, pixels
        )
        activation, proj_norm, dproj_hid, third, proj_rstd = activate(
            plane_parts(second), projected, cot, out_scale, out_shift, prows, rows, pixels
        )
        third, grad_proj, dhid, fourth = unproject(
            plane_parts(third),
            proj_norm,
            dproj_hid,
            proj_rstd,
            out_scale,
            proj,
            joined,
            branch,
            stats,
            scales,
            shifts,
            own,
            ha,
            rows,
            pixels,
        )
        dbranch, dpool, sums = branch_gradients(
            plane_parts(fourth), dhid, branch, stats, scales, weighted, pool, prows, rows, pixels
        )
        sums = jnp.concatenate([sums[:10], third[:2]])
    else:
        first = plane_sum(
            jnp.concatenate(
                [once * jnp.sum(branch, axis=1), once * jnp.sum(branch * branch, axis=1), pool_part]
            ),
            planes,
        )
        mean = first[0:4] / pixels
        rstd = lax.rsqrt(first[4:8] / pixels - mean * mean + EPS)
        pool_out = first[8:]
        norm = (branch - mean[:, None]) * rstd[:, None]
        hid = norm * scales[:4, None] + shifts[:4, None]
        act = silu(hid)
        weighted = counts[:, None]
        pool_mean = jnp.sum(weighted * pool_out, axis=0) / pixels
        pool_second = jnp.sum(weighted * pool_out * pool_out, axis=0) / pixels
        pool_rstd = lax.rsqrt(pool_second - pool_mean * pool_mean + EPS)
        pool_norm = (pool_out - pool_mean) * pool_rstd
        pool_hid = pool_norm * scales[4] + shifts[4]
        spread = jnp.dot(own, silu(pool_hid), precision=HIGHEST)
        spread = jnp.broadcast_to(spread[None], (valid, prows, out)).reshape(valid * prows, out)
        joined = jnp.concatenate([act[0], act[1], act[2], act[3], spread], axis=-1).astype(BF16)
        projected = jnp.dot(joined, proj, preferred_element_type=F32)

        held = projected * mask
        second = plane_sum(
            jnp.stack([jnp.sum(held, axis=0), jnp.sum(held * held, axis=0)]) * once, planes
        )
        proj_mean = second[0] / pixels
        proj_rstd = lax.rsqrt(second[1] / pixels - proj_mean * proj_mean + EPS)
        proj_norm = (projected - proj_mean) * proj_rstd
        proj_hid = proj_norm * out_scale + out_shift
        activation = silu(proj_hid).astype(BF16)
        dproj_hid = cot.astype(F32) * mask * silu_slope(proj_hid)
        third = plane_sum(
            jnp.stack([jnp.sum(dproj_hid, axis=0), jnp.sum(dproj_hid * proj_norm, axis=0)]) * once, planes
        )
        dproj = (
            out_scale * proj_rstd * (dproj_hid - (third[0] + proj_norm * third[1]) / pixels) * mask
        ).astype(BF16)
        djoined = lax.dot_general(dproj, proj, (((1,), (1,)), ((), ())), preferred_element_type=F32)
        grad_proj = dot(dproj, joined, TN)
        dact = jnp.stack([djoined[:, j * out : (j + 1) * out] for j in range(4)])
        dspread = jnp.sum(djoined[:, 4 * out :].reshape(valid, prows, out), axis=0)
        image_part = jnp.dot(own.T, dspread, precision=HIGHEST)
        dhid = dact * silu_slope(hid) * mask
        fourth = plane_sum(
            jnp.concatenate([jnp.sum(dhid, axis=1), jnp.sum(dhid * norm, axis=1), image_part]) * once,
            planes,
        )
        branch_shift, branch_scale, image_total = fourth[0:4], fourth[4:8], fourth[8:]
        dbranch = (
            (scales[:4] * rstd)[:, None]
            * (dhid - (branch_shift[:, None] + norm * branch_scale[:, None]) / pixels)
            * mask
        ).astype(BF16)
        dpool_hid = silu_slope(pool_hid) * image_total
        pool_shift = jnp.sum(dpool_hid, axis=0)
        pool_scale = jnp.sum(dpool_hid * pool_norm, axis=0)
        dpool = (
            scales[4] * pool_rstd * (dpool_hid - weighted * (pool_shift + pool_norm * pool_scale) / pixels)
        ).astype(BF16)
        sums = jnp.concatenate([branch_scale, pool_scale[None], branch_shift, pool_shift[None], third])
    grad_pool = dot(dpool, pooled, TN)
    dpooled = dot(dpool, wide_pool, NN)

    total = jnp.dot(member, dpooled / counts[:, None], precision=HIGHEST)
    if fast:
        pieces = gather_square(dbranch)
        tap_grads = weights_backward(x, group, pieces, wa, prows)
        back = features_backward(x, weights, group, pieces, total, h, unplace, fit, prows)
    else:
        total = jnp.broadcast_to(total[None], (valid,) + total.shape)
        near, far = gather_chunks(dbranch)
        every = jnp.stack([near, far], axis=1).reshape(ha, len(group), valid, prows, out)
        every = every.transpose(1, 2, 0, 3, 4).reshape(len(group), valid, pheight, out)
        found = []
        for (s, n, r, t), d in zip(group, every):
            grads, total = backward_plain(x, s, weights[n : n + len(t)], r, t, d, total)
            found.append(grads.reshape(len(t), wa, out // wa, deep).swapaxes(0, 1).astype(BF16))
        tap_grads = jnp.concatenate(found, axis=1)
        back = total.astype(BF16).reshape(valid, ha, prows, deep)[:, :, :rows]
        back = back.swapaxes(0, 1).reshape(ha, valid * rows, deep)
        back = by_distance(back)

    def in_place(grads):
        if planes == 1:
            return grads
        full = jnp.zeros(grads.shape[:-1] + (deep * planes,), grads.dtype)
        return lax.dynamic_update_slice_in_dim(full, grads, part * deep, grads.ndim - 1)

    if not fast:
        grad_proj = (grad_proj * once).reshape(out, ha, few).swapaxes(0, 1)
        grad_proj = jnp.pad(grad_proj, ((0, 0), (0, 0), (0, w_one.shape[0] - few))).astype(BF16)
    proj_chunk = lax.psum_scatter(grad_proj, "ha", scatter_dimension=0, tiled=False)
    grad_pool = in_place(grad_pool.astype(BF16)).reshape(wa, 1, out // wa, -1)
    proj_chunk = proj_chunk.reshape(wa, 1, out // wa, -1)
    tap_grads = line_scatter(in_place(tap_grads))
    rest = jnp.concatenate([grad_pool, proj_chunk], axis=1)
    if not fast:
        rest = line_scatter(rest)
    tap_out = [tap_grads[n : n + len(t)] for n, t in zip(ahead, taps)]
    blank = jnp.zeros((out // wa, w_one.shape[0]), F32)
    atrous = []
    for j in range(3):
        if len(taps[j]) == 9:
            atrous.append(tap_out[j])
        else:
            found = {3 * (a + 1) + b + 1: tap_out[j][t] for t, (a, b) in enumerate(taps[j])}
            atrous.append(jnp.stack([found.get(t, blank) for t in range(9)]))
    atrous = jnp.stack(atrous)
    atrous_out = atrous.swapaxes(2, 3)
    back = lax.all_to_all(back, "ha", 0, 0, tiled=True)

    def home(i, k):
        return i ^ k < blocks

    if fast:
        piece_spots = spots_of(block_rows(wa * tall, tall, rows, cols, valid, rows), np.arange(thick))
        chunk_spots = spots_of(block_rows(wa * tall, tall, rows, cols, valid, prows), np.arange(valid * prows))
        got = unchoose(
            back, activation, z, blocks, size, piece_spots.reshape(wa, tall, thick), chunk_spots.reshape(wa, tall, -1)
        )
        got = [got[0]] + [swap(got[k], "wa", k, partial(home, k=k)) for k in range(1, wa)]
        df, acts = interleave(got, z, blocks, rows, cols, out, [atrous])
        wide = jnp.broadcast_to(jnp.pad(sums, ((0, 4), (0, 0)))[None], (wa, 16, out))
        rest = jnp.concatenate([rest.astype(F32).reshape(wa, -1, out), wide], axis=1)
        rest = exchange_sum(rest)
        sums = rest[-16:-4]
        rest = rest[:-16].reshape(2, -1, out)
    else:

        def send_home(array):
            array = jnp.pad(array, ((0, wa * size - valid * rows), (0, 0))).reshape(wa, size, -1)
            got = [take(array, z)]
            got += [swap(take(array, z ^ k), "wa", k, partial(home, k=k)) for k in range(1, wa)]
            got = jnp.stack(got)
            got = jnp.where(z < blocks, got, jnp.zeros((), got.dtype))
            return jnp.stack([take(got, z ^ t) for t in range(wa)])

        back = back.swapaxes(0, 1).reshape(valid * rows, ha * deep)
        df = send_home(back).reshape(micro, planes, cols, rows, ha, deep)
        df = df.transpose(0, 3, 2, 4, 1, 5).reshape(features.shape)
        activation = activation.reshape(valid, prows, out)[:, :rows].reshape(valid * rows, out)
        acts = send_home(activation).reshape(micro, planes, cols, rows, out)[:, 0].swapaxes(1, 2)
    if not fast:
        sums = sums * once
        sums = tree_sum([sums] + [swap(sums, "wa", k) for k in range(1, wa)])
    one_out, pool_grad_out, proj_out = tap_grads[0].T, rest[0].T, rest[1][:, :few].T
    return (
        acts,
        df,
        one_out,
        atrous_out,
        pool_grad_out,
        proj_out,
        sums[0:5],
        sums[5:10],
        sums[11],
        sums[10],
    )


def solution(mesh):
    specs = (
        P(None, "ha", "wa", None),
        P(),
        P(None, "ha", "wa", None),
        P("ha", "wa"),
        P(None, None, "ha", "wa"),
        P("ha", "wa"),
        P("ha", "wa"),
        P(),
        P(),
        P(),
        P(),
    )
    out_specs = (
        P(None, "ha", "wa", None),
        P(None, "ha", "wa", None),
        P("ha", "wa"),
        P(None, None, "ha", "wa"),
        P("ha", "wa"),
        P("ha", "wa"),
        P(),
        P(),
        P(),
        P(),
    )
    return jax.shard_map(local, mesh=mesh, in_specs=specs, out_specs=out_specs, check_vma=False)
```

```python
from functools import partial

import jax
import jax.numpy as jnp
import numpy as np
from jax import lax
from jax.experimental import pallas as pl
from jax.experimental.pallas import tpu as pltpu
from jax.sharding import PartitionSpec as P

PADC = 7
IMG_DEV = 2
RATES = (6, 12, 18)
EPS = 1e-05
HIGHEST = lax.Precision.HIGHEST
F32 = jnp.float32
BF16 = jnp.bfloat16


def silu(u):
    return u * jax.nn.sigmoid(u)


def silu_slope(u):
    s = jax.nn.sigmoid(u)
    return s * (1.0 + u * (1.0 - s))


def swap(array, axis, bits, sources=None):
    count = lax.axis_size(axis)
    pairs = [(i, i ^ bits) for i in range(count) if sources is None or sources(i)]
    return lax.ppermute(array, axis, pairs)


def after(value, *others):
    return lax.optimization_barrier((value, *others))[0]


def tree_sum(parts):
    while len(parts) > 1:
        parts = [parts[i] + parts[i + 1] for i in range(0, len(parts), 2)]
    return parts[0]


def plane_parts(array):
    pair = array + swap(array, "ha", 1)
    return [pair] + [swap(pair, "ha", k) for k in range(2, lax.axis_size("ha"), 2)]


def plane_sum(array, groups):
    total = tree_sum(plane_parts(array))
    bits = 1
    while bits < groups:
        total = total + swap(total, "wa", bits)
        bits *= 2
    return total


def take(array, index):
    return lax.dynamic_index_in_dim(array, index, 0, keepdims=False)


def by_distance(array):
    h = lax.axis_index("ha")
    return jnp.stack([take(array, h ^ k) for k in range(array.shape[0])])


def spread_chunks(even, odd):
    other = swap(odd, "ha", 1)
    both = [even[q].astype(F32) + other[q].astype(F32) for q in range(even.shape[0])]
    return both[:1] + [swap(both[q].astype(BF16), "ha", 2 * q) for q in range(1, len(both))]


def sum_chunks(parts, groups):
    total = tree_sum([part.astype(F32) for part in parts])
    bits = 1
    while bits < groups:
        total = total + swap(total.astype(BF16), "wa", bits).astype(F32)
        bits *= 2
    return total


def reduce_square(even, odd):
    other = swap(odd, "ha", 1)
    half = even.shape[1] // 2
    low = even[:, :half].astype(F32) + other[:, :half].astype(F32)
    high = even[:, half:].astype(F32) + other[:, half:].astype(F32)
    low_got = swap(low[1::2].astype(BF16), "ha", 2)
    high_got = swap(high[2:].astype(BF16), "ha", 4)
    low_last = swap((low[2] + low_got[1].astype(F32)).astype(BF16), "ha", 4)
    high_last = swap((high[1] + high_got[1].astype(F32)).astype(BF16), "ha", 2)
    return low[0], low_got, low_last, high[0], high_got, high_last


def gather_square(chunk):
    half = chunk.shape[0] // 2
    low, high = chunk[:half], chunk[half:]
    low_one = swap(low, "ha", 2)
    high_one = swap(high, "ha", 4)
    low_two = swap(jnp.stack([low, low_one]), "ha", 4)
    high_two = swap(jnp.stack([high, high_one]), "ha", 2)
    near = [chunk, low_one, high_one, low_two, high_two]
    return near + [swap(piece, "ha", 1) for piece in near]


def piece_of(k, branch, branches):
    q, half = k // 2, branches // 2
    first = 5 * (k % 2)
    low = branch < half
    inner = branch if low else branch - half
    if q == 0:
        return first, (branch,)
    if q == (1 if low else 2):
        return first + (1 if low else 2), (inner,)
    return first + (3 if low else 4), (int(q == 3), inner)


def gather_near(chunk):
    return [chunk] + [swap(chunk, "ha", 2 * q) for q in range(1, lax.axis_size("ha") // 2)]


def gather_chunks(chunk):
    near = jnp.stack(gather_near(chunk))
    return near, swap(near, "ha", 1)


def in_order(near, far):
    every = jnp.stack([near, far], axis=1)
    return by_distance(every.reshape((2 * near.shape[0],) + near.shape[1:]))


def gather_columns(own):
    gathered = lax.all_gather(own, "wa", axis=0, tiled=False)
    planes, count, few, rows = gathered.shape
    return gathered.swapaxes(0, 1).reshape(count, planes * few, rows)


def neighbour(array, pairs):
    return lax.ppermute(array, "wa", pairs)


def gather_early(own, others):
    right = neighbour(own, [(0, 1), (1, 2), (2, 3)])
    left = neighbour(own, [(1, 0), (2, 1), (3, 2)])
    right_two = neighbour(after(right, others), [(2, 3)])
    left_two = neighbour(after(left, others), [(1, 0), (2, 1)])
    return right, left, right_two, left_two


def gather_late(own, early, *others):
    z = lax.axis_index("wa")
    right, left, right_two, left_two = early
    left_three = neighbour(left_two, [(1, 0)])
    last_two = neighbour(after(right, *others), [(1, 2)])
    last_three = neighbour(last_two, [(2, 3)])
    found = [
        lax.select_n(z, own, right, last_two, last_three),
        lax.select_n(z, left, own, right, right_two),
        lax.select_n(z, left_two, left, own, right),
        lax.select_n(z, left_three, left_two, left, own),
    ]
    return jnp.concatenate(found, axis=1)


def exchange_sum(parts):
    z = lax.axis_index("wa")
    got = [swap(take(parts, z ^ k), "wa", k) for k in range(1, lax.axis_size("wa"))]
    return tree_sum([take(parts, z)] + got)


def line_scatter(parts):
    return lax.psum_scatter(parts, "wa", scatter_dimension=0, tiled=False).astype(F32)


def live_taps(rate, valid):
    return [(a, b) for a in (-1, 0, 1) for b in (-1, 0, 1) if b == 0 or valid > rate]


def span(b, rate, valid):
    return max(0, -b * rate), min(valid, valid - b * rate)


def moves(taps):
    return sorted({a for a, b in taps})


def forward_plain(x, shift, weights, rate, taps):
    valid = x.shape[0]
    moved = {
        a: x if a == 0 else jnp.einsum("pq,wqk->wpk", shift[(a + 1) // 2], x) for a in moves(taps)
    }
    out = jnp.zeros(x.shape[:2] + (weights.shape[1],), F32)
    for t, (a, b) in enumerate(taps):
        low, high = span(b, rate, valid)
        part = jnp.einsum(
            "wpk,ek->wpe", moved[a][low + b * rate : high + b * rate], weights[t], preferred_element_type=F32
        )
        out = out.at[low:high].add(part)
    return out


def backward_plain(x, shift, weights, rate, taps, grad, total):
    valid = x.shape[0]
    moved = {
        a: grad if a == 0 else jnp.einsum("pq,wqe->wpe", shift[(1 - a) // 2], grad)
        for a in moves(taps)
    }
    weight_grads = []
    for t, (a, b) in enumerate(taps):
        low, high = span(b, rate, valid)
        d = moved[a][low:high]
        source = slice(low + b * rate, high + b * rate)
        weight_grads.append(jnp.einsum("wpe,wpk->ek", d, x[source], preferred_element_type=F32))
        total = total.at[source].add(
            jnp.einsum("wpe,ek->wpk", d, weights[t], preferred_element_type=F32)
        )
    return jnp.stack(weight_grads), total


def dot(left, right, dims):
    return lax.dot_general(left, right, ((dims[0], dims[1]), ((), ())), preferred_element_type=F32)


NN = ((1,), (0,))
NT = ((1,), (1,))
TN = ((0,), (0,))
WHOLE = pl.BlockSpec(memory_space=pltpu.VMEM)
SCALAR = pl.BlockSpec(memory_space=pltpu.SMEM)
NO_COST = pl.CostEstimate(flops=0, bytes_accessed=0, transcendentals=0)
WIDE = pltpu.CompilerParams(vmem_limit_bytes=60 * 1024 * 1024)
PARAMS = pltpu.CompilerParams(vmem_limit_bytes=32 * 1024 * 1024)


def ceil_to(n, step):
    return -(-n // step) * step


def pack_weights(w_one, dilated, w_pool, w_proj, taps):
    rows, deep = w_one.shape
    order = [(j, 3 * (a + 1) + b + 1) for j in range(3) for a, b in taps[j]]

    def kernel(one_ref, dilated_ref, pool_ref, proj_ref, out_ref):
        out_ref[0] = one_ref[...]
        for at, (j, t) in enumerate(order):
            out_ref[at + 1] = dilated_ref[j, t]
        out_ref[len(order) + 1] = pool_ref[...]
        out_ref[len(order) + 2] = proj_ref[...]

    return pl.pallas_call(
        kernel,
        out_shape=jax.ShapeDtypeStruct((len(order) + 3, rows, deep), BF16),
        in_specs=[WHOLE] * 4,
        out_specs=WHOLE,
        compiler_params=PARAMS,
        name="pack_weights",
    )(w_one, dilated, w_pool, w_proj)


def spots_of(wanted, held):
    return ((wanted[:, None] == held[None, :]) & (wanted >= 0)[:, None]).astype(BF16)


def block_rows(count, tall, rows, cols, valid, pitch):
    row = np.arange(count)
    column = row // tall * cols + row % tall % cols
    real = (row % tall < rows * cols) & (column < valid)
    return np.where(real, column * pitch + row % tall // cols, -1)


def padded_rows(count, valid, prows, rows):
    row = np.arange(count)
    real = (row < valid * prows) & (row % prows < rows)
    return np.where(real, row // prows * rows + row % prows, -1)


def extract(features, cotangent, z):
    rows, cols, micro, channels = features.shape
    out = cotangent.shape[-1]
    size = rows * cols
    steps = channels // out

    def kernel(z_ref, f_ref, c_ref, *refs):
        outs, held_ref = refs[:-1], refs[-1]

        def put(ref):
            values = ref[...]
            for m in range(micro):
                held_ref[m] = values[:, m, :].astype(F32)
            for k in range(micro):
                outs[k][...] = held_ref[z_ref[0] ^ k].astype(BF16)

        @pl.when(pl.program_id(0) < steps)
        def _():
            put(f_ref)

        @pl.when(pl.program_id(0) == steps)
        def _():
            put(c_ref)

    return pl.pallas_call(
        kernel,
        grid=(steps + 1,),
        out_shape=[jax.ShapeDtypeStruct((size, channels + out), BF16)] * micro,
        in_specs=[
            SCALAR,
            pl.BlockSpec((size, micro, out), lambda i: (0, 0, jnp.minimum(i, steps - 1))),
            pl.BlockSpec((size, micro, out), lambda i: (0, 0, 0)),
        ],
        out_specs=[pl.BlockSpec((size, out), lambda i: (0, i))] * micro,
        scratch_shapes=[pltpu.VMEM((micro, size, out), F32)],
        compiler_params=PARAMS,
        name="extract",
    )(z.reshape(1), features.reshape(size, micro, channels), cotangent.reshape(size, micro, out))


def choose(slots, z, blocks, spots, last_spots, lanes):
    size, wide = slots[0].shape
    tall = ceil_to(size, 16)
    high = spots.shape[1]
    count = wide // lanes - 1

    def kernel(z_ref, *refs):
        spots_ref, last_ref, send_ref, own_ref, held_ref = refs[len(slots) :]
        held_ref[...] = jnp.zeros((high, wide), BF16)
        for v in range(len(slots)):

            @pl.when(z_ref[0] == v)
            def _():
                for j in range(blocks):
                    held_ref[j * tall : j * tall + size] = refs[v ^ j][...]

        for d in range(count):
            part = held_ref[:, d * lanes : (d + 1) * lanes]
            send_ref[d] = dot(spots_ref[...], part, NN).astype(BF16)
        own_ref[...] = dot(last_ref[...], held_ref[:, count * lanes :], NN).astype(BF16)

    return pl.pallas_call(
        kernel,
        out_shape=[
            jax.ShapeDtypeStruct((count, spots.shape[0], lanes), BF16),
            jax.ShapeDtypeStruct((last_spots.shape[0], lanes), BF16),
        ],
        in_specs=[SCALAR] + [WHOLE] * (len(slots) + 2),
        out_specs=[WHOLE] * 2,
        scratch_shapes=[pltpu.VMEM((high, wide), BF16)],
        compiler_params=PARAMS,
        name="choose",
    )(z.reshape(1), *slots, spots, last_spots)


def unchoose(pieces, last, z, blocks, size, spots, last_spots):
    ha, fit, out = pieces.shape
    planes, tall, thick = spots.shape
    wide = (ha + 1) * out

    def kernel(z_ref, pieces_ref, last_ref, spots_ref, last_spots_ref, *refs):
        outs, held_ref = refs[:-1], refs[-1]
        held_ref[fit:] = jnp.zeros((thick - fit, ha * out), BF16)
        for d in range(ha):
            held_ref[:fit, d * out : (d + 1) * out] = pieces_ref[d]
        for v in range(planes):

            @pl.when(z_ref[0] == v)
            def _():
                for j in range(planes):
                    if j < blocks:
                        block = dot(spots_ref[j], held_ref[...], NN).astype(BF16)
                        outs[v ^ j][:, : ha * out] = block[:size]
                        block = dot(last_spots_ref[j], last_ref[...], NN).astype(BF16)
                        outs[v ^ j][:, ha * out :] = block[:size]
                    else:
                        outs[v ^ j][...] = jnp.zeros((size, wide), BF16)

    return pl.pallas_call(
        kernel,
        out_shape=[jax.ShapeDtypeStruct((size, wide), BF16)] * planes,
        in_specs=[SCALAR] + [WHOLE] * 4,
        out_specs=[WHOLE] * planes,
        scratch_shapes=[pltpu.VMEM((thick, ha * out), BF16)],
        compiler_params=PARAMS,
        name="unchoose",
    )(z.reshape(1), pieces, last, spots, last_spots)


def order_chunks(near, far, h, few):
    half, out, _ = near.shape

    def kernel(h_ref, near_ref, far_ref, out_ref):
        for k in range(2 * half):
            chunk = (far_ref if k % 2 else near_ref)[k // 2]
            at = pl.multiple_of((h_ref[0] ^ k) * few, 16)
            out_ref[pl.ds(at, few), :] = chunk.T[:few]

    return pl.pallas_call(
        kernel,
        out_shape=jax.ShapeDtypeStruct((2 * half * few, out), BF16),
        in_specs=[SCALAR, WHOLE, WHOLE],
        out_specs=WHOLE,
        compiler_params=PARAMS,
        cost_estimate=NO_COST,
        name="order_chunks",
    )(h.reshape(1), near, far)


def interleave(got, z, blocks, rows, cols, out, others):
    micro = len(got)
    size, channels = got[0].shape
    channels -= out
    lanes = 4 * out

    def kernel(z_ref, *refs):
        df_ref, act_ref = refs[-2:]

        def place(parts, to_ref):
            for v in range(micro):

                @pl.when(z_ref[0] == v)
                def _():
                    if v < blocks:
                        to_ref[...] = jnp.stack([parts[m ^ v][...] for m in range(micro)], axis=1)
                    else:
                        to_ref[...] = jnp.zeros(to_ref.shape, BF16)

        @pl.when(pl.program_id(0) == 0)
        def _():
            place(refs[micro : 2 * micro], act_ref)

        place(refs[:micro], df_ref)

    df, act = pl.pallas_call(
        kernel,
        grid=(channels // lanes,),
        out_shape=[jax.ShapeDtypeStruct((size, micro, n), BF16) for n in (channels, out)],
        in_specs=[SCALAR]
        + [pl.BlockSpec((size, lanes), lambda i: (0, i))] * micro
        + [pl.BlockSpec((size, out), lambda i: (0, channels // out))] * micro
        + [pl.BlockSpec(memory_space=pl.ANY)] * len(others),
        out_specs=[
            pl.BlockSpec((size, micro, lanes), lambda i: (0, 0, i)),
            pl.BlockSpec((size, micro, out), lambda i: (0, 0, 0)),
        ],
        compiler_params=PARAMS,
        name="interleave",
    )(z.reshape(1), *got, *got, *others)
    return [a.reshape(rows, cols, micro, -1).transpose(2, 0, 1, 3) for a in (df, act)]


def arrange(raw, place, h, valid, prows):
    ha, tall, deep = raw.shape
    high = place.shape[1]

    def kernel(h_ref, raw_ref, place_ref, x_ref, sum_ref, held_ref):
        held_ref[tall:] = jnp.zeros((high - tall, deep), BF16)
        for k in range(ha):
            held_ref[:tall] = raw_ref[h_ref[0] ^ k]
            block = dot(place_ref[...], held_ref[...], NN).reshape(valid, prows, deep)
            x_ref[:, k * prows : (k + 1) * prows, :] = block.astype(BF16)
            sum_ref[k * prows : (k + 1) * prows] = jnp.sum(block, axis=0)

    return pl.pallas_call(
        kernel,
        out_shape=[
            jax.ShapeDtypeStruct((valid, ha * prows, deep), BF16),
            jax.ShapeDtypeStruct((ha * prows, deep), F32),
        ],
        in_specs=[SCALAR, WHOLE, WHOLE],
        out_specs=[WHOLE, WHOLE],
        scratch_shapes=[pltpu.VMEM((high, deep), BF16)],
        compiler_params=PARAMS,
        name="arrange",
    )(h.reshape(1), raw, place)


def sides_of(taps):
    return sorted({b for a, b in taps}, key=abs)


def in_steps(low, high, step, body):
    whole = (high - low) // step
    if whole:

        def one(i, carry):
            body(low + i * step, step)
            return carry

        lax.fori_loop(0, whole, one, 0)
    if (high - low) % step:
        body(low + whole * step, (high - low) % step)


def forward_kernel(x, weights, group, prows):
    valid, pheight, deep = x.shape
    out = weights.shape[1]
    half = pheight // prows // 2
    operands, flops = [x, weights], 0
    for shift, first, rate, taps in group:
        operands += [] if shift is None else [shift]
        spans = [span(b, rate, valid) for a, b in taps]
        flops += 2 * pheight * deep * out * sum(high - low for low, high in spans)
    most = max(len(moves(g[3])) for g in group)
    most_sides = max(len(sides_of(g[3])) for g in group)

    def kernel(x_ref, w_ref, *refs):
        ins = list(refs[: len(operands) - 2])
        even_ref, odd_ref, moved_ref, wide_ref, sum_ref = refs[len(operands) - 2 :]
        for g, (shift, first, rate, taps) in enumerate(group):
            steps, sides = moves(taps), sides_of(taps)
            for i, b in enumerate(sides):
                for n, a in enumerate(steps):
                    wide_ref[i, :, n * deep : (n + 1) * deep] = w_ref[first + taps.index((a, b))]
            source_ref = x_ref
            if shift is not None:
                s_ref = ins.pop(0)
                source_ref = moved_ref

                def move(w, carry):
                    values = x_ref[w]
                    both = dot(s_ref[...].reshape(2 * pheight, pheight), values, NN).astype(BF16)
                    moved_ref[w, :, :deep] = both[:pheight]
                    moved_ref[w, :, deep : 2 * deep] = values
                    moved_ref[w, :, 2 * deep :] = both[pheight:]
                    return carry

                lax.fori_loop(0, valid, move, 0, unroll=True)

            for i, b in enumerate(sides):

                def columns(w, count):
                    values = source_ref[pl.ds(w + b * rate, count)].reshape(count * pheight, -1)
                    part = dot(values, wide_ref[i, :, : len(steps) * deep], NT)
                    part = part.reshape(count, pheight, out)
                    if b == 0:
                        sum_ref[pl.ds(w, count)] = part
                    else:
                        sum_ref[pl.ds(w, count)] += part

                in_steps(*span(b, rate, valid), 7, columns)

            def store(w, carry):
                at = pl.multiple_of(w * prows, prows)
                for k in range(2 * half):
                    to = odd_ref if k % 2 else even_ref
                    to[k // 2, g, pl.ds(at, prows), :] = sum_ref[w, k * prows : (k + 1) * prows].astype(BF16)
                return carry

            lax.fori_loop(0, valid, store, 0, unroll=True)

    shape = jax.ShapeDtypeStruct((half, len(group), valid * prows, out), BF16)
    return pl.pallas_call(
        kernel,
        out_shape=[shape] * 2,
        in_specs=[WHOLE] * len(operands),
        out_specs=[WHOLE] * 2,
        scratch_shapes=[
            pltpu.VMEM((valid, pheight, most * deep), BF16),
            pltpu.VMEM((most_sides, out, most * deep), BF16),
            pltpu.VMEM((valid, pheight, out), F32),
        ],
        compiler_params=PARAMS,
        cost_estimate=NO_COST,
        name="forward",
    )(*operands)


def loaded(operands):
    return [
        pl.BlockSpec(a.shape, lambda i, n=a.ndim: (0,) * n, pipeline_mode=pl.Buffered(1)) for a in operands
    ]


def build_moved(pieces, moved_ref, s_ref, g, branches, valid, ha, prows, out):
    middle = 0 if s_ref is None else out

    def move(w, carry):
        at = pl.multiple_of(w * prows, prows)
        for k in range(ha):
            piece, index = piece_of(k, g, branches)
            rows = slice(k * prows, (k + 1) * prows)
            moved_ref[w, rows, middle : middle + out] = pieces[piece][(*index, pl.ds(at, prows))]
        if s_ref is not None:
            held = moved_ref[w, :, out : 2 * out]
            both = dot(s_ref[...].reshape(2 * ha * prows, ha * prows), held, NN).astype(BF16)
            moved_ref[w, :, :out] = both[ha * prows :]
            moved_ref[w, :, 2 * out :] = both[: ha * prows]
        return carry

    lax.fori_loop(0, valid, move, 0, unroll=True)


def weights_backward(x, group, pieces, wa, prows):
    valid, pheight, deep = x.shape
    out = pieces[0].shape[-1]
    few, ha, branches = out // wa, pheight // prows, len(group)
    shifts = [g[0] for g in group if g[0] is not None]
    operands = [x, *shifts, *pieces]
    shape = wa, sum(len(g[3]) for g in group), few, deep
    most = max(len(moves(g[3])) for g in group)

    def kernel(x_ref, *refs):
        shift_refs = list(refs[: len(shifts)])
        piece_refs = refs[len(shifts) : len(operands) - 1]
        grad_ref, moved_ref = refs[len(operands) - 1 :]
        done = 0
        for g, (shift, first, rate, taps) in enumerate(group):
            steps = moves(taps)
            s_ref = None if shift is None else shift_refs.pop(0)
            build_moved(piece_refs, moved_ref, s_ref, g, branches, valid, ha, prows, out)
            wide = len(steps) * out
            for b in sides_of(taps):
                low, high = span(b, rate, valid)
                left = moved_ref[low:high, :, :wide].reshape((high - low) * pheight, wide)
                right = x_ref[low + b * rate : high + b * rate].reshape((high - low) * pheight, deep)
                part = dot(left, right, TN).astype(BF16)
                for n, a in enumerate(steps):
                    t = done + taps.index((a, b))
                    for j in range(wa):
                        at = n * out + j * few
                        grad_ref[j, t] = part[at : at + few]
            done += len(taps)

    return pl.pallas_call(
        kernel,
        out_shape=jax.ShapeDtypeStruct(shape, BF16),
        grid=(1,),
        in_specs=loaded(operands),
        out_specs=pl.BlockSpec(shape, lambda i: (0, 0, 0, 0)),
        scratch_shapes=[pltpu.VMEM((valid, pheight, most * out), BF16)],
        compiler_params=WIDE,
        cost_estimate=NO_COST,
        name="weights_backward",
    )(*operands)


def features_backward(x, weights, group, pieces, start, h, place, fit, prows):
    valid, pheight, deep = x.shape
    out = weights.shape[1]
    ha, branches = pheight // prows, len(group)
    shifts = [g[0] for g in group if g[0] is not None]
    operands = [h.reshape(1), start, weights, place, *shifts, *pieces]
    high = place.shape[1]
    most = max(len(moves(g[3])) for g in group)
    most_sides = max(len(sides_of(g[3])) for g in group)

    def kernel(h_ref, start_ref, w_ref, place_ref, *refs):
        shift_refs = list(refs[: len(shifts)])
        piece_refs = refs[len(shifts) : len(operands) - 4]
        last_ref, moved_ref, wide_ref, total_ref, held_ref = refs[len(operands) - 4 :]
        for g, (shift, first, rate, taps) in enumerate(group):
            steps, sides = moves(taps), sides_of(taps)
            s_ref = None if shift is None else shift_refs.pop(0)
            build_moved(piece_refs, moved_ref, s_ref, g, branches, valid, ha, prows, out)
            for i, b in enumerate(sides):
                for n, a in enumerate(steps):
                    wide_ref[i, n * out : (n + 1) * out] = w_ref[first + taps.index((a, b))]
            wide = len(steps) * out
            for i, b in enumerate(sides):

                def columns(w, count):
                    values = moved_ref[pl.ds(w - b * rate, count), :, :wide].reshape(count * pheight, wide)
                    part = dot(values, wide_ref[i, :wide], NN).reshape(count, pheight, deep)
                    if g or b != 0:
                        total_ref[pl.ds(w, count)] += part
                    else:
                        total_ref[pl.ds(w, count)] = part + start_ref[...][None]

                in_steps(*span(-b, rate, valid), 7, columns)
        held_ref[valid * prows :] = jnp.zeros((high - valid * prows, deep), BF16)
        for k in range(ha):
            block = total_ref[:, k * prows : (k + 1) * prows, :].astype(BF16)
            held_ref[: valid * prows] = block.reshape(valid * prows, deep)
            last_ref[h_ref[0] ^ k] = dot(place_ref[...], held_ref[...], NN).astype(BF16)

    return pl.pallas_call(
        kernel,
        out_shape=jax.ShapeDtypeStruct((ha, fit, deep), BF16),
        grid=(1,),
        in_specs=[SCALAR] + loaded(operands[1:]),
        out_specs=pl.BlockSpec((ha, fit, deep), lambda i: (0, 0, 0)),
        scratch_shapes=[
            pltpu.VMEM((valid, pheight, most * out), BF16),
            pltpu.VMEM((most_sides, most * out, deep), BF16),
            pltpu.VMEM(x.shape, F32),
            pltpu.VMEM((high, deep), BF16),
        ],
        compiler_params=WIDE,
        cost_estimate=NO_COST,
        name="features_backward",
    )(*operands)


def real_rows(pixels, prows, rows):
    return (lax.broadcasted_iota(jnp.int32, (pixels, 1), 0) % prows < rows).astype(F32)


def total_of(refs):
    return tree_sum([r[...] for r in refs])


def column_sum(values):
    return jnp.sum(values, axis=0, keepdims=True)


def small_kernel(kernel, name, operands, shapes):
    return pl.pallas_call(
        kernel,
        out_shape=[jax.ShapeDtypeStruct(s, t) for s, t in shapes],
        in_specs=[WHOLE] * len(operands),
        out_specs=[WHOLE] * len(shapes),
        compiler_params=PARAMS,
        cost_estimate=NO_COST,
        name=name,
    )(*operands)


def branch_sums(parts, pool_part):
    _, pixels, out = parts[0].shape
    images = pool_part.shape[0]

    def kernel(low, low_got, low_last, high, high_got, high_last, pool_ref, branch_ref, sum_ref):
        for j in range(4):
            own, got, last = (low, low_got, low_last) if j < 2 else (high, high_got, high_last)
            value = own[j % 2] + got[0, j % 2].astype(F32) + last[j % 2].astype(F32)
            branch_ref[j] = value
            sum_ref[j : j + 1] = column_sum(value)
            sum_ref[4 + j : 5 + j] = column_sum(value * value)
        sum_ref[8:] = pool_ref[...]

    shapes = [((4, pixels, out), F32), ((8 + images, out), F32)]
    return small_kernel(kernel, "branch_sums", [*parts, pool_part], shapes)


def project(sums, branch, scales, shifts, counts, own, proj, rows, pixel_total):
    _, pixels, out = branch.shape
    images = counts.shape[0]
    prows = own.shape[0]
    many = len(sums)

    def kernel(*refs):
        branch_ref, scale_ref, shift_ref, count_ref, own_ref, proj_ref = refs[many : many + 6]
        joined_ref, projected_ref, second_ref, stat_ref, pool_ref = refs[many + 6 :]
        total = total_of(refs[:many])
        mean = total[0:4] / pixel_total
        rstd = lax.rsqrt(total[4:8] / pixel_total - mean * mean + EPS)
        stat_ref[0:4] = mean
        stat_ref[4:8] = rstd
        scale, shift = scale_ref[...], shift_ref[...]
        for j in range(4):
            norm = (branch_ref[j] - mean[j : j + 1]) * rstd[j : j + 1]
            hid = norm * scale[j : j + 1] + shift[j : j + 1]
            joined_ref[:, j * out : (j + 1) * out] = silu(hid).astype(BF16)
        pool_out = total[8:]
        weighted = count_ref[...]
        pool_mean = column_sum(weighted * pool_out) / pixel_total
        pool_second = column_sum(weighted * pool_out * pool_out) / pixel_total
        pool_rstd = lax.rsqrt(pool_second - pool_mean * pool_mean + EPS)
        pool_norm = (pool_out - pool_mean) * pool_rstd
        pool_hid = pool_norm * scale[4:5] + shift[4:5]
        pool_ref[0] = pool_norm
        pool_ref[1] = pool_hid
        pool_ref[2] = jnp.broadcast_to(pool_rstd, pool_out.shape)
        pool_act = silu(pool_hid)
        spread = jnp.zeros((prows, out), F32)
        for i in range(images):
            spread = spread + own_ref[:, i : i + 1] * pool_act[i : i + 1]
        spread = spread.astype(BF16)
        for w in range(pixels // prows):
            joined_ref[w * prows : (w + 1) * prows, 4 * out :] = spread
        projected = dot(joined_ref[...], proj_ref[...], NN)
        projected_ref[...] = projected
        held = projected * real_rows(pixels, prows, rows)
        second_ref[...] = jnp.zeros(second_ref.shape, F32)
        second_ref[0:1] = column_sum(held)
        second_ref[1:2] = column_sum(held * held)

    shapes = [((pixels, 5 * out), BF16), ((pixels, out), F32), ((8, out), F32), ((8, out), F32), ((3, images, out), F32)]
    return small_kernel(kernel, "project", [*sums, branch, scales, shifts, counts, own, proj], shapes)


def activate(sums, projected, cot, out_scale, out_shift, prows, rows, pixel_total):
    pixels, out = projected.shape
    many = len(sums)

    def kernel(*refs):
        projected_ref, cot_ref, scale_ref, shift_ref = refs[many : many + 4]
        act_ref, norm_ref, dhid_ref, third_ref, rstd_ref = refs[many + 4 :]
        total = total_of(refs[:many])
        mean = total[0:1] / pixel_total
        rstd = lax.rsqrt(total[1:2] / pixel_total - mean * mean + EPS)
        rstd_ref[...] = jnp.broadcast_to(rstd, rstd_ref.shape)
        norm = (projected_ref[...] - mean) * rstd
        norm_ref[...] = norm
        hid = norm * scale_ref[...] + shift_ref[...]
        act_ref[...] = silu(hid).astype(BF16)
        dhid = cot_ref[...].astype(F32) * real_rows(pixels, prows, rows) * silu_slope(hid)
        dhid_ref[...] = dhid
        third_ref[...] = jnp.zeros(third_ref.shape, F32)
        third_ref[0:1] = column_sum(dhid)
        third_ref[1:2] = column_sum(dhid * norm)

    shapes = [((pixels, out), BF16), ((pixels, out), F32), ((pixels, out), F32), ((8, out), F32), ((8, out), F32)]
    operands = [*sums, projected, cot, out_scale[None], out_shift[None]]
    return small_kernel(kernel, "activate", operands, shapes)


def unproject(sums, norm, dhid, rstd, out_scale, proj, joined, branch, stats, scales, shifts, own, ha, rows, pixel_total):
    _, pixels, out = branch.shape
    prows, images = own.shape
    many = len(sums)

    def kernel(*refs):
        norm_ref, dhid_ref, rstd_ref, oscale_ref, proj_ref, joined_ref = refs[many : many + 6]
        branch_ref, stat_ref, scale_ref, shift_ref, own_ref = refs[many + 6 : many + 11]
        third_ref, grad_ref, back_ref, fourth_ref = refs[many + 11 :]
        total = total_of(refs[:many])
        third_ref[...] = total
        mask = real_rows(pixels, prows, rows)
        dproj = dhid_ref[...] - (total[0:1] + norm_ref[...] * total[1:2]) / pixel_total
        dproj = (oscale_ref[...] * rstd_ref[0:1] * dproj * mask).astype(BF16)
        grad = dot(joined_ref[...], dproj, TN)
        grad_ref[...] = jnp.zeros(grad_ref.shape, BF16)
        few = 5 * out // ha
        for d in range(ha):
            grad_ref[d, :, :few] = grad[d * few : (d + 1) * few].T.astype(BF16)
        for j in range(5):
            dact = dot(dproj, proj_ref[j * out : (j + 1) * out], NT)
            if j < 4:
                branch_norm = (branch_ref[j] - stat_ref[j : j + 1]) * stat_ref[4 + j : 5 + j]
                hid = branch_norm * scale_ref[j : j + 1] + shift_ref[j : j + 1]
                back = dact * silu_slope(hid) * mask
                back_ref[j] = back
                fourth_ref[j : j + 1] = column_sum(back)
                fourth_ref[4 + j : 5 + j] = column_sum(back * branch_norm)
            else:
                across = jnp.sum(dact.reshape(pixels // prows, prows, out), axis=0)
                for i in range(images):
                    fourth_ref[8 + i : 9 + i] = column_sum(own_ref[:, i : i + 1] * across)

    shapes = [((8, out), F32), ((ha, out, out), BF16), ((4, pixels, out), F32), ((8 + images, out), F32)]
    operands = [*sums, norm, dhid, rstd, out_scale[None], proj, joined, branch, stats, scales, shifts, own]
    return small_kernel(kernel, "unproject", operands, shapes)


def branch_gradients(sums, back, branch, stats, scales, counts, pool, prows, rows, pixel_total):
    _, pixels, out = branch.shape
    images = counts.shape[0]
    many = len(sums)

    def kernel(*refs):
        back_ref, branch_ref, stat_ref, scale_ref, count_ref, pool_ref = refs[many : many + 6]
        grad_ref, dpool_ref, sum_ref = refs[many + 6 :]
        total = total_of(refs[:many])
        mask = real_rows(pixels, prows, rows)
        for j in range(4):
            rstd = stat_ref[4 + j : 5 + j]
            norm = (branch_ref[j] - stat_ref[j : j + 1]) * rstd
            value = back_ref[j] - (total[j : j + 1] + norm * total[4 + j : 5 + j]) / pixel_total
            grad_ref[j] = (scale_ref[j : j + 1] * rstd * value * mask).astype(BF16)
        dhid = silu_slope(pool_ref[1]) * total[8:]
        pool_shift = column_sum(dhid)
        pool_scale = column_sum(dhid * pool_ref[0])
        value = dhid - count_ref[...] * (pool_shift + pool_ref[0] * pool_scale) / pixel_total
        dpool_ref[...] = (scale_ref[4:5] * pool_ref[2] * value).astype(BF16)
        sum_ref[...] = jnp.zeros(sum_ref.shape, F32)
        sum_ref[0:4] = total[4:8]
        sum_ref[4:5] = pool_scale
        sum_ref[5:9] = total[0:4]
        sum_ref[9:10] = pool_shift

    shapes = [((4, pixels, out), BF16), ((images, out), BF16), ((16, out), F32)]
    operands = [*sums, back, branch, stats, scales, counts, pool]
    return small_kernel(kernel, "branch_gradients", operands, shapes)


def local(
    features,
    row_image,
    cotangent,
    w_one,
    dilated_weight,
    w_pool,
    w_proj,
    scales,
    shifts,
    out_scale,
    out_shift,
):
    micro, rows, cols, channels = features.shape
    ha, wa = lax.axis_size("ha"), lax.axis_size("wa")
    h, z = lax.axis_index("ha"), lax.axis_index("wa")
    planes = wa // micro
    batch, part = z // planes, z % planes
    deep = w_one.shape[0] // planes
    out = w_one.shape[1] * wa
    valid = cols * wa - PADC
    blocks = -(-valid // cols)
    prows = -(-rows // 16) * 16
    height, pheight = rows * ha, prows * ha
    images = IMG_DEV * ha
    pixels = float(height * valid)
    size = cols * rows

    fast = planes == 1 and wa == 4 and 6 * valid * pheight * out < (16 << 20) and channels % out == 0 and deep == out

    taps = [live_taps(r, valid) for r in RATES]
    few = w_proj.shape[0]
    side = jnp.pad(w_proj.T, ((0, 0), (0, w_one.shape[0] - few)))
    turned = dilated_weight.swapaxes(2, 3)
    if fast:
        weights = pack_weights(w_one.T, turned, w_pool.T, side, taps)
    else:
        picked = [turned[j, 3 * (a + 1) + b + 1] for j in range(3) for a, b in taps[j]]
        weights = gather_columns(jnp.stack([w_one.T, *picked, w_pool.T, side]))

    if fast:
        slots = extract(features.transpose(1, 2, 0, 3), cotangent.transpose(1, 2, 0, 3), z)
        tall, fit = ceil_to(size, 16), ceil_to(valid * rows, 16)
        slots = [slots[0]] + [swap(slots[k], "wa", k, lambda i: i < blocks) for k in range(1, wa)]
        early = gather_early(weights, slots[1])
        high, thick = ceil_to(blocks * tall, 128), ceil_to(fit, 128)
        in_piece = block_rows(high, tall, rows, cols, valid, rows)
        in_chunk = block_rows(high, tall, rows, cols, valid, prows)
        spots = spots_of(np.arange(fit), in_piece)
        cot_spots = spots_of(np.arange(valid * prows), in_chunk)
        send, cot = choose(slots, z, blocks, spots, cot_spots, deep)
        raw = lax.all_to_all(send, "ha", 0, 0, tiled=True)
    else:
        f = features.transpose(0, 2, 1, 3).reshape(micro, size, ha, planes, deep)
        f = f.transpose(0, 3, 1, 2, 4).reshape(wa, size, ha * deep)
        c = cotangent.transpose(0, 2, 1, 3).reshape(micro, size, out)
        load = jnp.concatenate([f, jnp.repeat(c, planes, axis=0)], axis=-1)
        slots = [take(load, z)]
        for k in range(1, wa):
            slots.append(swap(take(load, z ^ k), "wa", k, lambda i: i < blocks))
        slots = jnp.stack(slots)
        block = jnp.concatenate([take(slots, z ^ j) for j in range(blocks)])[: valid * rows]
        raw = block[:, : ha * deep].reshape(valid * rows, ha, deep).swapaxes(0, 1)
        raw = lax.all_to_all(raw, "ha", 0, 0, tiled=True)
        cot = block[:, ha * deep :].reshape(valid, rows, out)
        cot = jnp.pad(cot, ((0, 0), (0, prows - rows), (0, 0))).reshape(valid * prows, out)
    if fast:
        weights = gather_late(weights, early, *slots)
    if fast:
        proj = order_chunks(*gather_chunks(weights[-1]), h, few)
    else:
        proj = in_order(*gather_chunks(weights[-1]))[..., :few].swapaxes(1, 2).reshape(ha * few, out)
    if planes > 1:
        weights = lax.dynamic_slice_in_dim(weights, part * deep, deep, 2)
    wide_pool = weights[-2]

    order = h ^ jnp.arange(ha, dtype=jnp.int32)
    labels = by_distance(take(row_image, batch).reshape(ha, rows))
    number = order[:, None] * rows + jnp.arange(rows, dtype=jnp.int32)[None, :]
    pad = ((0, 0), (0, prows - rows))
    labels = jnp.pad(labels, pad, constant_values=-1).reshape(pheight)
    number = jnp.pad(number, pad, constant_values=-(1 << 20)).reshape(pheight)
    same = (labels[:, None] == labels[None, :]) & (labels >= 0)[:, None]
    apart = number[None, :] - number[:, None]
    shift = [
        jnp.stack([(same & (apart == a * r)).astype(BF16) for a in (-1, 1)]) for r in RATES
    ]
    ids = jnp.arange(images, dtype=jnp.int32)
    member = (labels[:, None] == ids[None, :]).astype(F32)
    counts = jnp.sum(member, axis=0) * valid
    own = member[:prows]
    mask = jnp.tile(jnp.sum(own, axis=1), valid)[:, None]

    ahead = [1, 1 + len(taps[0]), 1 + len(taps[0]) + len(taps[1])]
    group = [(None, 0, 0, [(0, 0)])] + [(shift[j], ahead[j], RATES[j], taps[j]) for j in range(3)]
    if fast:
        place = spots_of(padded_rows(valid * prows, valid, prows, rows), np.arange(thick))
        x, row_sums = arrange(raw, place, h, valid, prows)
        unplace = spots_of(np.arange(fit), padded_rows(ceil_to(valid * prows, 128), valid, prows, rows))
    else:
        x = by_distance(raw).reshape(ha, valid, rows, deep)
        x = jnp.pad(x, ((0, 0), (0, 0), (0, prows - rows), (0, 0)))
        x = x.swapaxes(0, 1).reshape(valid, pheight, deep)
        row_sums = jnp.sum(x.astype(F32), axis=0)
    if fast:
        branch_parts = reduce_square(*forward_kernel(x, weights, group, prows))
    else:
        sums = jnp.stack([forward_plain(x, s, weights[n : n + len(t)], r, t) for s, n, r, t in group])
        sums = sums.astype(BF16).reshape(len(group), valid, ha // 2, 2, prows, out)
        sums = sums.transpose(3, 2, 0, 1, 4, 5).reshape(2, ha // 2, len(group), valid * prows, out)
        branch = sum_chunks(spread_chunks(sums[0], sums[1]), planes)
    pooled = (jnp.dot(member.T, row_sums, precision=HIGHEST) / counts[:, None]).astype(BF16)
    pool_part = dot(pooled, wide_pool, NT)

    weighted = counts[:, None]
    once = (part == 0).astype(F32)
    if fast:
        branch, first = branch_sums(branch_parts, pool_part)
        joined, projected, second, stats, pool = project(
            plane_parts(first), branch, scales, shifts, weighted, own, proj, rows, pixels
        )
        activation, proj_norm, dproj_hid, third, proj_rstd = activate(
            plane_parts(second), projected, cot, out_scale, out_shift, prows, rows, pixels
        )
        third, grad_proj, dhid, fourth = unproject(
            plane_parts(third),
            proj_norm,
            dproj_hid,
            proj_rstd,
            out_scale,
            proj,
            joined,
            branch,
            stats,
            scales,
            shifts,
            own,
            ha,
            rows,
            pixels,
        )
        dbranch, dpool, sums = branch_gradients(
            plane_parts(fourth), dhid, branch, stats, scales, weighted, pool, prows, rows, pixels
        )
        sums = jnp.concatenate([sums[:10], third[:2]])
    else:
        first = plane_sum(
            jnp.concatenate(
                [once * jnp.sum(branch, axis=1), once * jnp.sum(branch * branch, axis=1), pool_part]
            ),
            planes,
        )
        mean = first[0:4] / pixels
        rstd = lax.rsqrt(first[4:8] / pixels - mean * mean + EPS)
        pool_out = first[8:]
        norm = (branch - mean[:, None]) * rstd[:, None]
        hid = norm * scales[:4, None] + shifts[:4, None]
        act = silu(hid)
        weighted = counts[:, None]
        pool_mean = jnp.sum(weighted * pool_out, axis=0) / pixels
        pool_second = jnp.sum(weighted * pool_out * pool_out, axis=0) / pixels
        pool_rstd = lax.rsqrt(pool_second - pool_mean * pool_mean + EPS)
        pool_norm = (pool_out - pool_mean) * pool_rstd
        pool_hid = pool_norm * scales[4] + shifts[4]
        spread = jnp.dot(own, silu(pool_hid), precision=HIGHEST)
        spread = jnp.broadcast_to(spread[None], (valid, prows, out)).reshape(valid * prows, out)
        joined = jnp.concatenate([act[0], act[1], act[2], act[3], spread], axis=-1).astype(BF16)
        projected = jnp.dot(joined, proj, preferred_element_type=F32)

        held = projected * mask
        second = plane_sum(
            jnp.stack([jnp.sum(held, axis=0), jnp.sum(held * held, axis=0)]) * once, planes
        )
        proj_mean = second[0] / pixels
        proj_rstd = lax.rsqrt(second[1] / pixels - proj_mean * proj_mean + EPS)
        proj_norm = (projected - proj_mean) * proj_rstd
        proj_hid = proj_norm * out_scale + out_shift
        activation = silu(proj_hid).astype(BF16)
        dproj_hid = cot.astype(F32) * mask * silu_slope(proj_hid)
        third = plane_sum(
            jnp.stack([jnp.sum(dproj_hid, axis=0), jnp.sum(dproj_hid * proj_norm, axis=0)]) * once, planes
        )
        dproj = (
            out_scale * proj_rstd * (dproj_hid - (third[0] + proj_norm * third[1]) / pixels) * mask
        ).astype(BF16)
        djoined = lax.dot_general(dproj, proj, (((1,), (1,)), ((), ())), preferred_element_type=F32)
        grad_proj = dot(dproj, joined, TN)
        dact = jnp.stack([djoined[:, j * out : (j + 1) * out] for j in range(4)])
        dspread = jnp.sum(djoined[:, 4 * out :].reshape(valid, prows, out), axis=0)
        image_part = jnp.dot(own.T, dspread, precision=HIGHEST)
        dhid = dact * silu_slope(hid) * mask
        fourth = plane_sum(
            jnp.concatenate([jnp.sum(dhid, axis=1), jnp.sum(dhid * norm, axis=1), image_part]) * once,
            planes,
        )
        branch_shift, branch_scale, image_total = fourth[0:4], fourth[4:8], fourth[8:]
        dbranch = (
            (scales[:4] * rstd)[:, None]
            * (dhid - (branch_shift[:, None] + norm * branch_scale[:, None]) / pixels)
            * mask
        ).astype(BF16)
        dpool_hid = silu_slope(pool_hid) * image_total
        pool_shift = jnp.sum(dpool_hid, axis=0)
        pool_scale = jnp.sum(dpool_hid * pool_norm, axis=0)
        dpool = (
            scales[4] * pool_rstd * (dpool_hid - weighted * (pool_shift + pool_norm * pool_scale) / pixels)
        ).astype(BF16)
        sums = jnp.concatenate([branch_scale, pool_scale[None], branch_shift, pool_shift[None], third])
    grad_pool = dot(dpool, pooled, TN)
    dpooled = dot(dpool, wide_pool, NN)

    total = jnp.dot(member, dpooled / counts[:, None], precision=HIGHEST)
    if fast:
        pieces = gather_square(dbranch)
        tap_grads = weights_backward(x, group, pieces, wa, prows)
        back = features_backward(x, weights, group, pieces, total, h, unplace, fit, prows)
    else:
        total = jnp.broadcast_to(total[None], (valid,) + total.shape)
        near, far = gather_chunks(dbranch)
        every = jnp.stack([near, far], axis=1).reshape(ha, len(group), valid, prows, out)
        every = every.transpose(1, 2, 0, 3, 4).reshape(len(group), valid, pheight, out)
        found = []
        for (s, n, r, t), d in zip(group, every):
            grads, total = backward_plain(x, s, weights[n : n + len(t)], r, t, d, total)
            found.append(grads.reshape(len(t), wa, out // wa, deep).swapaxes(0, 1).astype(BF16))
        tap_grads = jnp.concatenate(found, axis=1)
        back = total.astype(BF16).reshape(valid, ha, prows, deep)[:, :, :rows]
        back = back.swapaxes(0, 1).reshape(ha, valid * rows, deep)
        back = by_distance(back)

    def in_place(grads):
        if planes == 1:
            return grads
        full = jnp.zeros(grads.shape[:-1] + (deep * planes,), grads.dtype)
        return lax.dynamic_update_slice_in_dim(full, grads, part * deep, grads.ndim - 1)

    if not fast:
        grad_proj = (grad_proj * once).reshape(out, ha, few).swapaxes(0, 1)
        grad_proj = jnp.pad(grad_proj, ((0, 0), (0, 0), (0, w_one.shape[0] - few))).astype(BF16)
    proj_chunk = lax.psum_scatter(grad_proj, "ha", scatter_dimension=0, tiled=False)
    grad_pool = in_place(grad_pool.astype(BF16)).reshape(wa, 1, out // wa, -1)
    proj_chunk = proj_chunk.reshape(wa, 1, out // wa, -1)
    tap_grads = line_scatter(in_place(tap_grads))
    rest = jnp.concatenate([grad_pool, proj_chunk], axis=1)
    if not fast:
        rest = line_scatter(rest)
    tap_out = [tap_grads[n : n + len(t)] for n, t in zip(ahead, taps)]
    blank = jnp.zeros((out // wa, w_one.shape[0]), F32)
    atrous = []
    for j in range(3):
        if len(taps[j]) == 9:
            atrous.append(tap_out[j])
        else:
            found = {3 * (a + 1) + b + 1: tap_out[j][t] for t, (a, b) in enumerate(taps[j])}
            atrous.append(jnp.stack([found.get(t, blank) for t in range(9)]))
    atrous = jnp.stack(atrous)
    atrous_out = atrous.swapaxes(2, 3)
    back = lax.all_to_all(back, "ha", 0, 0, tiled=True)

    def home(i, k):
        return i ^ k < blocks

    if fast:
        piece_spots = spots_of(block_rows(wa * tall, tall, rows, cols, valid, rows), np.arange(thick))
        chunk_spots = spots_of(block_rows(wa * tall, tall, rows, cols, valid, prows), np.arange(valid * prows))
        got = unchoose(
            back, activation, z, blocks, size, piece_spots.reshape(wa, tall, thick), chunk_spots.reshape(wa, tall, -1)
        )
        got = [got[0]] + [swap(got[k], "wa", k, partial(home, k=k)) for k in range(1, wa)]
        df, acts = interleave(got, z, blocks, rows, cols, out, [atrous])
        wide = jnp.broadcast_to(jnp.pad(sums, ((0, 4), (0, 0)))[None], (wa, 16, out))
        rest = jnp.concatenate([rest.astype(F32).reshape(wa, -1, out), wide], axis=1)
        rest = exchange_sum(rest)
        sums = rest[-16:-4]
        rest = rest[:-16].reshape(2, -1, out)
    else:

        def send_home(array):
            array = jnp.pad(array, ((0, wa * size - valid * rows), (0, 0))).reshape(wa, size, -1)
            got = [take(array, z)]
            got += [swap(take(array, z ^ k), "wa", k, partial(home, k=k)) for k in range(1, wa)]
            got = jnp.stack(got)
            got = jnp.where(z < blocks, got, jnp.zeros((), got.dtype))
            return jnp.stack([take(got, z ^ t) for t in range(wa)])

        back = back.swapaxes(0, 1).reshape(valid * rows, ha * deep)
        df = send_home(back).reshape(micro, planes, cols, rows, ha, deep)
        df = df.transpose(0, 3, 2, 4, 1, 5).reshape(features.shape)
        activation = activation.reshape(valid, prows, out)[:, :rows].reshape(valid * rows, out)
        acts = send_home(activation).reshape(micro, planes, cols, rows, out)[:, 0].swapaxes(1, 2)
    if not fast:
        sums = sums * once
        sums = tree_sum([sums] + [swap(sums, "wa", k) for k in range(1, wa)])
    one_out, pool_grad_out, proj_out = tap_grads[0].T, rest[0].T, rest[1][:, :few].T
    return (
        acts,
        df,
        one_out,
        atrous_out,
        pool_grad_out,
        proj_out,
        sums[0:5],
        sums[5:10],
        sums[11],
        sums[10],
    )


def solution(mesh):
    specs = (
        P(None, "ha", "wa", None),
        P(),
        P(None, "ha", "wa", None),
        P("ha", "wa"),
        P(None, None, "ha", "wa"),
        P("ha", "wa"),
        P("ha", "wa"),
        P(),
        P(),
        P(),
        P(),
    )
    out_specs = (
        P(None, "ha", "wa", None),
        P(None, "ha", "wa", None),
        P("ha", "wa"),
        P(None, None, "ha", "wa"),
        P("ha", "wa"),
        P("ha", "wa"),
        P(),
        P(),
        P(),
        P(),
    )
    return jax.shard_map(local, mesh=mesh, in_specs=specs, out_specs=out_specs, check_vma=False)
```
